512 devices in a mesh: seq: 64 (over z_hi, x, y), chan: 4 (over z_lo), dp: 2 (over core).
Axes of the slice: x: 4, y: 4, z: 16 (z_hi: 4, z_lo: 4; z = z_hi * 4 + z_lo), core: 2. Of those that a mesh axis runs over, the one named last changes fastest.
Arguments:
- projected: float32 [3, 4, 4096, 4096], P(None, 'dp', 'seq', 'chan'), may hold values from -6 to 6
- short_weight: float32 [3, 7, 4096], P(None, None, 'chan'), may hold values from -2 to 2
- decay_rates: float32 [4096], P('chan'), may hold values from 1.2207031e-05 to 0.03125
- first_weight: float32 [32, 64], replicated, may hold values from -1 to 1
- second_weight: float32 [64, 64], replicated, may hold values from -0.75 to 0.75
- out_weight: float32 [64, 4096], P(None, 'chan'), may hold values from -0.75 to 0.75
- cotangent: float32 [4, 4096, 4096], P('dp', 'seq', 'chan'), may hold values from -6 to 6
Outputs:
- mixed: float32 [4, 4096, 4096], P('dp', 'seq', 'chan')
- raw_grad: float32 [3, 4, 4096, 4096], P(None, 'dp', 'seq', 'chan')
- short_grad: float32 [3, 7, 4096], P(None, None, 'chan')
- out_grad: float32 [64, 4096], P(None, 'chan')
- first_grad: float32 [32, 64], replicated
- second_grad: float32 [64, 64], replicated
The draws below stay inside these ranges and needn't reach their ends.
All inputs are finite; a program needn't handle non-finite values.
Results may differ from the reference program's by a relative error of at most 0.00011.
Values sent between devices are 32-bit elements; how exact they have to be, the bound alone decides.
A program may use at most 64 MiB of HBM per device.

```python
import math
import jax
import jax.numpy as jnp
from jax import lax

D = 4096
SHORT = 7
E = 32
MH = 64
SEQ = 4096
WINS = 4


def steps_of(rng, extent, cuts, least, largest):
    def one(position, shards_of):
        draws = jax.random.uniform(jax.random.fold_in(jax.random.fold_in(rng, 6), position), (shards_of,), jnp.float32, least / len(cuts), largest / len(cuts))
        return jnp.repeat(jnp.exp(draws), extent[position] // shards_of).reshape((-1,) + (1,) * (len(extent) - position - 1))

    level = one(*cuts[0])
    for cut in cuts[1:]:
        level = level * one(*cut)
    return level


def noise(key, dims, width, limit, shards=(), kind=jnp.bfloat16):
    loudness = steps_of(key, dims, shards, -0.22, 0.18) if shards else 1.0
    values = jax.random.normal(key, dims, jnp.float32) * width * loudness
    return jnp.minimum(jnp.maximum(values, -limit), limit).astype(kind)


def setup_inputs(seed: int = 0) -> dict:
    key_of = jax.random.split(jax.random.key(seed), 8)
    return {
        "projected": noise(key_of[0], (3, WINS, SEQ, D), 1.0, 6.0, ((1, 2), (2, 64), (3, 4)), jnp.float32),
        "short_weight": noise(key_of[1], (3, SHORT, D), SHORT ** -0.5, 2.0, ((2, 4),), jnp.float32),
        "decay_rates": jnp.clip(jnp.exp(math.log(0.03125) - 7.8477625 * jax.random.uniform(key_of[2], (D,), jnp.float32) ** steps_of(key_of[2], (D,), ((0, 4),), -0.2, 0.2)), 1.220703143189894e-05, 0.03125),
        "first_weight": noise(key_of[3], (E, MH), E ** -0.5, 1.0, (), jnp.float32),
        "second_weight": noise(key_of[4], (MH, MH), MH ** -0.5, 0.75, (), jnp.float32),
        "out_weight": noise(key_of[5], (MH, D), MH ** -0.5, 0.75, ((1, 4),), jnp.float32),
        "cotangent": noise(key_of[6], (WINS, SEQ, D), 1.0, 6.0, ((0, 2), (1, 64), (2, 4)), jnp.float32),
    }


precise = lax.Precision.HIGHEST

def positional(positions, seq_len, count):
    half = count // 2
    orders = jnp.arange(half, dtype=jnp.int32)
    spread = max((half - 1) ** 2, 1)
    factors = 1 + (seq_len // 2 - 2) * orders * orders // spread
    phase = positions[:, None] * factors[None, :] % seq_len
    angle = phase.astype(jnp.float32) * (2.0 * math.pi / seq_len)
    return jnp.concatenate([jnp.cos(angle), jnp.sin(angle)], axis=1)

def envelope_of(steps_float, rates, seq_len):
    return jnp.exp(-rates[None, :] * steps_float[:, None]) * jnp.sqrt(2.0 * rates + 1.0 / seq_len)[None, :]

def reference(projected, short_weight, decay_rates, first_weight, second_weight, out_weight, cotangent):
    block = min(512, D)
    rim = SHORT - 1
    length = 2 * SEQ
    positions = jnp.arange(SEQ, dtype=jnp.int32)
    embedded = positional(positions, SEQ, E)
    first_pre = jnp.dot(embedded, first_weight, precision=precise, preferred_element_type=jnp.float32)
    first_act = jnp.sin(first_pre)
    second_pre = jnp.dot(first_act, second_weight, precision=precise, preferred_element_type=jnp.float32)
    second_act = jnp.sin(second_pre)
    steps_float = positions.astype(jnp.float32)

    def one_block(start):
        raw_block = lax.dynamic_slice_in_dim(projected, start, block, 3)
        cot_block = lax.dynamic_slice_in_dim(cotangent, start, block, 2)
        taps = lax.dynamic_slice_in_dim(short_weight, start, block, 2)
        rate_block = lax.dynamic_slice_in_dim(decay_rates, start, block, 0)
        out_block = lax.dynamic_slice_in_dim(out_weight, start, block, 1)
        padded = jnp.pad(raw_block, ((0, 0), (0, 0), (rim, 0), (0, 0)))
        featured = taps[:, 0][:, None, None, :] * padded[:, :, rim:rim + SEQ]
        for offset in range(1, rim + 1):
            featured = featured + taps[:, offset][:, None, None, :] * padded[:, :, rim - offset:rim - offset + SEQ]
        feat_q, feat_k, feat_v = (featured[0], featured[1], featured[2])
        product = feat_k * feat_v
        envelope = envelope_of(steps_float, rate_block, SEQ)
        kernel = jnp.dot(second_act, out_block, precision=precise, preferred_element_type=jnp.float32) * envelope
        prod_freq = jnp.fft.rfft(product, n=length, axis=1)
        kern_freq = jnp.fft.rfft(kernel, n=length, axis=0)[None]
        convolved = jnp.fft.irfft(prod_freq * kern_freq, n=length, axis=1)[:, :SEQ]
        mixed = feat_q * convolved
        grad_query = cot_block * convolved
        grad_conv = cot_block * feat_q
        grad_freq = jnp.fft.rfft(grad_conv, n=length, axis=1)
        grad_prod = jnp.fft.irfft(jnp.conj(kern_freq) * grad_freq, n=length, axis=1)[:, :SEQ]
        kernel_grad_raw = jnp.fft.irfft(lax.optimization_barrier(jnp.sum(jnp.conj(prod_freq) * grad_freq, axis=0)), n=length, axis=0)[:SEQ]
        grad_feat = jnp.stack([grad_query, grad_prod * feat_v, grad_prod * feat_k])
        padded_back = jnp.pad(grad_feat, ((0, 0), (0, 0), (0, rim), (0, 0)))
        raw_grad = taps[:, 0][:, None, None, :] * padded_back[:, :, 0:SEQ]
        for offset in range(1, rim + 1):
            raw_grad = raw_grad + taps[:, offset][:, None, None, :] * padded_back[:, :, offset:offset + SEQ]
        short_grad = jnp.stack([lax.optimization_barrier(jnp.sum(grad_feat * padded[:, :, rim - offset:rim - offset + SEQ], axis=(1, 2))) for offset in range(rim + 1)], axis=1)
        kernel_grad = kernel_grad_raw * envelope
        out_grad = jnp.dot(second_act.T, kernel_grad, precision=precise, preferred_element_type=jnp.float32)
        act_grad = jnp.dot(kernel_grad, out_block.T, precision=precise, preferred_element_type=jnp.float32)
        return (mixed, raw_grad, short_grad, out_grad, act_grad)
    starts = jnp.arange(D // block, dtype=jnp.int32) * block
    mixed, raw_grad, short_grad, out_grad, act_grad = lax.map(one_block, starts)
    tail_scale = 1.0 / math.sqrt(WINS * SEQ)
    mixed = jnp.moveaxis(mixed, 0, 2).reshape(WINS, SEQ, D)
    raw_grad = jnp.moveaxis(raw_grad, 0, 3).reshape(3, WINS, SEQ, D)
    short_grad = jnp.moveaxis(short_grad, 0, 2).reshape(3, SHORT, D) * tail_scale
    out_grad = jnp.moveaxis(out_grad, 0, 1).reshape(MH, D) * tail_scale
    act_grad = lax.optimization_barrier(jnp.sum(act_grad, axis=0))
    grad_scale = 4.0 / math.sqrt(WINS * SEQ * D)
    second_grad_pre = act_grad * jnp.cos(second_pre)
    second_grad = jnp.dot(first_act.T, second_grad_pre, precision=precise, preferred_element_type=jnp.float32) * grad_scale
    first_grad_pre = jnp.dot(second_grad_pre, second_weight.T, precision=precise, preferred_element_type=jnp.float32) * jnp.cos(first_pre)
    first_grad = jnp.dot(embedded.T, first_grad_pre, precision=precise, preferred_element_type=jnp.float32) * grad_scale
    return (mixed, raw_grad, short_grad, out_grad, first_grad, second_grad)
```

```python
import functools
import math

import jax
import jax.numpy as jnp
import ml_dtypes
import numpy as np
from jax import lax
from jax.experimental import pallas as pl
from jax.experimental.pallas import tpu as pltpu
from jax.sharding import PartitionSpec as P

MESH = pl.DeviceIdType.MESH
ROWS = 64
OWN = 16
LANES = 128
SEQ = ROWS * ROWS
RIM = 6
STEP = 512
FLOAT = jnp.float32
HALF = jnp.bfloat16


def halves(table):
    high = table.astype(ml_dtypes.bfloat16)
    low = (table - high.astype(np.float64)).astype(ml_dtypes.bfloat16)
    return high, low


@functools.cache
def tables():
    k = np.arange(ROWS)[:, None] + 0.25
    s = np.arange(ROWS)[None, :]
    theta = 2 * np.pi * k * s / ROWS
    first = np.concatenate([np.cos(theta), -np.sin(theta)], axis=0)
    high, low = halves(first)
    first_stack = np.concatenate([high, high, low], axis=1)
    last = np.concatenate([np.cos(theta).T, -np.sin(theta).T], axis=1) / SEQ
    high, low = halves(last)
    last_stack = np.concatenate([high, high, low], axis=1)
    phi = 2 * np.pi * k * s / SEQ
    turn = np.stack([np.tile(np.cos(phi), (1, 2)), np.tile(np.sin(phi), (1, 2))]).astype(np.float32)
    inner = 2 * np.pi * (np.arange(ROWS)[:, None] * s % ROWS) / ROWS
    cos, sin = np.kron(np.eye(2), np.cos(inner)), np.kron(np.eye(2), np.sin(inner))
    there = np.block([[cos, -sin], [sin, cos]])
    back = np.block([[cos, sin], [-sin, cos]])
    middle = np.stack(halves(there) + halves(back))
    half = 16
    orders = np.arange(half, dtype=np.int64)
    factors = 1 + (SEQ // 2 - 2) * orders * orders // max((half - 1) ** 2, 1)
    angle = 2 * np.pi * (factors[:, None] * np.arange(SEQ)[None, :] % SEQ) / SEQ
    embedded = np.concatenate([np.cos(angle), np.sin(angle)], axis=0).astype(np.float32)
    return first_stack, last_stack, turn, middle, embedded


def split(value):
    high = value.astype(HALF)
    return high, (value - high.astype(FLOAT)).astype(HALF)


def dot(a, b, kind="nn"):
    dims = {"nn": ((1,), (0,)), "nt": ((1,), (1,))}[kind]
    return lax.dot_general(a, b, (dims, ((), ())), preferred_element_type=FLOAT)


def dot3(a, b, kind="nn"):
    ah, al = split(a)
    bh, bl = split(b)
    return dot(ah, bh, kind) + (dot(ah, bl, kind) + dot(al, bh, kind))


def sin_cos(x):
    n = jnp.floor(x * (2.0 / math.pi) + 0.5)
    r = x - n * 1.5703125
    r = r - n * 4.837512969970703125e-4
    r = r - n * 7.549789948768648e-8
    z = r * r
    s = r + r * z * (-1.6666654611e-1 + z * (8.3321608736e-3 + z * -1.9515295891e-4))
    c = 1.0 - 0.5 * z + z * z * (4.166664568298827e-2 + z * (-1.388731625493765e-3 + z * 2.443315711809948e-5))
    q = n.astype(jnp.int32)
    odd = (q & 1) == 1
    sin = jnp.where(odd, c, s)
    cos = jnp.where(odd, s, c)
    sin = jnp.where((q & 2) == 2, -sin, sin)
    cos = jnp.where(((q + 1) & 2) == 2, -cos, cos)
    return sin, cos


def exchange_kernel(same, x_ref, o_ref, send_sem, recv_sem, here_sem):
    me = lax.axis_index("seq")
    barrier = pltpu.get_barrier_semaphore()

    def greet(i, carry):
        pl.semaphore_signal(
            barrier, inc=1, device_id={"seq": lax.rem(me + i, ROWS)}, device_id_type=MESH
        )
        return carry

    lax.fori_loop(1, ROWS, greet, 0)
    pl.semaphore_wait(barrier, ROWS - 1)
    block = (lambda i: x_ref) if same else (lambda i: x_ref.at[i])
    here = pltpu.make_async_copy(block(me), o_ref.at[me], here_sem)
    here.start()

    def send(i, carry):
        z = lax.rem(me // 16 + lax.rem(i, 4), 4)
        x = lax.rem(lax.rem(me // 4, 4) + lax.rem(i // 4, 4), 4)
        y = lax.rem(lax.rem(me, 4) + i // 16, 4)
        peer = z * 16 + x * 4 + y
        pltpu.make_async_remote_copy(
            src_ref=block(peer),
            dst_ref=o_ref.at[me],
            send_sem=send_sem,
            recv_sem=recv_sem,
            device_id={"seq": peer},
            device_id_type=MESH,
        ).start()
        return carry

    lax.fori_loop(1, ROWS, send, 0)
    here.wait()
    pltpu.make_async_remote_copy(
        src_ref=o_ref.at[pl.ds(0, ROWS - 1)],
        dst_ref=o_ref.at[pl.ds(0, ROWS - 1)],
        send_sem=send_sem,
        recv_sem=recv_sem,
        device_id={"seq": me},
        device_id_type=MESH,
    ).wait()


def exchange(value, collective_id, same=False):
    shape = (ROWS,) + value.shape if same else value.shape
    return pl.pallas_call(
        functools.partial(exchange_kernel, same),
        out_shape=jax.ShapeDtypeStruct(shape, FLOAT),
        in_specs=[pl.BlockSpec(memory_space=pl.ANY)],
        out_specs=pl.BlockSpec(memory_space=pl.ANY),
        scratch_shapes=[pltpu.SemaphoreType.DMA] * 3,
        compiler_params=pltpu.CompilerParams(collective_id=collective_id, has_side_effects=True),
        name="exchange%d" % collective_id,
    )(value)


def feature_kernel(proj_ref, rim_ref, taps_ref, cot_ref, feat_ref, send_ref, ext):
    ext[:, :, :8, :] = rim_ref[...]
    ext[:, :, 8:, :] = proj_ref[...]
    feats = [[None, None] for _ in range(3)]
    for i in range(3):
        for w in range(2):
            total = taps_ref[i, 0:1, :] * ext[i, w, 8:, :]
            for j in range(1, RIM + 1):
                total = total + taps_ref[i, j : j + 1, :] * ext[i, w, 8 - j : 8 - j + ROWS, :]
            feats[i][w] = total
            feat_ref[i, w] = total
    product = jnp.concatenate([feats[1][w] * feats[2][w] for w in range(2)], axis=0)
    grad = jnp.concatenate([cot_ref[w] * feats[0][w] for w in range(2)], axis=0)
    send_ref[:, :OWN, :] = product.T.reshape(8, OWN, LANES)
    send_ref[:, OWN:, :] = grad.T.reshape(8, OWN, LANES)


def by_channels(shape, size=LANES):
    block = shape[:-1] + (size,)
    lead = len(shape) - 1
    return pl.BlockSpec(block, lambda c: (0,) * lead + (c,))


def features(projected, rim, taps, cotangent):
    blocks = projected.shape[-1] // LANES
    return pl.pallas_call(
        feature_kernel,
        grid=(blocks,),
        out_shape=(
            jax.ShapeDtypeStruct(projected.shape, FLOAT),
            jax.ShapeDtypeStruct((ROWS, 2 * OWN, LANES), FLOAT),
        ),
        in_specs=[by_channels(v.shape) for v in (projected, rim, taps, cotangent)],
        out_specs=(
            by_channels(projected.shape),
            pl.BlockSpec((8, 2 * OWN, LANES), lambda c: (c, 0, 0)),
        ),
        scratch_shapes=[pltpu.VMEM((3, 2, ROWS + 8, LANES), FLOAT)],
        name="features",
    )(projected, rim, taps, cotangent)


def owner_kernel(
    scale_ref,
    got_ref,
    emb_ref,
    w1t_ref,
    w2t_ref,
    w2_ref,
    wot_ref,
    wo_ref,
    first_ref,
    last_ref,
    turn_ref,
    middle_ref,
    back_ref,
    out_ref,
    net_ref,
    act1,
    cos1,
    act2,
    cos2,
    filt,
    fgrad,
):
    lane = lax.broadcasted_iota(jnp.int32, (OWN, LANES), 1)
    low_half = lane < ROWS

    def net(step, carry):
        cols = pl.ds(pl.multiple_of(step * STEP, STEP), STEP)
        pre1 = dot3(w1t_ref[...], emb_ref[:, cols])
        s1, c1 = sin_cos(pre1)
        act1[:, cols] = s1
        cos1[:, cols] = c1
        pre2 = dot3(w2t_ref[...], s1)
        s2, c2 = sin_cos(pre2)
        act2[:, cols] = s2
        cos2[:, cols] = c2
        raw = dot3(wot_ref[...], s2)
        for pair in range(STEP // LANES):
            both = raw[:, pair * LANES : (pair + 1) * LANES]
            turned = pltpu.roll(both, ROWS, 1)
            base = pl.multiple_of((step * (STEP // ROWS) + 2 * pair) * OWN, OWN)
            filt[pl.ds(base, OWN), :] = jnp.where(low_half, both, turned)
            filt[pl.ds(base + OWN, OWN), :] = jnp.where(low_half, turned, both)
        return carry

    lax.fori_loop(0, SEQ // STEP, net, 0)

    place = lax.broadcasted_iota(jnp.int32, (ROWS, LANES), 0) * ROWS + (
        lax.broadcasted_iota(jnp.int32, (ROWS, LANES), 1) & (ROWS - 1)
    )
    place = place.astype(FLOAT)

    def channel(ch, carry):
        cos, sin = turn_ref[0], turn_ref[1]
        envelope = jnp.exp(place * -scale_ref[0, ch]) * scale_ref[1, ch]
        prod = got_ref[pl.ds(ch, ROWS, stride=2 * OWN), :]
        grad = got_ref[pl.ds(ch + OWN, ROWS, stride=2 * OWN), :]
        kern = filt[pl.ds(ch, ROWS, stride=OWN), :] * envelope
        high, low = split(jnp.concatenate([prod, grad, kern], axis=1))
        spec = dot(first_ref[...], jnp.concatenate([high, low, high], axis=0))
        rows = []
        for i in range(3):
            re = spec[:ROWS, i * LANES : (i + 1) * LANES]
            im = spec[ROWS:, i * LANES : (i + 1) * LANES]
            rows.append(jnp.concatenate([re * cos + im * sin, im * cos - re * sin], axis=1))
        high, low = split(jnp.concatenate(rows, axis=0))
        freq = dot(high, middle_ref[0]) + (dot(low, middle_ref[0]) + dot(high, middle_ref[1]))
        pr, pi = freq[:ROWS, :LANES], freq[:ROWS, LANES:]
        gr, gi = freq[ROWS : 2 * ROWS, :LANES], freq[ROWS : 2 * ROWS, LANES:]
        kr, ki = freq[2 * ROWS :, :LANES], freq[2 * ROWS :, LANES:]
        cr, ci = pr * gr + pi * gi, pr * gi - pi * gr
        cr, ci = cr + pltpu.roll(cr, ROWS, 1), ci + pltpu.roll(ci, ROWS, 1)
        rows = [
            jnp.concatenate([pr * kr - pi * ki, pr * ki + pi * kr], axis=1),
            jnp.concatenate([kr * gr + ki * gi, kr * gi - ki * gr], axis=1),
            jnp.concatenate([cr, ci], axis=1),
        ]
        high, low = split(jnp.concatenate(rows, axis=0))
        freq = dot(high, middle_ref[2]) + (dot(low, middle_ref[2]) + dot(high, middle_ref[3]))
        cols = []
        for i in range(3):
            re = freq[i * ROWS : (i + 1) * ROWS, :LANES]
            im = freq[i * ROWS : (i + 1) * ROWS, LANES:]
            cols.append(jnp.concatenate([re * cos - im * sin, re * sin + im * cos], axis=0))
        high, low = split(jnp.concatenate(cols, axis=1))
        time = dot(last_ref[...], jnp.concatenate([high, low, high], axis=0))
        back_ref[pl.ds(ch, ROWS, stride=2 * OWN), :] = time[:, :LANES]
        back_ref[pl.ds(ch + OWN, ROWS, stride=2 * OWN), :] = time[:, LANES : 2 * LANES]
        fgrad[pl.ds(ch, ROWS, stride=OWN), :] = time[:, 2 * LANES :] * envelope
        return carry

    lax.fori_loop(0, OWN, channel, 0)

    out_ref[...] = jnp.zeros_like(out_ref)
    net_ref[...] = jnp.zeros_like(net_ref)

    def net_back(step, carry):
        cols = pl.ds(pl.multiple_of(step * STEP, STEP), STEP)
        parts = []
        for pair in range(STEP // LANES):
            base = pl.multiple_of((step * (STEP // ROWS) + 2 * pair) * OWN, OWN)
            parts.append(
                jnp.where(low_half, fgrad[pl.ds(base, OWN), :], fgrad[pl.ds(base + OWN, OWN), :])
            )
        kgrad = jnp.concatenate(parts, axis=1)
        out_ref[...] += dot3(kgrad, act2[:, cols], "nt")
        pre2 = dot3(wo_ref[...], kgrad) * cos2[:, cols]
        net_ref[32:, :] += dot3(act1[:, cols], pre2, "nt")
        pre1 = dot3(w2_ref[...], pre2) * cos1[:, cols]
        net_ref[:32, :] += dot3(emb_ref[:, cols], pre1, "nt")
        return carry

    lax.fori_loop(0, SEQ // STEP, net_back, 0)


def owner(scale, got, w1, w2, wo):
    first_stack, last_stack, turn, middle, embedded = tables()
    vmem = pl.BlockSpec(memory_space=pltpu.VMEM)
    hidden = w2.shape[0]
    return pl.pallas_call(
        owner_kernel,
        out_shape=(
            jax.ShapeDtypeStruct((ROWS * 2 * OWN, LANES), FLOAT),
            jax.ShapeDtypeStruct((OWN, hidden), FLOAT),
            jax.ShapeDtypeStruct((w1.shape[0] + hidden, hidden), FLOAT),
        ),
        in_specs=[pl.BlockSpec(memory_space=pltpu.SMEM)] + [vmem] * 11,
        out_specs=(vmem, vmem, vmem),
        scratch_shapes=[pltpu.VMEM((hidden, SEQ), FLOAT)] * 4
        + [pltpu.VMEM((ROWS * OWN, LANES), FLOAT)] * 2,
        compiler_params=pltpu.CompilerParams(vmem_limit_bytes=40 << 20),
        name="owner",
    )(
        scale,
        got.reshape(ROWS * 2 * OWN, LANES),
        jnp.asarray(embedded),
        w1.T,
        w2.T,
        w2,
        wo.T,
        wo,
        jnp.asarray(first_stack),
        jnp.asarray(last_stack),
        jnp.asarray(turn),
        jnp.asarray(middle),
    )


def mix_kernel(feat_ref, cot_ref, got_ref, mixed_ref, grad_ref):
    conv = got_ref[:, :OWN, :].reshape(LANES, LANES).T
    back = got_ref[:, OWN:, :].reshape(LANES, LANES).T
    for w in range(2):
        rows = slice(w * ROWS, (w + 1) * ROWS)
        mixed_ref[w] = feat_ref[0, w] * conv[rows]
        grad_ref[0, w] = cot_ref[w] * conv[rows]
        grad_ref[1, w] = back[rows] * feat_ref[2, w]
        grad_ref[2, w] = back[rows] * feat_ref[1, w]


def mix(feat, cotangent, got):
    return pl.pallas_call(
        mix_kernel,
        grid=(feat.shape[-1] // LANES,),
        out_shape=(
            jax.ShapeDtypeStruct(cotangent.shape, FLOAT),
            jax.ShapeDtypeStruct(feat.shape, FLOAT),
        ),
        in_specs=[
            by_channels(feat.shape),
            by_channels(cotangent.shape),
            pl.BlockSpec((8, 2 * OWN, LANES), lambda c: (c, 0, 0)),
        ],
        out_specs=(by_channels(cotangent.shape), by_channels(feat.shape)),
        name="mix",
    )(feat, cotangent, got)


def taps_kernel(grad_ref, next_ref, proj_ref, rim_ref, taps_ref, raw_ref, short_ref, ext, ahead):
    ext[:, :, :8, :] = rim_ref[...]
    ext[:, :, 8:, :] = proj_ref[...]
    ahead[:, :, :ROWS, :] = grad_ref[...]
    ahead[:, :, ROWS:, :] = next_ref[...]
    for i in range(3):
        for w in range(2):
            total = taps_ref[i, 0:1, :] * grad_ref[i, w]
            for j in range(1, RIM + 1):
                total = total + taps_ref[i, j : j + 1, :] * ahead[i, w, j : j + ROWS, :]
            raw_ref[i, w] = total
        for j in range(RIM + 1):
            both = grad_ref[i, 0] * ext[i, 0, 8 - j : 8 - j + ROWS, :]
            both = both + grad_ref[i, 1] * ext[i, 1, 8 - j : 8 - j + ROWS, :]
            short_ref[i, j : j + 1, :] = jnp.sum(both, axis=0, keepdims=True)


def tap_grads(grad, following, projected, rim, taps):
    args = (grad, following, projected, rim, taps)
    return pl.pallas_call(
        taps_kernel,
        grid=(grad.shape[-1] // LANES,),
        out_shape=(
            jax.ShapeDtypeStruct(grad.shape, FLOAT),
            jax.ShapeDtypeStruct(taps.shape, FLOAT),
        ),
        in_specs=[by_channels(v.shape) for v in args],
        out_specs=(by_channels(grad.shape), by_channels(taps.shape)),
        scratch_shapes=[pltpu.VMEM((3, 2, ROWS + 8, LANES), FLOAT)] * 2,
        name="taps",
    )(*args)


def swapped(value, axis, bit):
    count = lax.axis_size(axis)
    return lax.ppermute(value, axis, [(i, i ^ bit) for i in range(count)])


def shards(projected, short_weight, decay_rates, w1, w2, out_weight, cotangent):
    place = lax.axis_index("seq")
    group = projected.shape[-1]
    rim = lax.ppermute(
        projected[:, :, ROWS - 8 :, :], "seq", [(i, i + 1) for i in range(ROWS - 1)]
    )
    feat, sends = features(projected, rim, short_weight, cotangent)
    got = exchange(sends, 1)
    rates = lax.dynamic_slice_in_dim(decay_rates, place * OWN, OWN, 0)
    wo = lax.dynamic_slice_in_dim(out_weight, place * OWN, OWN, 1)
    scale = jnp.stack([rates, jnp.sqrt(2.0 * rates + 1.0 / SEQ)])
    back, out_part, net_part = owner(scale, got, w1, w2, wo)
    back_got = exchange(back.reshape(ROWS, 2 * OWN, LANES), 2)
    small = jnp.concatenate([out_part, net_part], axis=0)
    small = small + swapped(small, "dp", 1)
    out_own, net_sum = small[:OWN], small[OWN:]
    net_sum = net_sum + swapped(net_sum, "chan", 1)
    net_sum = net_sum + swapped(net_sum, "chan", 2)
    mixed, grad = mix(feat, cotangent, back_got)
    following = lax.ppermute(
        grad[:, :, :8, :], "seq", [(i + 1, i) for i in range(ROWS - 1)]
    )
    raw, short = tap_grads(grad, following, projected, rim, short_weight)
    short = short + swapped(short, "dp", 1)
    tap_count = short.shape[0] * short.shape[1]
    pieces = jnp.concatenate(
        [
            jnp.moveaxis(short.reshape(tap_count, ROWS, OWN), 1, 0).reshape(ROWS, tap_count * OWN),
            net_sum.reshape(ROWS, -1),
        ],
        axis=1,
    )
    width = 4 * LANES
    pieces = jnp.pad(pieces, ((0, 0), (0, 2 * width - pieces.shape[1]))).reshape(ROWS, 8, LANES)
    summed = jnp.sum(exchange(pieces, 3), axis=0)
    every = exchange(jnp.concatenate([summed, out_own.reshape(8, LANES)], axis=0), 4, same=True)
    flat = every[:, :4].reshape(ROWS, width)
    short_total = jnp.moveaxis(flat[:, : tap_count * OWN].reshape(ROWS, tap_count, OWN), 0, 1)
    short_total = short_total.reshape(short.shape)
    net_total = flat[:, tap_count * OWN : tap_count * OWN + net_sum.size // ROWS]
    net_total = net_total.reshape(net_sum.shape)
    out_total = every[:, 8:].reshape(group, -1).T
    windows = projected.shape[1] * lax.axis_size("dp")
    tail = 1.0 / math.sqrt(windows * SEQ)
    scale = 4.0 / math.sqrt(windows * SEQ * group * lax.axis_size("chan"))
    split_at = w1.shape[0]
    return (
        mixed,
        raw,
        short_total * tail,
        out_total * tail,
        net_total[:split_at] * scale,
        net_total[split_at:] * scale,
    )


def solution(mesh):
    return jax.shard_map(
        shards,
        mesh=mesh,
        in_specs=(
            P(None, "dp", "seq", "chan"),
            P(None, None, "chan"),
            P("chan"),
            P(),
            P(),
            P(None, "chan"),
            P("dp", "seq", "chan"),
        ),
        out_specs=(
            P("dp", "seq", "chan"),
            P(None, "dp", "seq", "chan"),
            P(None, None, "chan"),
            P(None, "chan"),
            P(),
            P(),
        ),
        check_vma=False,
    )
```

```python
import functools
import math

import jax
import jax.numpy as jnp
import ml_dtypes
import numpy as np
from jax import lax
from jax.experimental import pallas as pl
from jax.experimental.pallas import tpu as pltpu
from jax.sharding import PartitionSpec as P

MESH = pl.DeviceIdType.MESH
ROWS = 64
OWN = 16
LANES = 128
SEQ = ROWS * ROWS
RIM = 6
STEP = 512
FLOAT = jnp.float32
HALF = jnp.bfloat16


def halves(table):
    high = table.astype(ml_dtypes.bfloat16)
    low = (table - high.astype(np.float64)).astype(ml_dtypes.bfloat16)
    return high, low


@functools.cache
def tables():
    k = np.arange(ROWS)[:, None] + 0.25
    s = np.arange(ROWS)[None, :]
    theta = 2 * np.pi * k * s / ROWS
    first = np.concatenate([np.cos(theta), -np.sin(theta)], axis=0)
    high, low = halves(first)
    first_stack = np.concatenate([high, high, low], axis=1)
    last = np.concatenate([np.cos(theta).T, -np.sin(theta).T], axis=1) / SEQ
    high, low = halves(last)
    last_stack = np.concatenate([high, high, low], axis=1)
    phi = 2 * np.pi * k * s / SEQ
    turn = np.stack([np.tile(np.cos(phi), (1, 2)), np.tile(np.sin(phi), (1, 2))]).astype(np.float32)
    inner = 2 * np.pi * (np.arange(ROWS)[:, None] * s % ROWS) / ROWS
    cos, sin = np.kron(np.eye(2), np.cos(inner)), np.kron(np.eye(2), np.sin(inner))
    there = np.block([[cos, -sin], [sin, cos]])
    back = np.block([[cos, sin], [-sin, cos]])
    middle = np.stack(halves(there) + halves(back))
    half = 16
    orders = np.arange(half, dtype=np.int64)
    factors = 1 + (SEQ // 2 - 2) * orders * orders // max((half - 1) ** 2, 1)
    angle = 2 * np.pi * (factors[:, None] * np.arange(SEQ)[None, :] % SEQ) / SEQ
    embedded = np.concatenate([np.cos(angle), np.sin(angle)], axis=0).astype(np.float32)
    return first_stack, last_stack, turn, middle, embedded


def split(value):
    high = value.astype(HALF)
    return high, (value - high.astype(FLOAT)).astype(HALF)


def dot(a, b, kind="nn"):
    dims = {"nn": ((1,), (0,)), "nt": ((1,), (1,))}[kind]
    return lax.dot_general(a, b, (dims, ((), ())), preferred_element_type=FLOAT)


def dot3(a, b, kind="nn"):
    ah, al = split(a)
    bh, bl = split(b)
    return dot(ah, bh, kind) + (dot(ah, bl, kind) + dot(al, bh, kind))


def sin_cos(x):
    n = jnp.floor(x * (2.0 / math.pi) + 0.5)
    r = x - n * 1.5703125
    r = r - n * 4.837512969970703125e-4
    r = r - n * 7.549789948768648e-8
    z = r * r
    s = r + r * z * (-1.6666654611e-1 + z * (8.3321608736e-3 + z * -1.9515295891e-4))
    c = 1.0 - 0.5 * z + z * z * (4.166664568298827e-2 + z * (-1.388731625493765e-3 + z * 2.443315711809948e-5))
    q = n.astype(jnp.int32)
    odd = (q & 1) == 1
    sin = jnp.where(odd, c, s)
    cos = jnp.where(odd, s, c)
    sin = jnp.where((q & 2) == 2, -sin, sin)
    cos = jnp.where(((q + 1) & 2) == 2, -cos, cos)
    return sin, cos


def columns(parts):
    return jnp.concatenate(parts, axis=1)


def forward(signals, first, turn, middle):
    cos, sin = turn[0], turn[1]
    high, low = split(columns(signals))
    spec = dot(first[...], jnp.concatenate([high, low, high], axis=0))
    rows = []
    for i in range(len(signals)):
        re = spec[:ROWS, i * LANES : (i + 1) * LANES]
        im = spec[ROWS:, i * LANES : (i + 1) * LANES]
        rows.append(columns([re * cos + im * sin, im * cos - re * sin]))
    high, low = split(jnp.concatenate(rows, axis=0))
    return dot(high, middle[0]) + (dot(low, middle[0]) + dot(high, middle[1]))


def inverse(rows, last, turn, middle):
    cos, sin = turn[0], turn[1]
    high, low = split(jnp.concatenate(rows, axis=0))
    freq = dot(high, middle[2]) + (dot(low, middle[2]) + dot(high, middle[3]))
    cols = []
    for i in range(len(rows)):
        re = freq[i * ROWS : (i + 1) * ROWS, :LANES]
        im = freq[i * ROWS : (i + 1) * ROWS, LANES:]
        cols.append(jnp.concatenate([re * cos - im * sin, re * sin + im * cos], axis=0))
    high, low = split(columns(cols))
    return dot(last[...], jnp.concatenate([high, low, high], axis=0))


def times(a, b):
    ar, ai, br, bi = a[:, :LANES], a[:, LANES:], b[:, :LANES], b[:, LANES:]
    return columns([ar * br - ai * bi, ar * bi + ai * br])


def times_conj(a, b):
    ar, ai, br, bi = a[:, :LANES], a[:, LANES:], b[:, :LANES], b[:, LANES:]
    return columns([ar * br + ai * bi, ar * bi - ai * br])


def flipped(small):
    rows, cols = small.shape
    tall = jnp.concatenate([small, jnp.zeros((LANES - rows, cols), FLOAT)], axis=0)
    square = columns([tall, jnp.zeros((LANES, LANES - cols), FLOAT)]) if cols < LANES else tall
    return square.T


def remote(src, dst, send_sem, recv_sem, device):
    return pltpu.make_async_remote_copy(
        src_ref=src,
        dst_ref=dst,
        send_sem=send_sem,
        recv_sem=recv_sem,
        device_id=device,
        device_id_type=MESH,
    )


GROUP = 4
AREA = ROWS * OWN


def whole_kernel(
    rates_ref,
    proj_ref,
    taps_ref,
    cot_ref,
    emb_ref,
    w1_ref,
    w2_ref,
    wo_ref,
    first_ref,
    last_ref,
    turn_ref,
    middle_ref,
    mixed_ref,
    raw_ref,
    short_ref,
    out_ref,
    netf_ref,
    nets_ref,
    ext,
    ahead,
    feat,
    sends,
    got,
    backs,
    home,
    act1,
    cos1,
    act2,
    cos2,
    filt,
    fspec,
    pspec,
    small,
    small_dp,
    by_chan,
    outs,
    tiles,
    phase1,
    sum1,
    phase2,
    sum2,
    phase3,
    acc_out,
    acc_net,
    here,
    sent,
    came,
):
    me = lax.axis_index("seq")
    chan = lax.axis_index("chan")
    core = lax.axis_index("dp")
    z, xy = me // 16, lax.rem(me, 16)
    blocks = proj_ref.shape[3] // LANES
    barrier = pltpu.get_barrier_semaphore()

    load = pltpu.make_async_copy(proj_ref, ext.at[:, :, pl.ds(8, ROWS), :], here)
    load.start()

    def signal(**device):
        pl.semaphore_signal(barrier, inc=1, device_id=device, device_id_type=MESH)

    def greet(i, carry):
        signal(seq=lax.rem(me + i, ROWS))
        return carry

    lax.fori_loop(1, ROWS, greet, 0)
    for dz in range(4):
        signal(seq=lax.rem(z + dz, 4) * 16 + xy, dp=1 - core)
    for dc in range(1, 4):
        signal(chan=lax.rem(chan + dc, 4))
    load.wait()
    pl.semaphore_wait(barrier, ROWS - 1 + 7)

    rim = remote(
        ext.at[:, :, pl.ds(ROWS, 8), :],
        ext.at[:, :, pl.ds(0, 8), :],
        sent.at[0],
        came.at[0],
        {"seq": lax.rem(me + 1, ROWS)},
    )
    rim.start()
    rim.wait()

    @pl.when(me == 0)
    def _():
        ext[:, :, :8, :] = jnp.zeros((3, 2, 8, ext.shape[3]), FLOAT)

    def lanes(b):
        return pl.ds(pl.multiple_of(b * LANES, LANES), LANES)

    def tapped(i, w, cols):
        total = taps_ref[i, 0:1, cols] * ext[i, w, 8:, cols]
        for j in range(1, RIM + 1):
            total = total + taps_ref[i, j : j + 1, cols] * ext[i, w, 8 - j : 8 - j + ROWS, cols]
        feat[i, w, :, cols] = total
        return total

    def to_peers(source, target, signal_at, sem):
        base = signal_at * AREA
        mine = pl.ds(pl.multiple_of(base + me * OWN, OWN), OWN)
        target[mine, :] = source[mine, :]

        def send(i, carry):
            px = lax.rem(lax.rem(me // 4, 4) + lax.rem(i // 4, 4), 4)
            py = lax.rem(lax.rem(me, 4) + i // 16, 4)
            peer = lax.rem(z + lax.rem(i, 4), 4) * 16 + px * 4 + py
            block = pl.ds(pl.multiple_of(base + peer * OWN, OWN), OWN)
            remote(source.at[block], target.at[mine], sent.at[sem], came.at[sem], {"seq": peer}).start()
            return carry

        lax.fori_loop(1, ROWS, send, 0)

    def peers_done(ref, sem):
        part = ref.at[pl.ds(0, AREA - OWN)]
        return remote(part, part, sent.at[sem], came.at[sem], {"seq": me})

    def products(b, carry):
        cols = lanes(b)
        parts = [tapped(1, w, cols) * tapped(2, w, cols) for w in range(2)]
        rows = pl.ds(pl.multiple_of(b * LANES, LANES), LANES)
        sends[rows, :] = jnp.concatenate(parts, axis=0).T
        return carry

    lax.fori_loop(0, blocks, products, 0)
    to_peers(sends, got, 0, 1)

    def gradients(b, carry):
        cols = lanes(b)
        parts = [tapped(0, w, cols) * cot_ref[w, :, cols] for w in range(2)]
        rows = pl.ds(pl.multiple_of(AREA + b * LANES, LANES), LANES)
        sends[rows, :] = jnp.concatenate(parts, axis=0).T
        return carry

    lax.fori_loop(0, blocks, gradients, 0)
    to_peers(sends, got, 1, 2)

    turned = pltpu.roll(
        wo_ref[:, lanes(me // 8)], lax.rem(LANES - lax.rem(me, 8) * OWN, LANES), 1
    )
    wo_own = turned[:, :OWN]
    wo_t = flipped(turned)[:OWN, :ROWS]
    w1_t = flipped(w1_ref[...])[:ROWS, : w1_ref.shape[0]]
    w2_t = flipped(w2_ref[...])[:ROWS, :ROWS]
    lane = lax.broadcasted_iota(jnp.int32, (OWN, LANES), 1)
    low_half = lane < ROWS

    def net(step, carry):
        cols = pl.ds(pl.multiple_of(step * STEP, STEP), STEP)
        s1, c1 = sin_cos(dot3(w1_t, emb_ref[:, cols]))
        act1[:, cols] = s1
        cos1[:, cols] = c1
        s2, c2 = sin_cos(dot3(w2_t, s1))
        act2[:, cols] = s2
        cos2[:, cols] = c2
        raw = dot3(wo_t, s2)
        for pair in range(STEP // LANES):
            both = raw[:, pair * LANES : (pair + 1) * LANES]
            other = pltpu.roll(both, ROWS, 1)
            base = pl.multiple_of((step * (STEP // ROWS) + 2 * pair) * OWN, OWN)
            filt[pl.ds(base, OWN), :] = jnp.where(low_half, both, other)
            filt[pl.ds(base + OWN, OWN), :] = jnp.where(low_half, other, both)
        return carry

    lax.fori_loop(0, SEQ // STEP, net, 0)

    place = lax.broadcasted_iota(jnp.int32, (ROWS, LANES), 0) * ROWS + (
        lax.broadcasted_iota(jnp.int32, (ROWS, LANES), 1) & (ROWS - 1)
    )
    place = place.astype(FLOAT)

    def envelope(ch):
        rate = rates_ref[me * OWN + ch]
        return jnp.exp(place * -rate) * jnp.sqrt(jnp.full((1, LANES), 2.0 * rate + 1.0 / SEQ, FLOAT))

    def strided(ref, base, ch):
        return ref[pl.ds(base + ch, ROWS, stride=OWN), :]

    def group_rows(step):
        return pl.ds(pl.multiple_of(step * GROUP * ROWS, GROUP * ROWS), GROUP * ROWS)

    def cut(value):
        return [value[i * ROWS : (i + 1) * ROWS] for i in range(GROUP)]

    def filters(step, carry):
        chans = [step * GROUP + i for i in range(GROUP)]
        signals = [strided(filt, 0, ch) * envelope(ch) for ch in chans]
        fspec[group_rows(step), :] = forward(signals, first_ref, turn_ref, middle_ref)
        return carry

    lax.fori_loop(0, OWN // GROUP, filters, 0)

    def put(value, base, step):
        for i in range(GROUP):
            backs[pl.ds(base + step * GROUP + i, ROWS, stride=OWN), :] = value[
                :, i * LANES : (i + 1) * LANES
            ]

    peers_done(got, 1).wait_recv()

    def convolve(step, carry):
        signals = [strided(got, 0, step * GROUP + i) for i in range(GROUP)]
        spec = forward(signals, first_ref, turn_ref, middle_ref)
        pspec[group_rows(step), :] = spec
        rows = cut(times(spec, fspec[group_rows(step), :]))
        put(inverse(rows, last_ref, turn_ref, middle_ref), 0, step)
        return carry

    lax.fori_loop(0, OWN // GROUP, convolve, 0)
    to_peers(backs, home, 0, 3)
    peers_done(got, 2).wait_recv()

    def correlate(step, carry):
        signals = [strided(got, AREA, step * GROUP + i) for i in range(GROUP)]
        spec = forward(signals, first_ref, turn_ref, middle_ref)
        rows = cut(times_conj(fspec[group_rows(step), :], spec))
        put(inverse(rows, last_ref, turn_ref, middle_ref), AREA, step)
        pair = times_conj(pspec[group_rows(step), :], spec)
        re, im = pair[:, :LANES], pair[:, LANES:]
        pspec[group_rows(step), :] = columns(
            [re + pltpu.roll(re, ROWS, 1), im + pltpu.roll(im, ROWS, 1)]
        )
        return carry

    lax.fori_loop(0, OWN // GROUP, correlate, 0)
    to_peers(backs, home, 1, 4)

    def filter_back(step, carry):
        rows = cut(pspec[group_rows(step), :])
        value = inverse(rows, last_ref, turn_ref, middle_ref)
        for i in range(GROUP):
            ch = step * GROUP + i
            filt[pl.ds(ch, ROWS, stride=OWN), :] = value[:, i * LANES : (i + 1) * LANES] * envelope(ch)
        return carry

    lax.fori_loop(0, OWN // GROUP, filter_back, 0)
    acc_out[...] = jnp.zeros_like(acc_out)
    acc_net[...] = jnp.zeros_like(acc_net)

    def net_back(step, carry):
        cols = pl.ds(pl.multiple_of(step * STEP, STEP), STEP)
        parts = []
        for pair in range(STEP // LANES):
            base = pl.multiple_of((step * (STEP // ROWS) + 2 * pair) * OWN, OWN)
            parts.append(jnp.where(low_half, filt[pl.ds(base, OWN), :], filt[pl.ds(base + OWN, OWN), :]))
        kgrad = columns(parts)
        acc_out[...] += dot3(kgrad, act2[:, cols], "nt")
        pre2 = dot3(wo_own, kgrad) * cos2[:, cols]
        acc_net[32:, :] += dot3(act1[:, cols], pre2, "nt")
        pre1 = dot3(w2_ref[...], pre2) * cos1[:, cols]
        acc_net[:32, :] += dot3(emb_ref[:, cols], pre1, "nt")
        return carry

    lax.fori_loop(0, SEQ // STEP, net_back, 0)
    small[:48, :] = columns([acc_net[:48, :], acc_net[48:, :]])
    small[48:, :] = columns([acc_out[:8, :], acc_out[8:, :]])
    swap = remote(small, small_dp, sent.at[5], came.at[5], {"dp": 1 - core})
    swap.start()
    swap.wait()
    total = small[...] + small_dp[...]
    by_chan[chan] = total[:48]
    outs[z, xy] = total[48:]
    for d in range(1, 4):
        remote(by_chan.at[chan], by_chan.at[chan], sent.at[6], came.at[6], {"chan": lax.rem(chan + d, 4)}).start()
        remote(outs.at[z, xy], outs.at[z, xy], sent.at[7], came.at[7], {"seq": lax.rem(z + d, 4) * 16 + xy}).start()
    chans_done = remote(by_chan.at[pl.ds(0, 3)], by_chan.at[pl.ds(0, 3)], sent.at[6], came.at[6], {"seq": me})
    zs_done = remote(outs.at[pl.ds(0, 3), 0], outs.at[pl.ds(0, 3), 0], sent.at[7], came.at[7], {"seq": me})
    zs_done.wait()

    def around(i):
        return lax.rem(xy // 4 + i // 4, 4) * 4 + lax.rem(lax.rem(xy, 4) + lax.rem(i, 4), 4)

    def spread_outs(i, carry):
        column = outs.at[:, xy]
        remote(column, column, sent.at[8], came.at[8], {"seq": z * 16 + around(i)}).start()
        return carry

    lax.fori_loop(1, 16, spread_outs, 0)
    chans_done.wait()
    net_sum = (by_chan[0] + by_chan[1]) + (by_chan[2] + by_chan[3])
    for i in range(6):
        tiles[24 + i] = net_sum[i * 8 : (i + 1) * 8]
    tiles[30] = jnp.zeros((8, LANES), FLOAT)
    tiles[31] = jnp.zeros((8, LANES), FLOAT)

    peers_done(home, 3).wait_recv()

    def mix(b, carry):
        cols = lanes(b)
        conv = home[pl.ds(pl.multiple_of(b * LANES, LANES), LANES), :].T
        for w in range(2):
            part = conv[w * ROWS : (w + 1) * ROWS]
            mixed_ref[w, :, cols] = feat[0, w, :, cols] * part
            ahead[0, w, :ROWS, cols] = cot_ref[w, :, cols] * part
        return carry

    lax.fori_loop(0, blocks, mix, 0)
    peers_done(home, 4).wait_recv()

    def unmix(b, carry):
        cols = lanes(b)
        back = home[pl.ds(pl.multiple_of(AREA + b * LANES, LANES), LANES), :].T
        for w in range(2):
            part = back[w * ROWS : (w + 1) * ROWS]
            ahead[1, w, :ROWS, cols] = part * feat[2, w, :, cols]
            ahead[2, w, :ROWS, cols] = part * feat[1, w, :, cols]
        return carry

    lax.fori_loop(0, blocks, unmix, 0)
    after = remote(
        ahead.at[:, :, pl.ds(0, 8), :],
        ahead.at[:, :, pl.ds(ROWS, 8), :],
        sent.at[9],
        came.at[9],
        {"seq": lax.rem(me + ROWS - 1, ROWS)},
    )
    after.start()

    def tap_sums(b, carry):
        cols = lanes(b)
        for i in range(3):
            sums = []
            for j in range(RIM + 1):
                both = ahead[i, 0, :ROWS, cols] * ext[i, 0, 8 - j : 8 - j + ROWS, cols]
                both = both + ahead[i, 1, :ROWS, cols] * ext[i, 1, 8 - j : 8 - j + ROWS, cols]
                sums.append(jnp.sum(both, axis=0, keepdims=True))
            sums.append(jnp.zeros((1, LANES), FLOAT))
            tiles[i * 8 + b] = jnp.concatenate(sums, axis=0)
        return carry

    lax.fori_loop(0, blocks, tap_sums, 0)

    phase1[xy] = tiles[pl.ds(2 * xy, 2)]

    def scatter(i, carry):
        q = around(i)
        remote(tiles.at[pl.ds(2 * q, 2)], phase1.at[xy], sent.at[10], came.at[10], {"seq": z * 16 + q}).start()
        return carry

    lax.fori_loop(1, 16, scatter, 0)
    after.wait()

    @pl.when(me == ROWS - 1)
    def _():
        ahead[:, :, ROWS:, :] = jnp.zeros((3, 2, 8, ahead.shape[3]), FLOAT)

    def raws(b, carry):
        cols = lanes(b)
        for i in range(3):
            for w in range(2):
                total = taps_ref[i, 0:1, cols] * ahead[i, w, :ROWS, cols]
                for j in range(1, RIM + 1):
                    total = total + taps_ref[i, j : j + 1, cols] * ahead[i, w, j : j + ROWS, cols]
                raw_ref[i, w, :, cols] = total
        return carry

    lax.fori_loop(0, blocks, raws, 0)
    first15 = phase1.at[pl.ds(0, 15)]
    remote(first15, first15, sent.at[10], came.at[10], {"seq": me}).wait()
    sum1[...] = jnp.sum(phase1[...], axis=0)
    phase2[z * 2 + core] = sum1[...]
    for dz in range(4):
        for dc in range(2):
            if dz or dc:
                to = lax.rem(z + dz, 4) * 16 + xy
                remote(sum1, phase2.at[z * 2 + core], sent.at[11], came.at[11], {"seq": to, "dp": lax.rem(core + dc, 2)}).start()
    first7 = phase2.at[pl.ds(0, 7)]
    remote(first7, first7, sent.at[11], came.at[11], {"seq": me}).wait()
    sum2[...] = jnp.sum(phase2[...], axis=0)
    phase3[xy] = sum2[...]

    def gather(i, carry):
        remote(sum2, phase3.at[xy], sent.at[12], came.at[12], {"seq": z * 16 + around(i)}).start()
        return carry

    lax.fori_loop(1, 16, gather, 0)

    outs_part = outs.at[:, pl.ds(0, 15)]
    remote(outs_part, outs_part, sent.at[8], came.at[8], {"seq": me}).wait()
    windows = 4
    tail = 1.0 / math.sqrt(windows * SEQ)
    scale = 2.0 / math.sqrt(windows * SEQ * blocks * LANES * 4)
    for b in range(blocks):
        rows = []
        for s in range(8 * b, 8 * b + 8):
            tile = outs[s // 16, s % 16]
            rows += [tile, pltpu.roll(tile, ROWS, 1)]
        square = jnp.concatenate(rows, axis=0).T
        out_ref[:, b * LANES : (b + 1) * LANES] = square[:ROWS] * tail

    last15 = phase3.at[pl.ds(0, 15)]
    remote(last15, last15, sent.at[12], came.at[12], {"seq": me}).wait()
    for i in range(3):
        for b in range(blocks):
            t = i * 8 + b
            short_ref[i, :, b * LANES : (b + 1) * LANES] = phase3[t // 2, t % 2][: RIM + 1] * tail
    net_sum = jnp.concatenate([phase3[t // 2, t % 2] for t in range(24, 30)], axis=0) * scale
    netf_ref[...] = net_sum[:32, :ROWS]
    nets_ref[:16, :] = net_sum[32:, :ROWS]
    nets_ref[16:, :] = net_sum[:, ROWS:]
    for sem in (1, 2):
        peers_done(sends, sem).wait_send()
    for sem in (3, 4):
        peers_done(backs, sem).wait_send()


def shards(projected, short_weight, decay_rates, w1, w2, out_weight, cotangent):
    first_stack, last_stack, turn, middle, embedded = tables()
    vmem = pl.BlockSpec(memory_space=pltpu.VMEM)
    group = projected.shape[3]
    hidden = w2.shape[0]

    def buffer(*shape):
        return pltpu.VMEM(shape, FLOAT)

    def like(value):
        return jax.ShapeDtypeStruct(value.shape, FLOAT)

    rows = projected.shape[2] + 8
    return pl.pallas_call(
        whole_kernel,
        out_shape=(
            like(cotangent),
            like(projected),
            like(short_weight),
            like(out_weight),
            like(w1),
            like(w2),
        ),
        in_specs=[pl.BlockSpec(memory_space=pltpu.SMEM), pl.BlockSpec(memory_space=pl.ANY)] + [vmem] * 10,
        out_specs=(vmem,) * 6,
        scratch_shapes=[
            buffer(3, 2, rows, group),
            buffer(3, 2, rows, group),
            buffer(3, 2, ROWS, group),
            buffer(2 * AREA, LANES),
            buffer(2 * AREA, LANES),
            buffer(2 * AREA, LANES),
            buffer(2 * AREA, LANES),
            buffer(hidden, SEQ),
            buffer(hidden, SEQ),
            buffer(hidden, SEQ),
            buffer(hidden, SEQ),
            buffer(AREA, LANES),
            buffer(AREA, 2 * LANES),
            buffer(AREA, 2 * LANES),
            buffer(56, LANES),
            buffer(56, LANES),
            buffer(4, 48, LANES),
            buffer(4, 16, 8, LANES),
            buffer(32, 8, LANES),
            buffer(16, 2, 8, LANES),
            buffer(2, 8, LANES),
            buffer(8, 2, 8, LANES),
            buffer(2, 8, LANES),
            buffer(16, 2, 8, LANES),
            buffer(OWN, hidden),
            buffer(96, hidden),
            pltpu.SemaphoreType.DMA,
            pltpu.SemaphoreType.DMA((13,)),
            pltpu.SemaphoreType.DMA((13,)),
        ],
        compiler_params=pltpu.CompilerParams(
            collective_id=1, has_side_effects=True, vmem_limit_bytes=52 << 20
        ),
        name="whole",
    )(
        decay_rates,
        projected,
        short_weight,
        cotangent,
        jnp.asarray(embedded),
        w1,
        w2,
        out_weight,
        jnp.asarray(first_stack),
        jnp.asarray(last_stack),
        jnp.asarray(turn),
        jnp.asarray(middle),
    )


def solution(mesh):
    return jax.shard_map(
        shards,
        mesh=mesh,
        in_specs=(
            P(None, "dp", "seq", "chan"),
            P(None, None, "chan"),
            P("chan"),
            P(),
            P(),
            P(None, "chan"),
            P("dp", "seq", "chan"),
        ),
        out_specs=(
            P("dp", "seq", "chan"),
            P(None, "dp", "seq", "chan"),
            P(None, None, "chan"),
            P(None, "chan"),
            P(),
            P(),
        ),
        check_vma=False,
    )
```

```python
import functools
import math

import jax
import jax.numpy as jnp
import ml_dtypes
import numpy as np
from jax import lax
from jax.experimental import pallas as pl
from jax.experimental.pallas import tpu as pltpu
from jax.sharding import PartitionSpec as P

MESH = pl.DeviceIdType.MESH
ROWS = 64
OWN = 16
LANES = 128
SEQ = ROWS * ROWS
RIM = 6
STEP = 512
FLOAT = jnp.float32
HALF = jnp.bfloat16


def halves(table):
    high = table.astype(ml_dtypes.bfloat16)
    low = (table - high.astype(np.float64)).astype(ml_dtypes.bfloat16)
    return high, low


@functools.cache
def tables():
    k = np.arange(ROWS)[:, None] + 0.25
    s = np.arange(ROWS)[None, :]
    theta = 2 * np.pi * k * s / ROWS
    first = np.concatenate([np.cos(theta), -np.sin(theta)], axis=0)
    high, low = halves(first)
    first_stack = np.concatenate([high, high, low], axis=1)
    last = np.concatenate([np.cos(theta).T, -np.sin(theta).T], axis=1) / SEQ
    high, low = halves(last)
    last_stack = np.concatenate([high, high, low], axis=1)
    phi = 2 * np.pi * k * s / SEQ
    turn = np.stack([np.tile(np.cos(phi), (1, 2)), np.tile(np.sin(phi), (1, 2))]).astype(np.float32)
    inner = 2 * np.pi * (np.arange(ROWS)[:, None] * s % ROWS) / ROWS
    cos, sin = np.kron(np.eye(2), np.cos(inner)), np.kron(np.eye(2), np.sin(inner))
    there = np.block([[cos, -sin], [sin, cos]])
    back = np.block([[cos, sin], [-sin, cos]])
    middle = np.stack(halves(there) + halves(back))
    half = 16
    orders = np.arange(half, dtype=np.int64)
    factors = 1 + (SEQ // 2 - 2) * orders * orders // max((half - 1) ** 2, 1)
    angle = 2 * np.pi * (factors[:, None] * np.arange(SEQ)[None, :] % SEQ) / SEQ
    embedded = np.concatenate([np.cos(angle), np.sin(angle)], axis=0).astype(np.float32)
    return (*(t.astype(np.float32) for t in (first_stack, last_stack)), turn, middle.astype(np.float32), embedded)


def split(value):
    high = value.astype(HALF)
    return high, (value - high.astype(FLOAT)).astype(HALF)


def dot(a, b, kind="nn"):
    dims = {"nn": ((1,), (0,)), "nt": ((1,), (1,))}[kind]
    return lax.dot_general(a, b, (dims, ((), ())), preferred_element_type=FLOAT)


def dot3(a, b, kind="nn"):
    ah, al = split(a)
    bh, bl = split(b)
    return dot(ah, bh, kind) + (dot(ah, bl, kind) + dot(al, bh, kind))


def sin_cos(x):
    n = jnp.floor(x * (2.0 / math.pi) + 0.5)
    r = x - n * 1.5703125
    r = r - n * 4.837512969970703125e-4
    r = r - n * 7.549789948768648e-8
    z = r * r
    s = r + r * z * (-1.6666654611e-1 + z * (8.3321608736e-3 + z * -1.9515295891e-4))
    c = 1.0 - 0.5 * z + z * z * (4.166664568298827e-2 + z * (-1.388731625493765e-3 + z * 2.443315711809948e-5))
    q = n.astype(jnp.int32)
    odd = (q & 1) == 1
    sin = jnp.where(odd, c, s)
    cos = jnp.where(odd, s, c)
    sin = jnp.where((q & 2) == 2, -sin, sin)
    cos = jnp.where(((q + 1) & 2) == 2, -cos, cos)
    return sin, cos


def columns(parts):
    return jnp.concatenate(parts, axis=1)


def forward(signals, first, turn, middle):
    cos, sin = turn[0], turn[1]
    high, low = split(columns(signals))
    spec = dot(first[...], jnp.concatenate([high, low, high], axis=0))
    rows = []
    for i in range(len(signals)):
        re = spec[:ROWS, i * LANES : (i + 1) * LANES]
        im = spec[ROWS:, i * LANES : (i + 1) * LANES]
        rows.append(columns([re * cos + im * sin, im * cos - re * sin]))
    high, low = split(jnp.concatenate(rows, axis=0))
    return dot(high, middle[0]) + (dot(low, middle[0]) + dot(high, middle[1]))


def inverse(rows, last, turn, middle):
    cos, sin = turn[0], turn[1]
    high, low = split(jnp.concatenate(rows, axis=0))
    freq = dot(high, middle[2]) + (dot(low, middle[2]) + dot(high, middle[3]))
    cols = []
    for i in range(len(rows)):
        re = freq[i * ROWS : (i + 1) * ROWS, :LANES]
        im = freq[i * ROWS : (i + 1) * ROWS, LANES:]
        cols.append(jnp.concatenate([re * cos - im * sin, re * sin + im * cos], axis=0))
    high, low = split(columns(cols))
    return dot(last[...], jnp.concatenate([high, low, high], axis=0))


def times(a, b):
    ar, ai, br, bi = a[:, :LANES], a[:, LANES:], b[:, :LANES], b[:, LANES:]
    return columns([ar * br - ai * bi, ar * bi + ai * br])


def times_conj(a, b):
    ar, ai, br, bi = a[:, :LANES], a[:, LANES:], b[:, :LANES], b[:, LANES:]
    return columns([ar * br + ai * bi, ar * bi - ai * br])


def flipped(small):
    rows, cols = small.shape
    tall = jnp.concatenate([small, jnp.zeros((LANES - rows, cols), FLOAT)], axis=0)
    square = columns([tall, jnp.zeros((LANES, LANES - cols), FLOAT)]) if cols < LANES else tall
    return square.T


def remote(src, dst, send_sem, recv_sem, device):
    return pltpu.make_async_remote_copy(
        src_ref=src,
        dst_ref=dst,
        send_sem=send_sem,
        recv_sem=recv_sem,
        device_id=device,
        device_id_type=MESH,
    )


GROUP = 4
AREA = ROWS * OWN


def whole_kernel(
    rates_ref,
    proj_hbm,
    taps_hbm,
    cot_hbm,
    emb_hbm,
    w1_hbm,
    w2_hbm,
    wo_hbm,
    first_hbm,
    last_hbm,
    turn_hbm,
    middle_hbm,
    mixed_hbm,
    raw_hbm,
    short_ref,
    out_ref,
    netf_ref,
    nets_ref,
    taps_ref,
    cot_ref,
    emb_ref,
    w1_ref,
    w2_ref,
    wo_ref,
    first_wide,
    last_wide,
    turn_ref,
    middle_wide,
    first_ref,
    last_ref,
    middle_ref,
    mixed_ref,
    raw_ref,
    ext,
    ahead,
    feat,
    sends,
    got,
    backs,
    home,
    act1,
    cos1,
    act2,
    cos2,
    filt,
    fspec,
    pspec,
    out_mine,
    out_dp,
    by_chan,
    outs,
    tiles,
    phase1,
    sum1,
    phase2,
    sum2,
    phase3,
    acc_out,
    acc_net,
    edge_kv,
    rim_kv,
    relay,
    after_kv_rows,
    edge_q,
    rim_q,
    after_q_rows,
    loads,
    saves,
    sent,
    came,
):
    me = lax.axis_index("seq")
    chan = lax.axis_index("chan")
    core = lax.axis_index("dp")
    z, xy = me // 16, lax.rem(me, 16)
    x, y = xy // 4, lax.rem(xy, 4)
    following, previous = lax.rem(me + 1, ROWS), lax.rem(me + ROWS - 1, ROWS)
    blocks = feat.shape[3] // LANES
    barrier = pltpu.get_barrier_semaphore()

    def signal(sem, **device):
        pl.semaphore_signal(sem, inc=1, device_id=device, device_id_type=MESH)

    for dz in (2, 1, 3, 0):
        plane = lax.rem(z + dz, 4) * 16

        def greet(i, carry):
            signal(barrier, seq=plane + lax.rem(xy + i, 16))
            return carry

        lax.fori_loop(0 if dz else 1, 16, greet, 0)
        signal(barrier, seq=plane + xy, dp=1 - core)
    for d in range(1, 4):
        signal(barrier, chan=lax.rem(chan + d, 4))

    pairs = [
        (proj_hbm, ext.at[:, :, pl.ds(8, ROWS), :]),
        (taps_hbm, taps_ref),
        (cot_hbm, cot_ref),
        (emb_hbm, emb_ref),
        (w1_hbm, w1_ref),
        (w2_hbm, w2_ref),
        (wo_hbm, wo_ref),
        (first_hbm, first_wide),
        (last_hbm, last_wide),
        (turn_hbm, turn_ref),
        (middle_hbm, middle_wide),
    ]
    copies = [pltpu.make_async_copy(src, dst, loads.at[i]) for i, (src, dst) in enumerate(pairs)]
    for copy in copies:
        copy.start()
    copies[0].wait()
    copies[1].wait()
    def lanes(b):
        return pl.ds(pl.multiple_of(b * LANES, LANES), LANES)

    def tapped(i, w, cols, start, count):
        total = taps_ref[i, 0:1, cols] * ext[i, w, 8 + start : 8 + start + count, cols]
        for j in range(1, RIM + 1):
            rows = slice(8 + start - j, 8 + start - j + count)
            total = total + taps_ref[i, j : j + 1, cols] * ext[i, w, rows, cols]
        feat[i, w, start : start + count, cols] = total

    def later_rows(group):
        def body(b, carry):
            for i in group:
                for w in range(2):
                    tapped(i, w, lanes(b), 8, ROWS - 8)
            return carry

        lax.fori_loop(0, blocks, body, 0)

    def to_peers(source, target, signal_at, sem):
        base = signal_at * AREA
        mine = pl.ds(pl.multiple_of(base + me * OWN, OWN), OWN)
        target[mine, :] = source[mine, :]

        def send(i, carry):
            px, py = lax.rem(x + lax.rem(i // 4, 4), 4), lax.rem(y + i // 16, 4)
            peer = lax.rem(z + lax.rem(i, 4), 4) * 16 + px * 4 + py
            block = pl.ds(pl.multiple_of(base + peer * OWN, OWN), OWN)
            remote(source.at[block], target.at[mine], sent.at[sem], came.at[sem], {"seq": peer}).start()
            return carry

        lax.fori_loop(1, ROWS, send, 0)

    def peers_done(ref, sem):
        part = ref.at[pl.ds(0, AREA - OWN)]
        return remote(part, part, sent.at[sem], came.at[sem], {"seq": me})

    def pack(buffer, features, row):
        for n, (i, w) in enumerate((i, w) for i in features for w in range(2)):
            yield n * RIM, buffer.at[i, w, pl.ds(row, RIM), :]

    def packed(target, buffer, features, row):
        for at, part in pack(buffer, features, row):
            target[at : at + RIM, :] = part[...]

    def unpacked(source, buffer, features, row):
        for at, part in pack(buffer, features, row):
            part[...] = source[at : at + RIM, :]

    def no_rows(buffer, features, row, where):
        @pl.when(me == where)
        def _():
            for i in features:
                buffer[i, :, row : row + 8, :] = jnp.zeros((2, 8, buffer.shape[3]), FLOAT)

    keys = (1, 2)
    edge_q[8:, :] = jnp.zeros((8, edge_q.shape[1]), FLOAT)
    packed(edge_kv, ext, keys, ROWS + 8 - RIM)
    packed(edge_q, ext, (0,), ROWS + 8 - RIM)
    later_rows(keys)
    later_rows((0,))
    pl.semaphore_wait(barrier, ROWS - 1 + 7)

    quarter = edge_kv.shape[1] // 4
    ahead_plane = lax.rem(z + 1, 4) * 16

    def piece(ref, c):
        return ref.at[:, c * quarter : (c + 1) * quarter]

    @pl.when(xy != 15)
    def _():
        remote(edge_kv, rim_kv, sent.at[0], came.at[0], {"seq": following}).start()

    @pl.when(xy == 15)
    def _():
        for c, via in enumerate((3, 12, 0)):
            to = {"seq": z * 16 + via}
            remote(piece(edge_kv, c), piece(relay, c), sent.at[0], came.at[16], to).start()
        remote(piece(edge_kv, 3), piece(rim_kv, 3), sent.at[0], came.at[0], {"seq": following}).start()

    for c, via in enumerate((3, 12, 0)):

        @pl.when(xy == via)
        def _(c=c):
            part = piece(relay, c)
            remote(part, part, sent.at[16], came.at[16], {"seq": me}).wait_recv()
            on = remote(part, piece(rim_kv, c), sent.at[16], came.at[0], {"seq": ahead_plane})
            on.start()
            on.wait_send()

    remote(rim_kv, rim_kv, sent.at[0], came.at[0], {"seq": me}).wait()
    to_q = remote(edge_q, rim_q, sent.at[13], came.at[13], {"seq": following})
    to_q.start()
    unpacked(rim_kv, ext, keys, 8 - RIM)
    no_rows(ext, keys, 0, 0)

    def products(b, carry):
        cols = lanes(b)
        for i in (1, 2):
            for w in range(2):
                tapped(i, w, cols, 0, 8)
        parts = [feat[1, w, :, cols] * feat[2, w, :, cols] for w in range(2)]
        sends[lanes(b), :] = jnp.concatenate(parts, axis=0).T
        return carry

    lax.fori_loop(0, blocks, products, 0)
    to_peers(sends, got, 0, 1)
    to_q.wait()
    unpacked(rim_q, ext, (0,), 8 - RIM)
    no_rows(ext, (0,), 0, 0)
    copies[2].wait()

    def gradients(b, carry):
        cols = lanes(b)
        for w in range(2):
            tapped(0, w, cols, 0, 8)
        parts = [feat[0, w, :, cols] * cot_ref[w, :, cols] for w in range(2)]
        rows = pl.ds(pl.multiple_of(AREA + b * LANES, LANES), LANES)
        sends[rows, :] = jnp.concatenate(parts, axis=0).T
        return carry

    lax.fori_loop(0, blocks, gradients, 0)
    for copy in copies[3:]:
        copy.wait()
    first_ref[...] = first_wide[...].astype(HALF)
    last_ref[...] = last_wide[...].astype(HALF)
    middle_ref[...] = middle_wide[...].astype(HALF)

    turned = pltpu.roll(
        wo_ref[:, lanes(me // 8)], lax.rem(LANES - lax.rem(me, 8) * OWN, LANES), 1
    )
    wo_own = turned[:, :OWN]
    wo_t = flipped(turned)[:OWN, :ROWS]
    w1_t = flipped(w1_ref[...])[:ROWS, : w1_ref.shape[0]]
    w2_t = flipped(w2_ref[...])[:ROWS, :ROWS]
    lane = lax.broadcasted_iota(jnp.int32, (OWN, LANES), 1)
    low_half = lane < ROWS

    def net(step, carry):
        cols = pl.ds(pl.multiple_of(step * STEP, STEP), STEP)
        s1, c1 = sin_cos(dot3(w1_t, emb_ref[:, cols]))
        act1[:, cols] = s1
        cos1[:, cols] = c1
        s2, c2 = sin_cos(dot3(w2_t, s1))
        act2[:, cols] = s2
        cos2[:, cols] = c2
        raw = dot3(wo_t, s2)
        for pair in range(STEP // LANES):
            both = raw[:, pair * LANES : (pair + 1) * LANES]
            other = pltpu.roll(both, ROWS, 1)
            base = pl.multiple_of((step * (STEP // ROWS) + 2 * pair) * OWN, OWN)
            filt[pl.ds(base, OWN), :] = jnp.where(low_half, both, other)
            filt[pl.ds(base + OWN, OWN), :] = jnp.where(low_half, other, both)
        return carry

    lax.fori_loop(0, SEQ // STEP, net, 0)

    place = lax.broadcasted_iota(jnp.int32, (ROWS, LANES), 0) * ROWS + (
        lax.broadcasted_iota(jnp.int32, (ROWS, LANES), 1) & (ROWS - 1)
    )
    place = place.astype(FLOAT)

    def envelope(ch):
        rate = rates_ref[me * OWN + ch]
        return jnp.exp(place * -rate) * jnp.sqrt(jnp.full((1, LANES), 2.0 * rate + 1.0 / SEQ, FLOAT))

    def strided(ref, base, ch):
        return ref[pl.ds(base + ch, ROWS, stride=OWN), :]

    def group_rows(step):
        return pl.ds(pl.multiple_of(step * GROUP * ROWS, GROUP * ROWS), GROUP * ROWS)

    def cut(value):
        return [value[i * ROWS : (i + 1) * ROWS] for i in range(GROUP)]

    def filters(step, carry):
        chans = [step * GROUP + i for i in range(GROUP)]
        signals = [strided(filt, 0, ch) * envelope(ch) for ch in chans]
        fspec[group_rows(step), :] = forward(signals, first_ref, turn_ref, middle_ref)
        return carry

    lax.fori_loop(0, OWN // GROUP, filters, 0)
    to_peers(sends, got, 1, 2)

    def put(value, base, step):
        for i in range(GROUP):
            backs[pl.ds(base + step * GROUP + i, ROWS, stride=OWN), :] = value[
                :, i * LANES : (i + 1) * LANES
            ]

    peers_done(got, 1).wait_recv()

    def convolve(step, carry):
        signals = [strided(got, 0, step * GROUP + i) for i in range(GROUP)]
        spec = forward(signals, first_ref, turn_ref, middle_ref)
        pspec[group_rows(step), :] = spec
        rows = cut(times(spec, fspec[group_rows(step), :]))
        put(inverse(rows, last_ref, turn_ref, middle_ref), 0, step)
        return carry

    lax.fori_loop(0, OWN // GROUP, convolve, 0)
    to_peers(backs, home, 0, 3)
    peers_done(got, 2).wait_recv()

    def correlate(step, carry):
        signals = [strided(got, AREA, step * GROUP + i) for i in range(GROUP)]
        spec = forward(signals, first_ref, turn_ref, middle_ref)
        rows = cut(times_conj(fspec[group_rows(step), :], spec))
        put(inverse(rows, last_ref, turn_ref, middle_ref), AREA, step)
        pair = times_conj(pspec[group_rows(step), :], spec)
        re, im = pair[:, :LANES], pair[:, LANES:]
        pspec[group_rows(step), :] = columns(
            [re + pltpu.roll(re, ROWS, 1), im + pltpu.roll(im, ROWS, 1)]
        )
        return carry

    lax.fori_loop(0, OWN // GROUP, correlate, 0)
    to_peers(backs, home, 1, 4)

    def filter_back(step, carry):
        rows = cut(pspec[group_rows(step), :])
        value = inverse(rows, last_ref, turn_ref, middle_ref)
        for i in range(GROUP):
            ch = step * GROUP + i
            filt[pl.ds(ch, ROWS, stride=OWN), :] = value[:, i * LANES : (i + 1) * LANES] * envelope(ch)
        return carry

    lax.fori_loop(0, OWN // GROUP, filter_back, 0)
    acc_out[...] = jnp.zeros_like(acc_out)
    acc_net[...] = jnp.zeros_like(acc_net)

    def net_back(step, carry):
        cols = pl.ds(pl.multiple_of(step * STEP, STEP), STEP)
        parts = []
        for pair in range(STEP // LANES):
            base = pl.multiple_of((step * (STEP // ROWS) + 2 * pair) * OWN, OWN)
            parts.append(jnp.where(low_half, filt[pl.ds(base, OWN), :], filt[pl.ds(base + OWN, OWN), :]))
        kgrad = columns(parts)
        acc_out[...] += dot3(kgrad, act2[:, cols], "nt")
        pre2 = dot3(wo_own, kgrad) * cos2[:, cols]
        acc_net[32:, :] += dot3(act1[:, cols], pre2, "nt")
        pre1 = dot3(w2_ref[...], pre2) * cos1[:, cols]
        acc_net[:32, :] += dot3(emb_ref[:, cols], pre1, "nt")
        return carry

    lax.fori_loop(0, SEQ // STEP, net_back, 0)
    out_mine[...] = columns([acc_out[:8, :], acc_out[8:, :]])
    by_chan[chan] = columns([acc_net[:48, :], acc_net[48:, :]])
    swap = remote(out_mine, out_dp, sent.at[5], came.at[5], {"dp": 1 - core})
    swap.start()
    for d in range(1, 4):
        part = by_chan.at[chan]
        remote(part, part, sent.at[6], came.at[6], {"chan": lax.rem(chan + d, 4)}).start()
    swap.wait()
    outs[z, xy] = out_mine[...] + out_dp[...]
    for d in range(1, 4):
        part = outs.at[z, xy]
        remote(part, part, sent.at[7], came.at[7], {"seq": lax.rem(z + d, 4) * 16 + xy}).start()
    chans_done = remote(by_chan.at[pl.ds(0, 3)], by_chan.at[pl.ds(0, 3)], sent.at[6], came.at[6], {"seq": me})
    zs_done = remote(outs.at[pl.ds(0, 3), 0], outs.at[pl.ds(0, 3), 0], sent.at[7], came.at[7], {"seq": me})
    zs_done.wait()

    def around(i):
        return z * 16 + lax.rem(x + i // 4, 4) * 4 + lax.rem(y + lax.rem(i, 4), 4)

    def spread_outs(i, carry):
        column = outs.at[:, xy]
        remote(column, column, sent.at[8], came.at[8], {"seq": around(i)}).start()
        return carry

    lax.fori_loop(1, 16, spread_outs, 0)
    chans_done.wait()
    net_sum = (by_chan[0] + by_chan[1]) + (by_chan[2] + by_chan[3])
    for i in range(6):
        tiles[24 + i] = net_sum[i * 8 : (i + 1) * 8]
    tiles[30] = jnp.zeros((8, LANES), FLOAT)
    tiles[31] = jnp.zeros((8, LANES), FLOAT)

    def scatter():
        phase1[xy] = tiles[pl.ds(2 * xy, 2)]

        def send(i, carry):
            q = around(i)
            part = tiles.at[pl.ds(2 * (q - z * 16), 2)]
            remote(part, phase1.at[xy], sent.at[10], came.at[10], {"seq": q}).start()
            return carry

        lax.fori_loop(1, 16, send, 0)

    def exchange():
        first15 = phase1.at[pl.ds(0, 15)]
        remote(first15, first15, sent.at[10], came.at[10], {"seq": me}).wait()
        sum1[...] = jnp.sum(phase1[...], axis=0)
        mine = phase2.at[z * 2 + core]
        phase2[z * 2 + core] = sum1[...]
        for dz in (2, 1, 3, 0):
            for dc in (0, 1):
                if dz or dc:
                    to = {"seq": lax.rem(z + dz, 4) * 16 + xy, "dp": lax.rem(core + dc, 2)}
                    remote(sum1, mine, sent.at[11], came.at[11], to).start()

    def gather():
        first7 = phase2.at[pl.ds(0, 7)]
        remote(first7, first7, sent.at[11], came.at[11], {"seq": me}).wait()
        sum2[...] = jnp.sum(phase2[...], axis=0)
        phase3[xy] = sum2[...]

        def send(i, carry):
            remote(sum2, phase3.at[xy], sent.at[12], came.at[12], {"seq": around(i)}).start()
            return carry

        lax.fori_loop(1, 16, send, 0)

    def tap_sums(features):
        def body(b, carry):
            cols = lanes(b)
            for i in features:
                sums = []
                for j in range(RIM + 1):
                    both = ahead[i, 0, :ROWS, cols] * ext[i, 0, 8 - j : 8 - j + ROWS, cols]
                    both = both + ahead[i, 1, :ROWS, cols] * ext[i, 1, 8 - j : 8 - j + ROWS, cols]
                    sums.append(jnp.sum(both, axis=0, keepdims=True))
                sums.append(jnp.zeros((1, LANES), FLOAT))
                tiles[i * 8 + b] = jnp.concatenate(sums, axis=0)
            return carry

        lax.fori_loop(0, blocks, body, 0)

    def raws(i):
        def body(b, carry):
            cols = lanes(b)
            for w in range(2):
                total = taps_ref[i, 0:1, cols] * ahead[i, w, :ROWS, cols]
                for j in range(1, RIM + 1):
                    total = total + taps_ref[i, j : j + 1, cols] * ahead[i, w, j : j + ROWS, cols]
                raw_ref[i, w, :, cols] = total
            return carry

        lax.fori_loop(0, blocks, body, 0)
        save = pltpu.make_async_copy(raw_ref.at[i], raw_hbm.at[i], saves.at[1 + i])
        save.start()
        return save

    peers_done(home, 3).wait_recv()

    def mix(b, carry):
        cols = lanes(b)
        conv = home[lanes(b), :].T
        for w in range(2):
            part = conv[w * ROWS : (w + 1) * ROWS]
            mixed_ref[w, :, cols] = feat[0, w, :, cols] * part
            ahead[0, w, :ROWS, cols] = cot_ref[w, :, cols] * part
        return carry

    lax.fori_loop(0, blocks, mix, 0)
    packed(edge_q, ahead, (0,), 0)
    after_q = remote(edge_q, after_q_rows, sent.at[9], came.at[9], {"seq": previous})
    after_q.start()
    save_mixed = pltpu.make_async_copy(mixed_ref, mixed_hbm, saves.at[0])
    save_mixed.start()
    tap_sums((0,))

    outs_part = outs.at[:, pl.ds(0, 15)]
    remote(outs_part, outs_part, sent.at[8], came.at[8], {"seq": me}).wait()
    windows = 4
    tail = 1.0 / math.sqrt(windows * SEQ)
    scale = 4.0 / math.sqrt(windows * SEQ * blocks * LANES * 4)
    for b in range(blocks):
        rows = []
        for s in range(8 * b, 8 * b + 8):
            tile = outs[s // 16, s % 16]
            rows += [tile, pltpu.roll(tile, ROWS, 1)]
        square = jnp.concatenate(rows, axis=0).T
        out_ref[:, b * LANES : (b + 1) * LANES] = square[:ROWS] * tail

    peers_done(home, 4).wait_recv()

    def unmix(b, carry):
        cols = lanes(b)
        back = home[pl.ds(pl.multiple_of(AREA + b * LANES, LANES), LANES), :].T
        for w in range(2):
            part = back[w * ROWS : (w + 1) * ROWS]
            ahead[1, w, :ROWS, cols] = part * feat[2, w, :, cols]
            ahead[2, w, :ROWS, cols] = part * feat[1, w, :, cols]
        return carry

    lax.fori_loop(0, blocks, unmix, 0)
    packed(edge_kv, ahead, keys, 0)
    after_kv = remote(edge_kv, after_kv_rows, sent.at[14], came.at[14], {"seq": previous})
    after_kv.start()
    tap_sums(keys)
    scatter()
    after_q.wait()
    unpacked(after_q_rows, ahead, (0,), ROWS)
    no_rows(ahead, (0,), ROWS, ROWS - 1)
    save_q = raws(0)
    exchange()
    after_kv.wait()
    unpacked(after_kv_rows, ahead, keys, ROWS)
    no_rows(ahead, keys, ROWS, ROWS - 1)
    save_k = raws(1)
    save_v = raws(2)
    gather()
    for sem in (1, 2):
        peers_done(sends, sem).wait_send()
    for sem in (3, 4):
        peers_done(backs, sem).wait_send()
    for save in (save_mixed, save_q, save_k, save_v):
        save.wait()
    last15 = phase3.at[pl.ds(0, 15)]
    remote(last15, last15, sent.at[12], came.at[12], {"seq": me}).wait()
    for i in range(3):
        for b in range(blocks):
            t = i * 8 + b
            short_ref[i, :, b * LANES : (b + 1) * LANES] = phase3[t // 2, t % 2][: RIM + 1] * tail
    net_sum = jnp.concatenate([phase3[t // 2, t % 2] for t in range(24, 30)], axis=0) * scale
    netf_ref[...] = net_sum[:32, :ROWS]
    nets_ref[:16, :] = net_sum[32:, :ROWS]
    nets_ref[16:, :] = net_sum[:, ROWS:]


def shards(projected, short_weight, decay_rates, w1, w2, out_weight, cotangent):
    first_stack, last_stack, turn, middle, embedded = tables()
    vmem = pl.BlockSpec(memory_space=pltpu.VMEM)
    hbm = pl.BlockSpec(memory_space=pl.ANY)
    group = projected.shape[3]
    hidden = w2.shape[0]

    def buffer(*shape):
        return pltpu.VMEM(shape, FLOAT)

    def held(value):
        return buffer(*value.shape)

    def like(value):
        return jax.ShapeDtypeStruct(value.shape, FLOAT)

    rows = projected.shape[2] + 8
    return pl.pallas_call(
        whole_kernel,
        out_shape=(
            like(cotangent),
            like(projected),
            like(short_weight),
            like(out_weight),
            like(w1),
            like(w2),
        ),
        in_specs=[pl.BlockSpec(memory_space=pltpu.SMEM)] + [hbm] * 11,
        out_specs=(hbm, hbm) + (vmem,) * 4,
        scratch_shapes=[
            held(short_weight),
            held(cotangent),
            buffer(w1.shape[0], SEQ),
            held(w1),
            held(w2),
            held(out_weight),
            held(first_stack),
            held(last_stack),
            held(turn),
            held(middle),
            pltpu.VMEM(first_stack.shape, HALF),
            pltpu.VMEM(last_stack.shape, HALF),
            pltpu.VMEM(middle.shape, HALF),
            held(cotangent),
            held(projected),
            buffer(3, 2, rows, group),
            buffer(3, 2, rows, group),
            buffer(3, 2, ROWS, group),
            buffer(2 * AREA, LANES),
            buffer(2 * AREA, LANES),
            buffer(2 * AREA, LANES),
            buffer(2 * AREA, LANES),
            buffer(hidden, SEQ),
            buffer(hidden, SEQ),
            buffer(hidden, SEQ),
            buffer(hidden, SEQ),
            buffer(AREA, LANES),
            buffer(AREA, 2 * LANES),
            buffer(AREA, 2 * LANES),
            buffer(8, LANES),
            buffer(8, LANES),
            buffer(4, 48, LANES),
            buffer(4, 16, 8, LANES),
            buffer(32, 8, LANES),
            buffer(16, 2, 8, LANES),
            buffer(2, 8, LANES),
            buffer(8, 2, 8, LANES),
            buffer(2, 8, LANES),
            buffer(16, 2, 8, LANES),
            buffer(OWN, hidden),
            buffer(96, hidden),
            buffer(24, group),
            buffer(24, group),
            buffer(24, group),
            buffer(24, group),
            buffer(16, group),
            buffer(16, group),
            buffer(16, group),
            pltpu.SemaphoreType.DMA((11,)),
            pltpu.SemaphoreType.DMA((4,)),
            pltpu.SemaphoreType.DMA((18,)),
            pltpu.SemaphoreType.DMA((18,)),
        ],
        compiler_params=pltpu.CompilerParams(
            collective_id=1, has_side_effects=True, vmem_limit_bytes=60 << 20
        ),
        name="whole",
    )(
        decay_rates,
        projected,
        short_weight,
        cotangent,
        jnp.asarray(embedded),
        w1,
        w2,
        out_weight,
        jnp.asarray(first_stack),
        jnp.asarray(last_stack),
        jnp.asarray(turn),
        jnp.asarray(middle),
    )


def solution(mesh):
    return jax.shard_map(
        shards,
        mesh=mesh,
        in_specs=(
            P(None, "dp", "seq", "chan"),
            P(None, None, "chan"),
            P("chan"),
            P(),
            P(),
            P(None, "chan"),
            P("dp", "seq", "chan"),
        ),
        out_specs=(
            P("dp", "seq", "chan"),
            P(None, "dp", "seq", "chan"),
            P(None, None, "chan"),
            P(None, "chan"),
            P(),
            P(),
        ),
        check_vma=False,
    )
```

```python
import functools
import math

import jax
import jax.numpy as jnp
import ml_dtypes
import numpy as np
from jax import lax
from jax.experimental import pallas as pl
from jax.experimental.pallas import tpu as pltpu
from jax.sharding import PartitionSpec as P

MESH = pl.DeviceIdType.MESH
ROWS = 64
OWN = 16
LANES = 128
SEQ = ROWS * ROWS
RIM = 6
STEP = 512
FLOAT = jnp.float32
HALF = jnp.bfloat16


def halves(table):
    high = table.astype(ml_dtypes.bfloat16)
    low = (table - high.astype(np.float64)).astype(ml_dtypes.bfloat16)
    return high, low


@functools.cache
def tables():
    k = np.arange(ROWS)[:, None] + 0.25
    s = np.arange(ROWS)[None, :]
    theta = 2 * np.pi * k * s / ROWS
    first = np.concatenate([np.cos(theta), -np.sin(theta)], axis=0)
    high, low = halves(first)
    first_stack = np.concatenate([high, high, low], axis=1)
    last = np.concatenate([np.cos(theta).T, -np.sin(theta).T], axis=1) / SEQ
    high, low = halves(last)
    last_stack = np.concatenate([high, high, low], axis=1)
    phi = 2 * np.pi * k * s / SEQ
    turn = np.stack([np.tile(np.cos(phi), (1, 2)), np.tile(np.sin(phi), (1, 2))]).astype(np.float32)
    inner = 2 * np.pi * (np.arange(ROWS)[:, None] * s % ROWS) / ROWS
    cos, sin = np.kron(np.eye(2), np.cos(inner)), np.kron(np.eye(2), np.sin(inner))
    there = np.block([[cos, -sin], [sin, cos]])
    back = np.block([[cos, sin], [-sin, cos]])
    middle = np.stack(halves(there) + halves(back))
    half = 16
    orders = np.arange(half, dtype=np.int64)
    factors = 1 + (SEQ // 2 - 2) * orders * orders // max((half - 1) ** 2, 1)
    angle = 2 * np.pi * (factors[:, None] * np.arange(SEQ)[None, :] % SEQ) / SEQ
    embedded = np.concatenate([np.cos(angle), np.sin(angle)], axis=0).astype(np.float32)
    return (*(t.astype(np.float32) for t in (first_stack, last_stack)), turn, middle.astype(np.float32), embedded)


def split(value):
    high = value.astype(HALF)
    return high, (value - high.astype(FLOAT)).astype(HALF)


def dot(a, b, kind="nn"):
    dims = {"nn": ((1,), (0,)), "nt": ((1,), (1,))}[kind]
    return lax.dot_general(a, b, (dims, ((), ())), preferred_element_type=FLOAT)


def dot3(a, b, kind="nn"):
    ah, al = split(a)
    bh, bl = split(b)
    return dot(ah, bh, kind) + (dot(ah, bl, kind) + dot(al, bh, kind))


def sin_cos(x):
    n = jnp.floor(x * (2.0 / math.pi) + 0.5)
    r = x - n * 1.5703125
    r = r - n * 4.837512969970703125e-4
    r = r - n * 7.549789948768648e-8
    z = r * r
    s = r + r * z * (-1.6666654611e-1 + z * (8.3321608736e-3 + z * -1.9515295891e-4))
    c = 1.0 - 0.5 * z + z * z * (4.166664568298827e-2 + z * (-1.388731625493765e-3 + z * 2.443315711809948e-5))
    q = n.astype(jnp.int32)
    odd = (q & 1) == 1
    sin = jnp.where(odd, c, s)
    cos = jnp.where(odd, s, c)
    sin = jnp.where((q & 2) == 2, -sin, sin)
    cos = jnp.where(((q + 1) & 2) == 2, -cos, cos)
    return sin, cos


def columns(parts):
    return jnp.concatenate(parts, axis=1)


def forward(signals, first, turn, middle):
    cos, sin = turn[0], turn[1]
    high, low = split(columns(signals))
    spec = dot(first[...], jnp.concatenate([high, low, high], axis=0))
    rows = []
    for i in range(len(signals)):
        re = spec[:ROWS, i * LANES : (i + 1) * LANES]
        im = spec[ROWS:, i * LANES : (i + 1) * LANES]
        rows.append(columns([re * cos + im * sin, im * cos - re * sin]))
    high, low = split(jnp.concatenate(rows, axis=0))
    return dot(high, middle[0]) + (dot(low, middle[0]) + dot(high, middle[1]))


def inverse(rows, last, turn, middle):
    cos, sin = turn[0], turn[1]
    high, low = split(jnp.concatenate(rows, axis=0))
    freq = dot(high, middle[2]) + (dot(low, middle[2]) + dot(high, middle[3]))
    cols = []
    for i in range(len(rows)):
        re = freq[i * ROWS : (i + 1) * ROWS, :LANES]
        im = freq[i * ROWS : (i + 1) * ROWS, LANES:]
        cols.append(jnp.concatenate([re * cos - im * sin, re * sin + im * cos], axis=0))
    high, low = split(columns(cols))
    return dot(last[...], jnp.concatenate([high, low, high], axis=0))


def times(a, b):
    ar, ai, br, bi = a[:, :LANES], a[:, LANES:], b[:, :LANES], b[:, LANES:]
    return columns([ar * br - ai * bi, ar * bi + ai * br])


def times_conj(a, b):
    ar, ai, br, bi = a[:, :LANES], a[:, LANES:], b[:, :LANES], b[:, LANES:]
    return columns([ar * br + ai * bi, ar * bi - ai * br])


def flipped(small):
    rows, cols = small.shape
    tall = jnp.concatenate([small, jnp.zeros((LANES - rows, cols), FLOAT)], axis=0)
    square = columns([tall, jnp.zeros((LANES, LANES - cols), FLOAT)]) if cols < LANES else tall
    return square.T


def remote(src, dst, send_sem, recv_sem, device):
    return pltpu.make_async_remote_copy(
        src_ref=src,
        dst_ref=dst,
        send_sem=send_sem,
        recv_sem=recv_sem,
        device_id=device,
        device_id_type=MESH,
    )


GROUP = 4
AREA = ROWS * OWN


def whole_kernel(
    rates_ref,
    proj_hbm,
    taps_hbm,
    cot_hbm,
    emb_hbm,
    w1_hbm,
    w2_hbm,
    wo_hbm,
    first_hbm,
    last_hbm,
    turn_hbm,
    middle_hbm,
    mixed_hbm,
    raw_hbm,
    short_ref,
    out_ref,
    netf_ref,
    nets_ref,
    taps_ref,
    cot_ref,
    emb_ref,
    w1_ref,
    w2_ref,
    wo_ref,
    first_wide,
    last_wide,
    turn_ref,
    middle_wide,
    first_ref,
    last_ref,
    middle_ref,
    mixed_ref,
    raw_ref,
    ext,
    ahead,
    feat,
    sends,
    got,
    backs,
    home,
    act1,
    cos1,
    act2,
    cos2,
    filt,
    fspec,
    gspec,
    out_mine,
    out_dp,
    by_chan,
    outs,
    tiles,
    phase1,
    sum1,
    phase2,
    sum2,
    phase3,
    acc_out,
    acc_net,
    edge_kv,
    rim_kv,
    after_kv_rows,
    edge_q,
    rim_q,
    after_q_rows,
    loads,
    saves,
    sent,
    came,
):
    me = lax.axis_index("seq")
    chan = lax.axis_index("chan")
    core = lax.axis_index("dp")
    z, xy = me // 16, lax.rem(me, 16)
    x, y = xy // 4, lax.rem(xy, 4)
    following, previous = lax.rem(me + 1, ROWS), lax.rem(me + ROWS - 1, ROWS)
    blocks = feat.shape[3] // LANES
    barrier = pltpu.get_barrier_semaphore()

    def signal(sem, **device):
        pl.semaphore_signal(sem, inc=1, device_id=device, device_id_type=MESH)

    for dz in (2, 1, 3, 0):
        plane = lax.rem(z + dz, 4) * 16

        def greet(i, carry):
            signal(barrier, seq=plane + lax.rem(xy + i, 16))
            return carry

        lax.fori_loop(0 if dz else 1, 16, greet, 0)
        signal(barrier, seq=plane + xy, dp=1 - core)
    for d in range(1, 4):
        signal(barrier, chan=lax.rem(chan + d, 4))

    pairs = [
        (proj_hbm, ext.at[:, :, pl.ds(8, ROWS), :]),
        (taps_hbm, taps_ref),
        (cot_hbm, cot_ref),
        (emb_hbm, emb_ref),
        (w1_hbm, w1_ref),
        (w2_hbm, w2_ref),
        (wo_hbm, wo_ref),
        (first_hbm, first_wide),
        (last_hbm, last_wide),
        (turn_hbm, turn_ref),
        (middle_hbm, middle_wide),
    ]
    copies = [pltpu.make_async_copy(src, dst, loads.at[i]) for i, (src, dst) in enumerate(pairs)]
    for copy in copies:
        copy.start()
    copies[0].wait()
    copies[1].wait()

    def lanes(b):
        return pl.ds(pl.multiple_of(b * LANES, LANES), LANES)

    def tapped(i, w, cols, start, count):
        total = taps_ref[i, 0:1, cols] * ext[i, w, 8 + start : 8 + start + count, cols]
        for j in range(1, RIM + 1):
            rows = slice(8 + start - j, 8 + start - j + count)
            total = total + taps_ref[i, j : j + 1, cols] * ext[i, w, rows, cols]
        feat[i, w, start : start + count, cols] = total

    def later_rows(group):
        def body(b, carry):
            for i in group:
                for w in range(2):
                    tapped(i, w, lanes(b), 8, ROWS - 8)
            return carry

        lax.fori_loop(0, blocks, body, 0)

    def to_peers(source, target, signal_at, sem):
        base = signal_at * AREA
        mine = pl.ds(pl.multiple_of(base + me * OWN, OWN), OWN)
        target[mine, :] = source[mine, :]

        def send(i, carry):
            px, py = lax.rem(x + lax.rem(i // 4, 4), 4), lax.rem(y + i // 16, 4)
            peer = lax.rem(z + lax.rem(i, 4), 4) * 16 + px * 4 + py
            block = pl.ds(pl.multiple_of(base + peer * OWN, OWN), OWN)
            remote(source.at[block], target.at[mine], sent.at[sem], came.at[sem], {"seq": peer}).start()
            return carry

        lax.fori_loop(1, ROWS, send, 0)

    def peers_done(ref, sem):
        part = ref.at[pl.ds(0, AREA - OWN)]
        return remote(part, part, sent.at[sem], came.at[sem], {"seq": me})

    def pack(buffer, features, row):
        for n, (i, w) in enumerate((i, w) for i in features for w in range(2)):
            yield n * RIM, buffer.at[i, w, pl.ds(row, RIM), :]

    def packed(target, buffer, features, row):
        for at, part in pack(buffer, features, row):
            target[at : at + RIM, :] = part[...]

    def unpacked(source, buffer, features, row):
        for at, part in pack(buffer, features, row):
            part[...] = source[at : at + RIM, :]

    def no_rows(buffer, features, row, where):
        @pl.when(me == where)
        def _():
            for i in features:
                buffer[i, :, row : row + 8, :] = jnp.zeros((2, 8, buffer.shape[3]), FLOAT)

    keys = (1, 2)
    edge_q[8:, :] = jnp.zeros((8, edge_q.shape[1]), FLOAT)
    packed(edge_kv, ext, keys, ROWS + 8 - RIM)
    packed(edge_q, ext, (0,), ROWS + 8 - RIM)
    later_rows(keys)
    later_rows((0,))
    pl.semaphore_wait(barrier, ROWS - 1 + 7)

    to_q = remote(edge_q, rim_q, sent.at[13], came.at[13], {"seq": following})
    to_kv = remote(edge_kv, rim_kv, sent.at[0], came.at[0], {"seq": following})
    to_q.start()
    to_q.wait()
    to_kv.start()
    unpacked(rim_q, ext, (0,), 8 - RIM)
    no_rows(ext, (0,), 0, 0)

    copies[2].wait()

    def gradients(b, carry):
        cols = lanes(b)
        for w in range(2):
            tapped(0, w, cols, 0, 8)
        parts = [feat[0, w, :, cols] * cot_ref[w, :, cols] for w in range(2)]
        rows = pl.ds(pl.multiple_of(AREA + b * LANES, LANES), LANES)
        sends[rows, :] = jnp.concatenate(parts, axis=0).T
        return carry

    lax.fori_loop(0, blocks, gradients, 0)
    to_peers(sends, got, 1, 2)
    for copy in copies[3:]:
        copy.wait()
    first_ref[...] = first_wide[...].astype(HALF)
    last_ref[...] = last_wide[...].astype(HALF)
    middle_ref[...] = middle_wide[...].astype(HALF)

    turned = pltpu.roll(
        wo_ref[:, lanes(me // 8)], lax.rem(LANES - lax.rem(me, 8) * OWN, LANES), 1
    )
    wo_own = turned[:, :OWN]
    wo_t = flipped(turned)[:OWN, :ROWS]
    w1_t = flipped(w1_ref[...])[:ROWS, : w1_ref.shape[0]]
    w2_t = flipped(w2_ref[...])[:ROWS, :ROWS]
    lane = lax.broadcasted_iota(jnp.int32, (OWN, LANES), 1)
    low_half = lane < ROWS

    def net(step, carry):
        cols = pl.ds(pl.multiple_of(step * STEP, STEP), STEP)
        s1, c1 = sin_cos(dot3(w1_t, emb_ref[:, cols]))
        act1[:, cols] = s1
        cos1[:, cols] = c1
        s2, c2 = sin_cos(dot3(w2_t, s1))
        act2[:, cols] = s2
        cos2[:, cols] = c2
        raw = dot3(wo_t, s2)
        for pair in range(STEP // LANES):
            both = raw[:, pair * LANES : (pair + 1) * LANES]
            other = pltpu.roll(both, ROWS, 1)
            base = pl.multiple_of((step * (STEP // ROWS) + 2 * pair) * OWN, OWN)
            filt[pl.ds(base, OWN), :] = jnp.where(low_half, both, other)
            filt[pl.ds(base + OWN, OWN), :] = jnp.where(low_half, other, both)
        return carry

    lax.fori_loop(0, SEQ // STEP, net, 0)

    place = lax.broadcasted_iota(jnp.int32, (ROWS, LANES), 0) * ROWS + (
        lax.broadcasted_iota(jnp.int32, (ROWS, LANES), 1) & (ROWS - 1)
    )
    place = place.astype(FLOAT)

    def envelope(ch):
        rate = rates_ref[me * OWN + ch]
        return jnp.exp(place * -rate) * jnp.sqrt(jnp.full((1, LANES), 2.0 * rate + 1.0 / SEQ, FLOAT))

    def strided(ref, base, ch):
        return ref[pl.ds(base + ch, ROWS, stride=OWN), :]

    def group_rows(step):
        return pl.ds(pl.multiple_of(step * GROUP * ROWS, GROUP * ROWS), GROUP * ROWS)

    def cut(value):
        return [value[i * ROWS : (i + 1) * ROWS] for i in range(GROUP)]

    def filters(step, carry):
        chans = [step * GROUP + i for i in range(GROUP)]
        signals = [strided(filt, 0, ch) * envelope(ch) for ch in chans]
        fspec[group_rows(step), :] = forward(signals, first_ref, turn_ref, middle_ref)
        return carry

    lax.fori_loop(0, OWN // GROUP, filters, 0)
    to_kv.wait()
    unpacked(rim_kv, ext, keys, 8 - RIM)
    no_rows(ext, keys, 0, 0)

    def products(b, carry):
        cols = lanes(b)
        for i in (1, 2):
            for w in range(2):
                tapped(i, w, cols, 0, 8)
        parts = [feat[1, w, :, cols] * feat[2, w, :, cols] for w in range(2)]
        sends[lanes(b), :] = jnp.concatenate(parts, axis=0).T
        return carry

    lax.fori_loop(0, blocks, products, 0)
    to_peers(sends, got, 0, 1)

    def put(value, base, step):
        for i in range(GROUP):
            backs[pl.ds(base + step * GROUP + i, ROWS, stride=OWN), :] = value[
                :, i * LANES : (i + 1) * LANES
            ]

    peers_done(got, 2).wait_recv()

    def correlate(step, carry):
        signals = [strided(got, AREA, step * GROUP + i) for i in range(GROUP)]
        spec = forward(signals, first_ref, turn_ref, middle_ref)
        gspec[group_rows(step), :] = spec
        rows = cut(times_conj(fspec[group_rows(step), :], spec))
        put(inverse(rows, last_ref, turn_ref, middle_ref), AREA, step)
        return carry

    lax.fori_loop(0, OWN // GROUP, correlate, 0)
    to_peers(backs, home, 1, 4)
    peers_done(got, 1).wait_recv()

    def convolve(step, carry):
        signals = [strided(got, 0, step * GROUP + i) for i in range(GROUP)]
        spec = forward(signals, first_ref, turn_ref, middle_ref)
        rows = cut(times(spec, fspec[group_rows(step), :]))
        put(inverse(rows, last_ref, turn_ref, middle_ref), 0, step)
        pair = times_conj(spec, gspec[group_rows(step), :])
        re, im = pair[:, :LANES], pair[:, LANES:]
        gspec[group_rows(step), :] = columns(
            [re + pltpu.roll(re, ROWS, 1), im + pltpu.roll(im, ROWS, 1)]
        )
        return carry

    lax.fori_loop(0, OWN // GROUP, convolve, 0)
    to_peers(backs, home, 0, 3)

    def filter_back(step, carry):
        rows = cut(gspec[group_rows(step), :])
        value = inverse(rows, last_ref, turn_ref, middle_ref)
        for i in range(GROUP):
            ch = step * GROUP + i
            filt[pl.ds(ch, ROWS, stride=OWN), :] = value[:, i * LANES : (i + 1) * LANES] * envelope(ch)
        return carry

    lax.fori_loop(0, OWN // GROUP, filter_back, 0)
    acc_out[...] = jnp.zeros_like(acc_out)
    acc_net[...] = jnp.zeros_like(acc_net)

    def net_back(step, carry):
        cols = pl.ds(pl.multiple_of(step * STEP, STEP), STEP)
        parts = []
        for pair in range(STEP // LANES):
            base = pl.multiple_of((step * (STEP // ROWS) + 2 * pair) * OWN, OWN)
            parts.append(jnp.where(low_half, filt[pl.ds(base, OWN), :], filt[pl.ds(base + OWN, OWN), :]))
        kgrad = columns(parts)
        acc_out[...] += dot3(kgrad, act2[:, cols], "nt")
        pre2 = dot3(wo_own, kgrad) * cos2[:, cols]
        acc_net[32:, :] += dot3(act1[:, cols], pre2, "nt")
        pre1 = dot3(w2_ref[...], pre2) * cos1[:, cols]
        acc_net[:32, :] += dot3(emb_ref[:, cols], pre1, "nt")
        return carry

    lax.fori_loop(0, SEQ // STEP, net_back, 0)
    out_mine[...] = columns([acc_out[:8, :], acc_out[8:, :]])
    by_chan[chan] = columns([acc_net[:48, :], acc_net[48:, :]])
    swap = remote(out_mine, out_dp, sent.at[5], came.at[5], {"dp": 1 - core})
    swap.start()
    for d in range(1, 4):
        part = by_chan.at[chan]
        remote(part, part, sent.at[6], came.at[6], {"chan": lax.rem(chan + d, 4)}).start()
    swap.wait()
    outs[z, xy] = out_mine[...] + out_dp[...]
    for d in range(1, 4):
        part = outs.at[z, xy]
        remote(part, part, sent.at[7], came.at[7], {"seq": lax.rem(z + d, 4) * 16 + xy}).start()
    chans_done = remote(by_chan.at[pl.ds(0, 3)], by_chan.at[pl.ds(0, 3)], sent.at[6], came.at[6], {"seq": me})
    zs_done = remote(outs.at[pl.ds(0, 3), 0], outs.at[pl.ds(0, 3), 0], sent.at[7], came.at[7], {"seq": me})
    zs_done.wait()

    def around(i):
        return z * 16 + lax.rem(x + i // 4, 4) * 4 + lax.rem(y + lax.rem(i, 4), 4)

    def spread_outs(i, carry):
        column = outs.at[:, xy]
        remote(column, column, sent.at[8], came.at[8], {"seq": around(i)}).start()
        return carry

    lax.fori_loop(1, 16, spread_outs, 0)
    chans_done.wait()
    net_sum = (by_chan[0] + by_chan[1]) + (by_chan[2] + by_chan[3])
    for i in range(6):
        tiles[24 + i] = net_sum[i * 8 : (i + 1) * 8]
    tiles[30] = jnp.zeros((8, LANES), FLOAT)
    tiles[31] = jnp.zeros((8, LANES), FLOAT)

    def scatter():
        phase1[xy] = tiles[pl.ds(2 * xy, 2)]

        def send(i, carry):
            q = around(i)
            part = tiles.at[pl.ds(2 * (q - z * 16), 2)]
            remote(part, phase1.at[xy], sent.at[10], came.at[10], {"seq": q}).start()
            return carry

        lax.fori_loop(1, 16, send, 0)

    def exchange():
        first15 = phase1.at[pl.ds(0, 15)]
        remote(first15, first15, sent.at[10], came.at[10], {"seq": me}).wait()
        sum1[...] = jnp.sum(phase1[...], axis=0)
        mine = phase2.at[z * 2 + core]
        phase2[z * 2 + core] = sum1[...]
        for dz in (2, 1, 3, 0):
            for dc in (0, 1):
                if dz or dc:
                    to = {"seq": lax.rem(z + dz, 4) * 16 + xy, "dp": lax.rem(core + dc, 2)}
                    remote(sum1, mine, sent.at[11], came.at[11], to).start()

    def gather():
        first7 = phase2.at[pl.ds(0, 7)]
        remote(first7, first7, sent.at[11], came.at[11], {"seq": me}).wait()
        sum2[...] = jnp.sum(phase2[...], axis=0)
        phase3[xy] = sum2[...]

        def send(i, carry):
            remote(sum2, phase3.at[xy], sent.at[12], came.at[12], {"seq": around(i)}).start()
            return carry

        lax.fori_loop(1, 16, send, 0)

    def tap_sums(features):
        def body(b, carry):
            cols = lanes(b)
            for i in features:
                sums = []
                for j in range(RIM + 1):
                    both = ahead[i, 0, :ROWS, cols] * ext[i, 0, 8 - j : 8 - j + ROWS, cols]
                    both = both + ahead[i, 1, :ROWS, cols] * ext[i, 1, 8 - j : 8 - j + ROWS, cols]
                    sums.append(jnp.sum(both, axis=0, keepdims=True))
                sums.append(jnp.zeros((1, LANES), FLOAT))
                tiles[i * 8 + b] = jnp.concatenate(sums, axis=0)
            return carry

        lax.fori_loop(0, blocks, body, 0)

    def raws(i):
        def body(b, carry):
            cols = lanes(b)
            for w in range(2):
                total = taps_ref[i, 0:1, cols] * ahead[i, w, :ROWS, cols]
                for j in range(1, RIM + 1):
                    total = total + taps_ref[i, j : j + 1, cols] * ahead[i, w, j : j + ROWS, cols]
                raw_ref[i, w, :, cols] = total
            return carry

        lax.fori_loop(0, blocks, body, 0)
        save = pltpu.make_async_copy(raw_ref.at[i], raw_hbm.at[i], saves.at[1 + i])
        save.start()
        return save

    outs_part = outs.at[:, pl.ds(0, 15)]
    remote(outs_part, outs_part, sent.at[8], came.at[8], {"seq": me}).wait()
    windows = 4
    tail = 1.0 / math.sqrt(windows * SEQ)
    scale = 4.0 / math.sqrt(windows * SEQ * blocks * LANES * 4)
    for b in range(blocks):
        rows = []
        for s in range(8 * b, 8 * b + 8):
            tile = outs[s // 16, s % 16]
            rows += [tile, pltpu.roll(tile, ROWS, 1)]
        square = jnp.concatenate(rows, axis=0).T
        out_ref[:, b * LANES : (b + 1) * LANES] = square[:ROWS] * tail

    peers_done(home, 4).wait_recv()

    def unmix(b, carry):
        cols = lanes(b)
        back = home[pl.ds(pl.multiple_of(AREA + b * LANES, LANES), LANES), :].T
        for w in range(2):
            part = back[w * ROWS : (w + 1) * ROWS]
            ahead[1, w, :ROWS, cols] = part * feat[2, w, :, cols]
            ahead[2, w, :ROWS, cols] = part * feat[1, w, :, cols]
        return carry

    lax.fori_loop(0, blocks, unmix, 0)
    packed(edge_kv, ahead, keys, 0)
    after_kv = remote(edge_kv, after_kv_rows, sent.at[14], came.at[14], {"seq": previous})
    after_kv.start()
    tap_sums(keys)
    peers_done(home, 3).wait_recv()

    def mix(b, carry):
        cols = lanes(b)
        conv = home[lanes(b), :].T
        for w in range(2):
            part = conv[w * ROWS : (w + 1) * ROWS]
            mixed_ref[w, :, cols] = feat[0, w, :, cols] * part
            ahead[0, w, :ROWS, cols] = cot_ref[w, :, cols] * part
        return carry

    lax.fori_loop(0, blocks, mix, 0)
    packed(edge_q, ahead, (0,), 0)
    after_q = remote(edge_q, after_q_rows, sent.at[9], came.at[9], {"seq": previous})
    after_q.start()
    save_mixed = pltpu.make_async_copy(mixed_ref, mixed_hbm, saves.at[0])
    save_mixed.start()
    tap_sums((0,))
    scatter()
    after_kv.wait()
    unpacked(after_kv_rows, ahead, keys, ROWS)
    no_rows(ahead, keys, ROWS, ROWS - 1)
    save_k = raws(1)
    save_v = raws(2)
    exchange()
    after_q.wait()
    unpacked(after_q_rows, ahead, (0,), ROWS)
    no_rows(ahead, (0,), ROWS, ROWS - 1)
    save_q = raws(0)
    gather()
    for sem in (1, 2):
        peers_done(sends, sem).wait_send()
    for sem in (3, 4):
        peers_done(backs, sem).wait_send()
    for save in (save_mixed, save_q, save_k, save_v):
        save.wait()
    last15 = phase3.at[pl.ds(0, 15)]
    remote(last15, last15, sent.at[12], came.at[12], {"seq": me}).wait()
    for i in range(3):
        for b in range(blocks):
            t = i * 8 + b
            short_ref[i, :, b * LANES : (b + 1) * LANES] = phase3[t // 2, t % 2][: RIM + 1] * tail
    net_sum = jnp.concatenate([phase3[t // 2, t % 2] for t in range(24, 30)], axis=0) * scale
    netf_ref[...] = net_sum[:32, :ROWS]
    nets_ref[:16, :] = net_sum[32:, :ROWS]
    nets_ref[16:, :] = net_sum[:, ROWS:]


def land_kernel(*refs):
    count = (len(refs) - 1) // 2
    sems = refs[-1]
    pairs = []
    for source, target in zip(refs[:count], refs[count : 2 * count]):
        if len(source.shape) == 4:
            pairs += [(source.at[i, w], target.at[i, w]) for i in range(3) for w in range(2)]
        elif source.shape[0] == 2:
            pairs += [(source.at[w], target.at[w]) for w in range(2)]
        else:
            pairs.append((source, target))
    copies = [pltpu.make_async_copy(*pair, sems.at[n]) for n, pair in enumerate(pairs)]
    for copy in copies:
        copy.start()
    for copy in copies:
        copy.wait()


def shards(projected, short_weight, decay_rates, w1, w2, out_weight, cotangent):
    first_stack, last_stack, turn, middle, embedded = tables()
    vmem = pl.BlockSpec(memory_space=pltpu.VMEM)
    hbm = pl.BlockSpec(memory_space=pl.ANY)
    group = projected.shape[3]
    hidden = w2.shape[0]

    def buffer(*shape):
        return pltpu.VMEM(shape, FLOAT)

    def held(value):
        return buffer(*value.shape)

    def like(value):
        return jax.ShapeDtypeStruct(value.shape, FLOAT)

    rows = projected.shape[2] + 8
    results = pl.pallas_call(
        whole_kernel,
        out_shape=(
            like(cotangent),
            like(projected),
            like(short_weight),
            like(out_weight),
            like(w1),
            like(w2),
        ),
        in_specs=[pl.BlockSpec(memory_space=pltpu.SMEM)] + [hbm] * 11,
        out_specs=(hbm, hbm) + (vmem,) * 4,
        scratch_shapes=[
            held(short_weight),
            held(cotangent),
            buffer(w1.shape[0], SEQ),
            held(w1),
            held(w2),
            held(out_weight),
            held(first_stack),
            held(last_stack),
            held(turn),
            held(middle),
            pltpu.VMEM(first_stack.shape, HALF),
            pltpu.VMEM(last_stack.shape, HALF),
            pltpu.VMEM(middle.shape, HALF),
            held(cotangent),
            held(projected),
            buffer(3, 2, rows, group),
            buffer(3, 2, rows, group),
            buffer(3, 2, ROWS, group),
            buffer(2 * AREA, LANES),
            buffer(2 * AREA, LANES),
            buffer(2 * AREA, LANES),
            buffer(2 * AREA, LANES),
            buffer(hidden, SEQ),
            buffer(hidden, SEQ),
            buffer(hidden, SEQ),
            buffer(hidden, SEQ),
            buffer(AREA, LANES),
            buffer(AREA, 2 * LANES),
            buffer(AREA, 2 * LANES),
            buffer(8, LANES),
            buffer(8, LANES),
            buffer(4, 48, LANES),
            buffer(4, 16, 8, LANES),
            buffer(32, 8, LANES),
            buffer(16, 2, 8, LANES),
            buffer(2, 8, LANES),
            buffer(8, 2, 8, LANES),
            buffer(2, 8, LANES),
            buffer(16, 2, 8, LANES),
            buffer(OWN, hidden),
            buffer(96, hidden),
            buffer(24, group),
            buffer(24, group),
            buffer(24, group),
            buffer(16, group),
            buffer(16, group),
            buffer(16, group),
            pltpu.SemaphoreType.DMA((11,)),
            pltpu.SemaphoreType.DMA((4,)),
            pltpu.SemaphoreType.DMA((18,)),
            pltpu.SemaphoreType.DMA((18,)),
        ],
        compiler_params=pltpu.CompilerParams(
            collective_id=1, has_side_effects=True, vmem_limit_bytes=60 << 20
        ),
        name="whole",
    )(
        decay_rates,
        projected,
        short_weight,
        cotangent,
        jnp.asarray(embedded),
        w1,
        w2,
        out_weight,
        jnp.asarray(first_stack),
        jnp.asarray(last_stack),
        jnp.asarray(turn),
        jnp.asarray(middle),
    )
    return pl.pallas_call(
        land_kernel,
        out_shape=tuple(like(v) for v in results),
        in_specs=[hbm] * len(results),
        out_specs=(hbm,) * len(results),
        scratch_shapes=[pltpu.SemaphoreType.DMA((12,))],
        compiler_params=pltpu.CompilerParams(vmem_limit_bytes=60 << 20),
        name="land",
    )(*results)


def solution(mesh):
    return jax.shard_map(
        shards,
        mesh=mesh,
        in_specs=(
            P(None, "dp", "seq", "chan"),
            P(None, None, "chan"),
            P("chan"),
            P(),
            P(),
            P(None, "chan"),
            P("dp", "seq", "chan"),
        ),
        out_specs=(
            P("dp", "seq", "chan"),
            P(None, "dp", "seq", "chan"),
            P(None, None, "chan"),
            P(None, "chan"),
            P(),
            P(),
        ),
        check_vma=False,
    )
```

```python
import functools
import math

import jax
import jax.numpy as jnp
import ml_dtypes
import numpy as np
from jax import lax
from jax.experimental import pallas as pl
from jax.experimental.pallas import tpu as pltpu
from jax.sharding import PartitionSpec as P

MESH = pl.DeviceIdType.MESH
ROWS = 64
OWN = 16
LANES = 128
SEQ = ROWS * ROWS
RIM = 6
STEP = 512
FLOAT = jnp.float32
HALF = jnp.bfloat16


def halves(table):
    high = table.astype(ml_dtypes.bfloat16)
    low = (table - high.astype(np.float64)).astype(ml_dtypes.bfloat16)
    return high, low


@functools.cache
def tables():
    k = np.arange(ROWS)[:, None] + 0.25
    s = np.arange(ROWS)[None, :]
    theta = 2 * np.pi * k * s / ROWS
    first = np.concatenate([np.cos(theta), -np.sin(theta)], axis=0)
    high, low = halves(first)
    first_stack = np.concatenate([high, high, low], axis=1)
    last = np.concatenate([np.cos(theta).T, -np.sin(theta).T], axis=1) / SEQ
    high, low = halves(last)
    last_stack = np.concatenate([high, high, low], axis=1)
    phi = 2 * np.pi * k * s / SEQ
    turn = np.stack([np.tile(np.cos(phi), (1, 2)), np.tile(np.sin(phi), (1, 2))]).astype(np.float32)
    inner = 2 * np.pi * (np.arange(ROWS)[:, None] * s % ROWS) / ROWS
    cos, sin = np.kron(np.eye(2), np.cos(inner)), np.kron(np.eye(2), np.sin(inner))
    there = np.block([[cos, -sin], [sin, cos]])
    back = np.block([[cos, sin], [-sin, cos]])
    middle = np.stack(halves(there) + halves(back))
    half = 16
    orders = np.arange(half, dtype=np.int64)
    factors = 1 + (SEQ // 2 - 2) * orders * orders // max((half - 1) ** 2, 1)
    angle = 2 * np.pi * (factors[:, None] * np.arange(SEQ)[None, :] % SEQ) / SEQ
    embedded = np.concatenate([np.cos(angle), np.sin(angle)], axis=0).astype(np.float32)
    return (*(t.astype(np.float32) for t in (first_stack, last_stack)), turn, middle.astype(np.float32), embedded)


def split(value):
    high = value.astype(HALF)
    return high, (value - high.astype(FLOAT)).astype(HALF)


def dot(a, b, kind="nn"):
    dims = {"nn": ((1,), (0,)), "nt": ((1,), (1,))}[kind]
    return lax.dot_general(a, b, (dims, ((), ())), preferred_element_type=FLOAT)


def dot3(a, b, kind="nn"):
    ah, al = split(a)
    bh, bl = split(b)
    return dot(ah, bh, kind) + (dot(ah, bl, kind) + dot(al, bh, kind))


def sin_cos(x):
    n = jnp.floor(x * (2.0 / math.pi) + 0.5)
    r = x - n * 1.5703125
    r = r - n * 4.837512969970703125e-4
    r = r - n * 7.549789948768648e-8
    z = r * r
    s = r + r * z * (-1.6666654611e-1 + z * (8.3321608736e-3 + z * -1.9515295891e-4))
    c = 1.0 - 0.5 * z + z * z * (4.166664568298827e-2 + z * (-1.388731625493765e-3 + z * 2.443315711809948e-5))
    q = n.astype(jnp.int32)
    odd = (q & 1) == 1
    sin = jnp.where(odd, c, s)
    cos = jnp.where(odd, s, c)
    sin = jnp.where((q & 2) == 2, -sin, sin)
    cos = jnp.where(((q + 1) & 2) == 2, -cos, cos)
    return sin, cos


def columns(parts):
    return jnp.concatenate(parts, axis=1)


def forward(signals, first, turn, middle):
    cos, sin = turn[0], turn[1]
    high, low = split(columns(signals))
    spec = dot(first[...], jnp.concatenate([high, low, high], axis=0))
    rows = []
    for i in range(len(signals)):
        re = spec[:ROWS, i * LANES : (i + 1) * LANES]
        im = spec[ROWS:, i * LANES : (i + 1) * LANES]
        rows.append(columns([re * cos + im * sin, im * cos - re * sin]))
    high, low = split(jnp.concatenate(rows, axis=0))
    return dot(high, middle[0]) + (dot(low, middle[0]) + dot(high, middle[1]))


def inverse(rows, last, turn, middle):
    cos, sin = turn[0], turn[1]
    high, low = split(jnp.concatenate(rows, axis=0))
    freq = dot(high, middle[2]) + (dot(low, middle[2]) + dot(high, middle[3]))
    cols = []
    for i in range(len(rows)):
        re = freq[i * ROWS : (i + 1) * ROWS, :LANES]
        im = freq[i * ROWS : (i + 1) * ROWS, LANES:]
        cols.append(jnp.concatenate([re * cos - im * sin, re * sin + im * cos], axis=0))
    high, low = split(columns(cols))
    return dot(last[...], jnp.concatenate([high, low, high], axis=0))


def times(a, b):
    ar, ai, br, bi = a[:, :LANES], a[:, LANES:], b[:, :LANES], b[:, LANES:]
    return columns([ar * br - ai * bi, ar * bi + ai * br])


def times_conj(a, b):
    ar, ai, br, bi = a[:, :LANES], a[:, LANES:], b[:, :LANES], b[:, LANES:]
    return columns([ar * br + ai * bi, ar * bi - ai * br])


def flipped(small):
    rows, cols = small.shape
    tall = jnp.concatenate([small, jnp.zeros((LANES - rows, cols), FLOAT)], axis=0)
    square = columns([tall, jnp.zeros((LANES, LANES - cols), FLOAT)]) if cols < LANES else tall
    return square.T


def remote(src, dst, send_sem, recv_sem, device):
    return pltpu.make_async_remote_copy(
        src_ref=src,
        dst_ref=dst,
        send_sem=send_sem,
        recv_sem=recv_sem,
        device_id=device,
        device_id_type=MESH,
    )


GROUP = 4
AREA = ROWS * OWN


def whole_kernel(
    rates_ref,
    proj_hbm,
    taps_hbm,
    cot_hbm,
    emb_hbm,
    w1_hbm,
    w2_hbm,
    wo_hbm,
    first_hbm,
    last_hbm,
    turn_hbm,
    middle_hbm,
    mixed_hbm,
    raw_hbm,
    short_ref,
    out_ref,
    netf_ref,
    nets_ref,
    taps_ref,
    cot_ref,
    emb_ref,
    w1_ref,
    w2_ref,
    wo_ref,
    first_wide,
    last_wide,
    turn_ref,
    middle_wide,
    first_ref,
    last_ref,
    middle_ref,
    mixed_ref,
    raw_ref,
    ext,
    ahead,
    feat,
    sends,
    got,
    backs,
    home,
    act1,
    cos1,
    act2,
    cos2,
    filt,
    fspec,
    pspec,
    gspec,
    out_mine,
    out_dp,
    by_chan,
    outs,
    tiles,
    phase1,
    sum1,
    phase2,
    sum2,
    phase3,
    acc_out,
    acc_net,
    edge_kv,
    rim_kv,
    relay,
    after_kv_rows,
    edge_q,
    rim_q,
    after_q_rows,
    loads,
    saves,
    sent,
    came,
):
    me = lax.axis_index("seq")
    chan = lax.axis_index("chan")
    core = lax.axis_index("dp")
    z, xy = me // 16, lax.rem(me, 16)
    x, y = xy // 4, lax.rem(xy, 4)
    following, previous = lax.rem(me + 1, ROWS), lax.rem(me + ROWS - 1, ROWS)
    blocks = feat.shape[3] // LANES
    barrier = pltpu.get_barrier_semaphore()

    def signal(sem, **device):
        pl.semaphore_signal(sem, inc=1, device_id=device, device_id_type=MESH)

    for dz in (2, 1, 3, 0):
        plane = lax.rem(z + dz, 4) * 16

        def greet(i, carry):
            signal(barrier, seq=plane + lax.rem(xy + i, 16))
            return carry

        lax.fori_loop(0 if dz else 1, 16, greet, 0)
        signal(barrier, seq=plane + xy, dp=1 - core)
    for d in range(1, 4):
        signal(barrier, chan=lax.rem(chan + d, 4))

    pairs = [
        (proj_hbm, ext.at[:, :, pl.ds(8, ROWS), :]),
        (taps_hbm, taps_ref),
        (cot_hbm, cot_ref),
        (emb_hbm, emb_ref),
        (w1_hbm, w1_ref),
        (w2_hbm, w2_ref),
        (wo_hbm, wo_ref),
        (first_hbm, first_wide),
        (last_hbm, last_wide),
        (turn_hbm, turn_ref),
        (middle_hbm, middle_wide),
    ]
    copies = [pltpu.make_async_copy(src, dst, loads.at[i]) for i, (src, dst) in enumerate(pairs)]
    for copy in copies:
        copy.start()
    copies[0].wait()
    copies[1].wait()

    def lanes(b):
        return pl.ds(pl.multiple_of(b * LANES, LANES), LANES)

    def tapped(i, w, cols, start, count):
        total = taps_ref[i, 0:1, cols] * ext[i, w, 8 + start : 8 + start + count, cols]
        for j in range(1, RIM + 1):
            rows = slice(8 + start - j, 8 + start - j + count)
            total = total + taps_ref[i, j : j + 1, cols] * ext[i, w, rows, cols]
        feat[i, w, start : start + count, cols] = total

    def later_rows(group):
        def body(b, carry):
            for i in group:
                for w in range(2):
                    tapped(i, w, lanes(b), 8, ROWS - 8)
            return carry

        lax.fori_loop(0, blocks, body, 0)

    def to_peers(source, target, signal_at, sem):
        base = signal_at * AREA
        mine = pl.ds(pl.multiple_of(base + me * OWN, OWN), OWN)
        target[mine, :] = source[mine, :]

        def send(i, carry):
            px, py = lax.rem(x + lax.rem(i // 4, 4), 4), lax.rem(y + i // 16, 4)
            peer = lax.rem(z + lax.rem(i, 4), 4) * 16 + px * 4 + py
            block = pl.ds(pl.multiple_of(base + peer * OWN, OWN), OWN)
            remote(source.at[block], target.at[mine], sent.at[sem], came.at[sem], {"seq": peer}).start()
            return carry

        lax.fori_loop(1, ROWS, send, 0)

    def peers_done(ref, sem):
        part = ref.at[pl.ds(0, AREA - OWN)]
        return remote(part, part, sent.at[sem], came.at[sem], {"seq": me})

    def pack(buffer, features, row):
        for n, (i, w) in enumerate((i, w) for i in features for w in range(2)):
            yield n * RIM, buffer.at[i, w, pl.ds(row, RIM), :]

    def packed(target, buffer, features, row):
        for at, part in pack(buffer, features, row):
            target[at : at + RIM, :] = part[...]

    def unpacked(source, buffer, features, row):
        for at, part in pack(buffer, features, row):
            part[...] = source[at : at + RIM, :]

    def no_rows(buffer, features, row, where):
        @pl.when(me == where)
        def _():
            for i in features:
                buffer[i, :, row : row + 8, :] = jnp.zeros((2, 8, buffer.shape[3]), FLOAT)

    keys = (1, 2)
    edge_q[8:, :] = jnp.zeros((8, edge_q.shape[1]), FLOAT)
    packed(edge_kv, ext, keys, ROWS + 8 - RIM)
    packed(edge_q, ext, (0,), ROWS + 8 - RIM)
    later_rows(keys)
    later_rows((0,))
    pl.semaphore_wait(barrier, ROWS - 1 + 7)

    quarter = edge_kv.shape[1] // 4
    ahead_plane = lax.rem(z + 1, 4) * 16

    def piece(ref, c):
        return ref.at[:, c * quarter : (c + 1) * quarter]

    @pl.when(xy != 15)
    def _():
        remote(edge_kv, rim_kv, sent.at[0], came.at[0], {"seq": following}).start()

    @pl.when(xy == 15)
    def _():
        for c, via in enumerate((3, 12, 0)):
            to = {"seq": z * 16 + via}
            remote(piece(edge_kv, c), piece(relay, c), sent.at[0], came.at[16], to).start()
        remote(piece(edge_kv, 3), piece(rim_kv, 3), sent.at[0], came.at[0], {"seq": following}).start()

    for c, via in enumerate((3, 12, 0)):

        @pl.when(xy == via)
        def _(c=c):
            part = piece(relay, c)
            remote(part, part, sent.at[16], came.at[16], {"seq": me}).wait_recv()
            on = remote(part, piece(rim_kv, c), sent.at[16], came.at[0], {"seq": ahead_plane})
            on.start()
            on.wait_send()

    remote(rim_kv, rim_kv, sent.at[0], came.at[0], {"seq": me}).wait()
    to_q = remote(edge_q, rim_q, sent.at[13], came.at[13], {"seq": following})
    to_q.start()
    unpacked(rim_kv, ext, keys, 8 - RIM)
    no_rows(ext, keys, 0, 0)

    def products(b, carry):
        cols = lanes(b)
        for i in (1, 2):
            for w in range(2):
                tapped(i, w, cols, 0, 8)
        parts = [feat[1, w, :, cols] * feat[2, w, :, cols] for w in range(2)]
        sends[lanes(b), :] = jnp.concatenate(parts, axis=0).T
        return carry

    lax.fori_loop(0, blocks, products, 0)
    to_peers(sends, got, 0, 1)
    to_q.wait()
    unpacked(rim_q, ext, (0,), 8 - RIM)
    no_rows(ext, (0,), 0, 0)
    copies[2].wait()

    def gradients(b, carry):
        cols = lanes(b)
        for w in range(2):
            tapped(0, w, cols, 0, 8)
        parts = [feat[0, w, :, cols] * cot_ref[w, :, cols] for w in range(2)]
        rows = pl.ds(pl.multiple_of(AREA + b * LANES, LANES), LANES)
        sends[rows, :] = jnp.concatenate(parts, axis=0).T
        return carry

    lax.fori_loop(0, blocks, gradients, 0)
    for copy in copies[3:]:
        copy.wait()
    first_ref[...] = first_wide[...].astype(HALF)
    last_ref[...] = last_wide[...].astype(HALF)
    middle_ref[...] = middle_wide[...].astype(HALF)

    turned = pltpu.roll(
        wo_ref[:, lanes(me // 8)], lax.rem(LANES - lax.rem(me, 8) * OWN, LANES), 1
    )
    wo_own = turned[:, :OWN]
    wo_t = flipped(turned)[:OWN, :ROWS]
    w1_t = flipped(w1_ref[...])[:ROWS, : w1_ref.shape[0]]
    w2_t = flipped(w2_ref[...])[:ROWS, :ROWS]
    lane = lax.broadcasted_iota(jnp.int32, (OWN, LANES), 1)
    low_half = lane < ROWS

    def net(step, carry):
        cols = pl.ds(pl.multiple_of(step * STEP, STEP), STEP)
        s1, c1 = sin_cos(dot3(w1_t, emb_ref[:, cols]))
        act1[:, cols] = s1
        cos1[:, cols] = c1
        s2, c2 = sin_cos(dot3(w2_t, s1))
        act2[:, cols] = s2
        cos2[:, cols] = c2
        raw = dot3(wo_t, s2)
        for pair in range(STEP // LANES):
            both = raw[:, pair * LANES : (pair + 1) * LANES]
            other = pltpu.roll(both, ROWS, 1)
            base = pl.multiple_of((step * (STEP // ROWS) + 2 * pair) * OWN, OWN)
            filt[pl.ds(base, OWN), :] = jnp.where(low_half, both, other)
            filt[pl.ds(base + OWN, OWN), :] = jnp.where(low_half, other, both)
        return carry

    lax.fori_loop(0, SEQ // STEP, net, 0)

    place = lax.broadcasted_iota(jnp.int32, (ROWS, LANES), 0) * ROWS + (
        lax.broadcasted_iota(jnp.int32, (ROWS, LANES), 1) & (ROWS - 1)
    )
    place = place.astype(FLOAT)

    def envelope(ch):
        rate = rates_ref[me * OWN + ch]
        return jnp.exp(place * -rate) * jnp.sqrt(jnp.full((1, LANES), 2.0 * rate + 1.0 / SEQ, FLOAT))

    def strided(ref, base, ch):
        return ref[pl.ds(base + ch, ROWS, stride=OWN), :]

    def group_rows(step):
        return pl.ds(pl.multiple_of(step * GROUP * ROWS, GROUP * ROWS), GROUP * ROWS)

    def cut(value):
        return [value[i * ROWS : (i + 1) * ROWS] for i in range(GROUP)]

    def filters(step, carry):
        chans = [step * GROUP + i for i in range(GROUP)]
        signals = [strided(filt, 0, ch) * envelope(ch) for ch in chans]
        fspec[group_rows(step), :] = forward(signals, first_ref, turn_ref, middle_ref)
        return carry

    lax.fori_loop(0, OWN // GROUP, filters, 0)
    to_peers(sends, got, 1, 2)

    def put(value, base, step):
        for i in range(GROUP):
            backs[pl.ds(base + step * GROUP + i, ROWS, stride=OWN), :] = value[
                :, i * LANES : (i + 1) * LANES
            ]

    peers_done(got, 1).wait_recv()

    def convolve(step, carry):
        signals = [strided(got, 0, step * GROUP + i) for i in range(GROUP)]
        spec = forward(signals, first_ref, turn_ref, middle_ref)
        pspec[group_rows(step), :] = spec
        rows = cut(times(spec, fspec[group_rows(step), :]))
        put(inverse(rows, last_ref, turn_ref, middle_ref), 0, step)
        return carry

    lax.fori_loop(0, OWN // GROUP, convolve, 0)
    to_peers(backs, home, 0, 3)
    peers_done(got, 2).wait_recv()

    def correlate(step, carry):
        signals = [strided(got, AREA, step * GROUP + i) for i in range(GROUP)]
        spec = forward(signals, first_ref, turn_ref, middle_ref)
        rows = cut(times_conj(fspec[group_rows(step), :], spec))
        put(inverse(rows, last_ref, turn_ref, middle_ref), AREA, step)
        gspec[group_rows(step), :] = spec
        return carry

    lax.fori_loop(0, OWN // GROUP, correlate, 0)
    to_peers(backs, home, 1, 4)

    def filter_back(step, carry):
        pair = times_conj(pspec[group_rows(step), :], gspec[group_rows(step), :])
        re, im = pair[:, :LANES], pair[:, LANES:]
        rows = cut(columns([re + pltpu.roll(re, ROWS, 1), im + pltpu.roll(im, ROWS, 1)]))
        value = inverse(rows, last_ref, turn_ref, middle_ref)
        for i in range(GROUP):
            ch = step * GROUP + i
            filt[pl.ds(ch, ROWS, stride=OWN), :] = value[:, i * LANES : (i + 1) * LANES] * envelope(ch)
        return carry

    lax.fori_loop(0, OWN // GROUP, filter_back, 0)
    acc_out[...] = jnp.zeros_like(acc_out)
    acc_net[...] = jnp.zeros_like(acc_net)

    def net_back(step, carry):
        cols = pl.ds(pl.multiple_of(step * STEP, STEP), STEP)
        parts = []
        for pair in range(STEP // LANES):
            base = pl.multiple_of((step * (STEP // ROWS) + 2 * pair) * OWN, OWN)
            parts.append(jnp.where(low_half, filt[pl.ds(base, OWN), :], filt[pl.ds(base + OWN, OWN), :]))
        kgrad = columns(parts)
        acc_out[...] += dot3(kgrad, act2[:, cols], "nt")
        pre2 = dot3(wo_own, kgrad) * cos2[:, cols]
        acc_net[32:, :] += dot3(act1[:, cols], pre2, "nt")
        pre1 = dot3(w2_ref[...], pre2) * cos1[:, cols]
        acc_net[:32, :] += dot3(emb_ref[:, cols], pre1, "nt")
        return carry

    lax.fori_loop(0, SEQ // STEP, net_back, 0)
    out_mine[...] = columns([acc_out[:8, :], acc_out[8:, :]])
    by_chan[chan] = columns([acc_net[:48, :], acc_net[48:, :]])
    swap = remote(out_mine, out_dp, sent.at[5], came.at[5], {"dp": 1 - core})
    swap.start()
    for d in range(1, 4):
        part = by_chan.at[chan]
        remote(part, part, sent.at[6], came.at[6], {"chan": lax.rem(chan + d, 4)}).start()
    swap.wait()
    outs[z, xy] = out_mine[...] + out_dp[...]
    for d in range(1, 4):
        part = outs.at[z, xy]
        remote(part, part, sent.at[7], came.at[7], {"seq": lax.rem(z + d, 4) * 16 + xy}).start()
    chans_done = remote(by_chan.at[pl.ds(0, 3)], by_chan.at[pl.ds(0, 3)], sent.at[6], came.at[6], {"seq": me})
    zs_done = remote(outs.at[pl.ds(0, 3), 0], outs.at[pl.ds(0, 3), 0], sent.at[7], came.at[7], {"seq": me})
    zs_done.wait()

    def around(i):
        return z * 16 + lax.rem(x + i // 4, 4) * 4 + lax.rem(y + lax.rem(i, 4), 4)

    def spread_outs(i, carry):
        column = outs.at[:, xy]
        remote(column, column, sent.at[8], came.at[8], {"seq": around(i)}).start()
        return carry

    lax.fori_loop(1, 16, spread_outs, 0)
    chans_done.wait()
    net_sum = (by_chan[0] + by_chan[1]) + (by_chan[2] + by_chan[3])
    for i in range(6):
        tiles[24 + i] = net_sum[i * 8 : (i + 1) * 8]
    tiles[30] = jnp.zeros((8, LANES), FLOAT)
    tiles[31] = jnp.zeros((8, LANES), FLOAT)

    def scatter():
        phase1[xy] = tiles[pl.ds(2 * xy, 2)]

        def send(i, carry):
            q = around(i)
            part = tiles.at[pl.ds(2 * (q - z * 16), 2)]
            remote(part, phase1.at[xy], sent.at[10], came.at[10], {"seq": q}).start()
            return carry

        lax.fori_loop(1, 16, send, 0)

    def exchange():
        first15 = phase1.at[pl.ds(0, 15)]
        remote(first15, first15, sent.at[10], came.at[10], {"seq": me}).wait()
        sum1[...] = jnp.sum(phase1[...], axis=0)
        mine = phase2.at[z * 2 + core]
        phase2[z * 2 + core] = sum1[...]
        for dz in (2, 1, 3, 0):
            for dc in (0, 1):
                if dz or dc:
                    to = {"seq": lax.rem(z + dz, 4) * 16 + xy, "dp": lax.rem(core + dc, 2)}
                    remote(sum1, mine, sent.at[11], came.at[11], to).start()

    def gather():
        first7 = phase2.at[pl.ds(0, 7)]
        remote(first7, first7, sent.at[11], came.at[11], {"seq": me}).wait()
        sum2[...] = jnp.sum(phase2[...], axis=0)
        phase3[xy] = sum2[...]

        def send(i, carry):
            remote(sum2, phase3.at[xy], sent.at[12], came.at[12], {"seq": around(i)}).start()
            return carry

        lax.fori_loop(1, 16, send, 0)

    def tap_sums(features):
        def body(b, carry):
            cols = lanes(b)
            for i in features:
                sums = []
                for j in range(RIM + 1):
                    both = ahead[i, 0, :ROWS, cols] * ext[i, 0, 8 - j : 8 - j + ROWS, cols]
                    both = both + ahead[i, 1, :ROWS, cols] * ext[i, 1, 8 - j : 8 - j + ROWS, cols]
                    sums.append(jnp.sum(both, axis=0, keepdims=True))
                sums.append(jnp.zeros((1, LANES), FLOAT))
                tiles[i * 8 + b] = jnp.concatenate(sums, axis=0)
            return carry

        lax.fori_loop(0, blocks, body, 0)

    def raws(i):
        def body(b, carry):
            cols = lanes(b)
            for w in range(2):
                total = taps_ref[i, 0:1, cols] * ahead[i, w, :ROWS, cols]
                for j in range(1, RIM + 1):
                    total = total + taps_ref[i, j : j + 1, cols] * ahead[i, w, j : j + ROWS, cols]
                raw_ref[i, w, :, cols] = total
            return carry

        lax.fori_loop(0, blocks, body, 0)
        save = pltpu.make_async_copy(raw_ref.at[i], raw_hbm.at[i], saves.at[1 + i])
        save.start()
        return save

    peers_done(home, 3).wait_recv()

    def mix(b, carry):
        cols = lanes(b)
        conv = home[lanes(b), :].T
        for w in range(2):
            part = conv[w * ROWS : (w + 1) * ROWS]
            mixed_ref[w, :, cols] = feat[0, w, :, cols] * part
            ahead[0, w, :ROWS, cols] = cot_ref[w, :, cols] * part
        return carry

    lax.fori_loop(0, blocks, mix, 0)
    packed(edge_q, ahead, (0,), 0)
    after_q = remote(edge_q, after_q_rows, sent.at[9], came.at[9], {"seq": previous})
    after_q.start()
    save_mixed = pltpu.make_async_copy(mixed_ref, mixed_hbm, saves.at[0])
    save_mixed.start()
    tap_sums((0,))

    outs_part = outs.at[:, pl.ds(0, 15)]
    remote(outs_part, outs_part, sent.at[8], came.at[8], {"seq": me}).wait()
    windows = 4
    tail = 1.0 / math.sqrt(windows * SEQ)
    scale = 4.0 / math.sqrt(windows * SEQ * blocks * LANES * 4)
    for b in range(blocks):
        rows = []
        for s in range(8 * b, 8 * b + 8):
            tile = outs[s // 16, s % 16]
            rows += [tile, pltpu.roll(tile, ROWS, 1)]
        square = jnp.concatenate(rows, axis=0).T
        out_ref[:, b * LANES : (b + 1) * LANES] = square[:ROWS] * tail

    peers_done(home, 4).wait_recv()

    def unmix(b, carry):
        cols = lanes(b)
        back = home[pl.ds(pl.multiple_of(AREA + b * LANES, LANES), LANES), :].T
        for w in range(2):
            part = back[w * ROWS : (w + 1) * ROWS]
            ahead[1, w, :ROWS, cols] = part * feat[2, w, :, cols]
            ahead[2, w, :ROWS, cols] = part * feat[1, w, :, cols]
        return carry

    lax.fori_loop(0, blocks, unmix, 0)
    packed(edge_kv, ahead, keys, 0)
    after_kv = remote(edge_kv, after_kv_rows, sent.at[14], came.at[14], {"seq": previous})
    after_kv.start()
    tap_sums(keys)
    scatter()
    after_q.wait()
    unpacked(after_q_rows, ahead, (0,), ROWS)
    no_rows(ahead, (0,), ROWS, ROWS - 1)
    save_q = raws(0)
    exchange()
    after_kv.wait()
    unpacked(after_kv_rows, ahead, keys, ROWS)
    no_rows(ahead, keys, ROWS, ROWS - 1)
    save_k = raws(1)
    save_v = raws(2)
    gather()
    for sem in (1, 2):
        peers_done(sends, sem).wait_send()
    for sem in (3, 4):
        peers_done(backs, sem).wait_send()
    for save in (save_mixed, save_q, save_k, save_v):
        save.wait()
    last15 = phase3.at[pl.ds(0, 15)]
    remote(last15, last15, sent.at[12], came.at[12], {"seq": me}).wait()
    for i in range(3):
        for b in range(blocks):
            t = i * 8 + b
            short_ref[i, :, b * LANES : (b + 1) * LANES] = phase3[t // 2, t % 2][: RIM + 1] * tail
    net_sum = jnp.concatenate([phase3[t // 2, t % 2] for t in range(24, 30)], axis=0) * scale
    netf_ref[...] = net_sum[:32, :ROWS]
    nets_ref[:16, :] = net_sum[32:, :ROWS]
    nets_ref[16:, :] = net_sum[:, ROWS:]


def land_kernel(*refs):
    count = (len(refs) - 2) // 3
    sources, targets, held = refs[:count], refs[count : 2 * count], refs[2 * count : 3 * count]
    loads, stores = refs[3 * count :]
    pieces = []
    for n, source in enumerate(sources):
        lead = source.shape[:-2]
        pieces += [(n, at) for at in np.ndindex(*lead)] if source.shape[-2] == ROWS else [(n, ())]

    def part(ref, at):
        return ref.at[at] if at else ref

    first = [
        pltpu.make_async_copy(part(sources[n], at), part(held[n], at), loads.at[k])
        for k, (n, at) in enumerate(pieces)
    ]
    second = [
        pltpu.make_async_copy(part(held[n], at), part(targets[n], at), stores.at[k])
        for k, (n, at) in enumerate(pieces)
    ]
    for copy in first:
        copy.start()
    for load, store in zip(first, second):
        load.wait()
        store.start()
    for copy in second:
        copy.wait()


def shards(projected, short_weight, decay_rates, w1, w2, out_weight, cotangent):
    first_stack, last_stack, turn, middle, embedded = tables()
    vmem = pl.BlockSpec(memory_space=pltpu.VMEM)
    hbm = pl.BlockSpec(memory_space=pl.ANY)
    group = projected.shape[3]
    hidden = w2.shape[0]

    def buffer(*shape):
        return pltpu.VMEM(shape, FLOAT)

    def held(value):
        return buffer(*value.shape)

    def like(value):
        return jax.ShapeDtypeStruct(value.shape, FLOAT)

    rows = projected.shape[2] + 8
    results = pl.pallas_call(
        whole_kernel,
        out_shape=(
            like(cotangent),
            like(projected),
            like(short_weight),
            like(out_weight),
            like(w1),
            like(w2),
        ),
        in_specs=[pl.BlockSpec(memory_space=pltpu.SMEM)] + [hbm] * 11,
        out_specs=(hbm, hbm) + (vmem,) * 4,
        scratch_shapes=[
            held(short_weight),
            held(cotangent),
            buffer(w1.shape[0], SEQ),
            held(w1),
            held(w2),
            held(out_weight),
            held(first_stack),
            held(last_stack),
            held(turn),
            held(middle),
            pltpu.VMEM(first_stack.shape, HALF),
            pltpu.VMEM(last_stack.shape, HALF),
            pltpu.VMEM(middle.shape, HALF),
            held(cotangent),
            held(projected),
            buffer(3, 2, rows, group),
            buffer(3, 2, rows, group),
            buffer(3, 2, ROWS, group),
            buffer(2 * AREA, LANES),
            buffer(2 * AREA, LANES),
            buffer(2 * AREA, LANES),
            buffer(2 * AREA, LANES),
            buffer(hidden, SEQ),
            buffer(hidden, SEQ),
            buffer(hidden, SEQ),
            buffer(hidden, SEQ),
            buffer(AREA, LANES),
            buffer(AREA, 2 * LANES),
            buffer(AREA, 2 * LANES),
            buffer(AREA, 2 * LANES),
            buffer(8, LANES),
            buffer(8, LANES),
            buffer(4, 48, LANES),
            buffer(4, 16, 8, LANES),
            buffer(32, 8, LANES),
            buffer(16, 2, 8, LANES),
            buffer(2, 8, LANES),
            buffer(8, 2, 8, LANES),
            buffer(2, 8, LANES),
            buffer(16, 2, 8, LANES),
            buffer(OWN, hidden),
            buffer(96, hidden),
            buffer(24, group),
            buffer(24, group),
            buffer(24, group),
            buffer(24, group),
            buffer(16, group),
            buffer(16, group),
            buffer(16, group),
            pltpu.SemaphoreType.DMA((11,)),
            pltpu.SemaphoreType.DMA((4,)),
            pltpu.SemaphoreType.DMA((18,)),
            pltpu.SemaphoreType.DMA((18,)),
        ],
        compiler_params=pltpu.CompilerParams(
            collective_id=1, has_side_effects=True, vmem_limit_bytes=60 << 20
        ),
        name="whole",
    )(
        decay_rates,
        projected,
        short_weight,
        cotangent,
        jnp.asarray(embedded),
        w1,
        w2,
        out_weight,
        jnp.asarray(first_stack),
        jnp.asarray(last_stack),
        jnp.asarray(turn),
        jnp.asarray(middle),
    )
    return pl.pallas_call(
        land_kernel,
        out_shape=tuple(like(v) for v in results),
        in_specs=[hbm] * len(results),
        out_specs=(hbm,) * len(results),
        scratch_shapes=[held(v) for v in results]
        + [pltpu.SemaphoreType.DMA((16,)), pltpu.SemaphoreType.DMA((16,))],
        compiler_params=pltpu.CompilerParams(vmem_limit_bytes=60 << 20),
        name="land",
    )(*results)


def solution(mesh):
    return jax.shard_map(
        shards,
        mesh=mesh,
        in_specs=(
            P(None, "dp", "seq", "chan"),
            P(None, None, "chan"),
            P("chan"),
            P(),
            P(),
            P(None, "chan"),
            P("dp", "seq", "chan"),
        ),
        out_specs=(
            P("dp", "seq", "chan"),
            P(None, "dp", "seq", "chan"),
            P(None, None, "chan"),
            P(None, "chan"),
            P(),
            P(),
        ),
        check_vma=False,
    )
```

```python
import functools
import math

import jax
import jax.numpy as jnp
import ml_dtypes
import numpy as np
from jax import lax
from jax.experimental import pallas as pl
from jax.experimental.pallas import tpu as pltpu
from jax.sharding import PartitionSpec as P

MESH = pl.DeviceIdType.MESH
ROWS = 64
OWN = 16
LANES = 128
SEQ = ROWS * ROWS
RIM = 6
STEP = 512
FLOAT = jnp.float32
HALF = jnp.bfloat16


def halves(table):
    high = table.astype(ml_dtypes.bfloat16)
    low = (table - high.astype(np.float64)).astype(ml_dtypes.bfloat16)
    return high, low


@functools.cache
def tables():
    k = np.arange(ROWS)[:, None] + 0.25
    s = np.arange(ROWS)[None, :]
    theta = 2 * np.pi * k * s / ROWS
    first = np.concatenate([np.cos(theta), -np.sin(theta)], axis=0)
    high, low = halves(first)
    first_stack = np.concatenate([high, high, low], axis=1)
    last = np.concatenate([np.cos(theta).T, -np.sin(theta).T], axis=1) / SEQ
    high, low = halves(last)
    last_stack = np.concatenate([high, high, low], axis=1)
    phi = 2 * np.pi * k * s / SEQ
    turn = np.stack([np.tile(np.cos(phi), (1, 2)), np.tile(np.sin(phi), (1, 2))]).astype(np.float32)
    inner = 2 * np.pi * (np.arange(ROWS)[:, None] * s % ROWS) / ROWS
    cos, sin = np.kron(np.eye(2), np.cos(inner)), np.kron(np.eye(2), np.sin(inner))
    there = np.block([[cos, -sin], [sin, cos]])
    back = np.block([[cos, sin], [-sin, cos]])
    middle = np.stack(halves(there) + halves(back))
    half = 16
    orders = np.arange(half, dtype=np.int64)
    factors = 1 + (SEQ // 2 - 2) * orders * orders // max((half - 1) ** 2, 1)
    angle = 2 * np.pi * (factors[:, None] * np.arange(SEQ)[None, :] % SEQ) / SEQ
    embedded = np.concatenate([np.cos(angle), np.sin(angle)], axis=0).astype(np.float32)
    return (*(t.astype(np.float32) for t in (first_stack, last_stack)), turn, middle.astype(np.float32), embedded)


def split(value):
    high = value.astype(HALF)
    return high, (value - high.astype(FLOAT)).astype(HALF)


def dot(a, b, kind="nn"):
    dims = {"nn": ((1,), (0,)), "nt": ((1,), (1,))}[kind]
    return lax.dot_general(a, b, (dims, ((), ())), preferred_element_type=FLOAT)


def dot3(a, b, kind="nn"):
    ah, al = split(a)
    bh, bl = split(b)
    return dot(ah, bh, kind) + (dot(ah, bl, kind) + dot(al, bh, kind))


def sin_cos(x):
    n = jnp.floor(x * (2.0 / math.pi) + 0.5)
    r = x - n * 1.5703125
    r = r - n * 4.837512969970703125e-4
    r = r - n * 7.549789948768648e-8
    z = r * r
    s = r + r * z * (-1.6666654611e-1 + z * (8.3321608736e-3 + z * -1.9515295891e-4))
    c = 1.0 - 0.5 * z + z * z * (4.166664568298827e-2 + z * (-1.388731625493765e-3 + z * 2.443315711809948e-5))
    q = n.astype(jnp.int32)
    odd = (q & 1) == 1
    sin = jnp.where(odd, c, s)
    cos = jnp.where(odd, s, c)
    sin = jnp.where((q & 2) == 2, -sin, sin)
    cos = jnp.where(((q + 1) & 2) == 2, -cos, cos)
    return sin, cos


def columns(parts):
    return jnp.concatenate(parts, axis=1)


def forward(signals, first, turn, middle):
    cos, sin = turn[0], turn[1]
    high, low = split(columns(signals))
    spec = dot(first[...], jnp.concatenate([high, low, high], axis=0))
    rows = []
    for i in range(len(signals)):
        re = spec[:ROWS, i * LANES : (i + 1) * LANES]
        im = spec[ROWS:, i * LANES : (i + 1) * LANES]
        rows.append(columns([re * cos + im * sin, im * cos - re * sin]))
    high, low = split(jnp.concatenate(rows, axis=0))
    return dot(high, middle[0]) + (dot(low, middle[0]) + dot(high, middle[1]))


def inverse(rows, last, turn, middle):
    cos, sin = turn[0], turn[1]
    high, low = split(jnp.concatenate(rows, axis=0))
    freq = dot(high, middle[2]) + (dot(low, middle[2]) + dot(high, middle[3]))
    cols = []
    for i in range(len(rows)):
        re = freq[i * ROWS : (i + 1) * ROWS, :LANES]
        im = freq[i * ROWS : (i + 1) * ROWS, LANES:]
        cols.append(jnp.concatenate([re * cos - im * sin, re * sin + im * cos], axis=0))
    high, low = split(columns(cols))
    return dot(last[...], jnp.concatenate([high, low, high], axis=0))


def times(a, b):
    ar, ai, br, bi = a[:, :LANES], a[:, LANES:], b[:, :LANES], b[:, LANES:]
    return columns([ar * br - ai * bi, ar * bi + ai * br])


def times_conj(a, b):
    ar, ai, br, bi = a[:, :LANES], a[:, LANES:], b[:, :LANES], b[:, LANES:]
    return columns([ar * br + ai * bi, ar * bi - ai * br])


def flipped(small):
    rows, cols = small.shape
    tall = jnp.concatenate([small, jnp.zeros((LANES - rows, cols), FLOAT)], axis=0)
    square = columns([tall, jnp.zeros((LANES, LANES - cols), FLOAT)]) if cols < LANES else tall
    return square.T


def remote(src, dst, send_sem, recv_sem, device):
    return pltpu.make_async_remote_copy(
        src_ref=src,
        dst_ref=dst,
        send_sem=send_sem,
        recv_sem=recv_sem,
        device_id=device,
        device_id_type=MESH,
    )


GROUP = 4
AREA = ROWS * OWN


def whole_kernel(
    rates_ref,
    proj_hbm,
    taps_hbm,
    cot_hbm,
    emb_hbm,
    w1_hbm,
    w2_hbm,
    wo_hbm,
    first_hbm,
    last_hbm,
    turn_hbm,
    middle_hbm,
    mixed_hbm,
    raw_hbm,
    short_ref,
    out_ref,
    netf_ref,
    nets_ref,
    taps_ref,
    cot_ref,
    emb_ref,
    w1_ref,
    w2_ref,
    wo_ref,
    first_wide,
    last_wide,
    turn_ref,
    middle_wide,
    first_ref,
    last_ref,
    middle_ref,
    mixed_ref,
    raw_ref,
    ext,
    ahead,
    feat,
    sends,
    got,
    backs,
    home,
    act1,
    cos1,
    act2,
    cos2,
    filt,
    fspec,
    pspec,
    gspec,
    out_mine,
    out_dp,
    by_chan,
    outs,
    tiles,
    phase1,
    sum1,
    phase2,
    sum2,
    phase3,
    acc_out,
    acc_net,
    edge_kv,
    rim_kv,
    relay,
    after_kv_rows,
    edge_q,
    rim_q,
    after_q_rows,
    loads,
    saves,
    sent,
    came,
):
    me = lax.axis_index("seq")
    chan = lax.axis_index("chan")
    core = lax.axis_index("dp")
    z, xy = me // 16, lax.rem(me, 16)
    x, y = xy // 4, lax.rem(xy, 4)
    following, previous = lax.rem(me + 1, ROWS), lax.rem(me + ROWS - 1, ROWS)
    blocks = feat.shape[3] // LANES
    barrier = pltpu.get_barrier_semaphore()

    def signal(sem, **device):
        pl.semaphore_signal(sem, inc=1, device_id=device, device_id_type=MESH)

    for dz in (2, 1, 3, 0):
        plane = lax.rem(z + dz, 4) * 16

        def greet(i, carry):
            signal(barrier, seq=plane + lax.rem(xy + i, 16))
            return carry

        lax.fori_loop(0 if dz else 1, 16, greet, 0)
        signal(barrier, seq=plane + xy, dp=1 - core)
    for d in range(1, 4):
        signal(barrier, chan=lax.rem(chan + d, 4))

    pairs = [
        (proj_hbm, ext.at[:, :, pl.ds(8, ROWS), :]),
        (taps_hbm, taps_ref),
        (cot_hbm, cot_ref),
        (emb_hbm, emb_ref),
        (w1_hbm, w1_ref),
        (w2_hbm, w2_ref),
        (wo_hbm, wo_ref),
        (first_hbm, first_wide),
        (last_hbm, last_wide),
        (turn_hbm, turn_ref),
        (middle_hbm, middle_wide),
    ]
    copies = [pltpu.make_async_copy(src, dst, loads.at[i]) for i, (src, dst) in enumerate(pairs)]
    for copy in copies:
        copy.start()
    copies[0].wait()
    copies[1].wait()

    def lanes(b):
        return pl.ds(pl.multiple_of(b * LANES, LANES), LANES)

    def tapped(i, w, cols, start, count):
        total = taps_ref[i, 0:1, cols] * ext[i, w, 8 + start : 8 + start + count, cols]
        for j in range(1, RIM + 1):
            rows = slice(8 + start - j, 8 + start - j + count)
            total = total + taps_ref[i, j : j + 1, cols] * ext[i, w, rows, cols]
        feat[i, w, start : start + count, cols] = total

    def later_rows(group):
        def body(b, carry):
            for i in group:
                for w in range(2):
                    tapped(i, w, lanes(b), 8, ROWS - 8)
            return carry

        lax.fori_loop(0, blocks, body, 0)

    def to_peers(source, target, signal_at, sem):
        base = signal_at * AREA
        mine = pl.ds(pl.multiple_of(base + me * OWN, OWN), OWN)
        target[mine, :] = source[mine, :]

        def send(i, carry):
            i = lax.rem(i - 1 + 31 * core + 5 * xy, ROWS - 1) + 1
            px, py = lax.rem(x + lax.rem(i // 4, 4), 4), lax.rem(y + i // 16, 4)
            peer = lax.rem(z + lax.rem(i, 4), 4) * 16 + px * 4 + py
            block = pl.ds(pl.multiple_of(base + peer * OWN, OWN), OWN)
            remote(source.at[block], target.at[mine], sent.at[sem], came.at[sem], {"seq": peer}).start()
            return carry

        lax.fori_loop(1, ROWS, send, 0)

    def peers_done(ref, sem):
        part = ref.at[pl.ds(0, AREA - OWN)]
        return remote(part, part, sent.at[sem], came.at[sem], {"seq": me})

    def pack(buffer, features, row):
        for n, (i, w) in enumerate((i, w) for i in features for w in range(2)):
            yield n * RIM, buffer.at[i, w, pl.ds(row, RIM), :]

    def packed(target, buffer, features, row):
        for at, part in pack(buffer, features, row):
            target[at : at + RIM, :] = part[...]

    def unpacked(source, buffer, features, row):
        for at, part in pack(buffer, features, row):
            part[...] = source[at : at + RIM, :]

    def no_rows(buffer, features, row, where):
        @pl.when(me == where)
        def _():
            for i in features:
                buffer[i, :, row : row + 8, :] = jnp.zeros((2, 8, buffer.shape[3]), FLOAT)

    keys = (1, 2)
    edge_q[8:, :] = jnp.zeros((8, edge_q.shape[1]), FLOAT)
    packed(edge_kv, ext, keys, ROWS + 8 - RIM)
    packed(edge_q, ext, (0,), ROWS + 8 - RIM)
    later_rows(keys)
    later_rows((0,))
    pl.semaphore_wait(barrier, ROWS - 1 + 7)

    quarter = edge_kv.shape[1] // 4
    ahead_plane = lax.rem(z + 1, 4) * 16

    def piece(ref, c):
        return ref.at[:, c * quarter : (c + 1) * quarter]

    @pl.when(xy != 15)
    def _():
        remote(edge_kv, rim_kv, sent.at[0], came.at[0], {"seq": following}).start()

    @pl.when(xy == 15)
    def _():
        for c, via in enumerate((3, 12, 0)):
            to = {"seq": z * 16 + via}
            remote(piece(edge_kv, c), piece(relay, c), sent.at[0], came.at[16], to).start()
        remote(piece(edge_kv, 3), piece(rim_kv, 3), sent.at[0], came.at[0], {"seq": following}).start()

    for c, via in enumerate((3, 12, 0)):

        @pl.when(xy == via)
        def _(c=c):
            part = piece(relay, c)
            remote(part, part, sent.at[16], came.at[16], {"seq": me}).wait_recv()
            on = remote(part, piece(rim_kv, c), sent.at[16], came.at[0], {"seq": ahead_plane})
            on.start()
            on.wait_send()

    remote(rim_kv, rim_kv, sent.at[0], came.at[0], {"seq": me}).wait()
    to_q = remote(edge_q, rim_q, sent.at[13], came.at[13], {"seq": following})
    to_q.start()
    unpacked(rim_kv, ext, keys, 8 - RIM)
    no_rows(ext, keys, 0, 0)

    def products(b, carry):
        cols = lanes(b)
        for i in (1, 2):
            for w in range(2):
                tapped(i, w, cols, 0, 8)
        parts = [feat[1, w, :, cols] * feat[2, w, :, cols] for w in range(2)]
        sends[lanes(b), :] = jnp.concatenate(parts, axis=0).T
        return carry

    lax.fori_loop(0, blocks, products, 0)
    to_peers(sends, got, 0, 1)
    to_q.wait()
    unpacked(rim_q, ext, (0,), 8 - RIM)
    no_rows(ext, (0,), 0, 0)
    copies[2].wait()

    def gradients(b, carry):
        cols = lanes(b)
        for w in range(2):
            tapped(0, w, cols, 0, 8)
        parts = [feat[0, w, :, cols] * cot_ref[w, :, cols] for w in range(2)]
        rows = pl.ds(pl.multiple_of(AREA + b * LANES, LANES), LANES)
        sends[rows, :] = jnp.concatenate(parts, axis=0).T
        return carry

    lax.fori_loop(0, blocks, gradients, 0)
    for copy in copies[3:]:
        copy.wait()
    first_ref[...] = first_wide[...].astype(HALF)
    last_ref[...] = last_wide[...].astype(HALF)
    middle_ref[...] = middle_wide[...].astype(HALF)

    turned = pltpu.roll(
        wo_ref[:, lanes(me // 8)], lax.rem(LANES - lax.rem(me, 8) * OWN, LANES), 1
    )
    wo_own = turned[:, :OWN]
    wo_t = flipped(turned)[:OWN, :ROWS]
    w1_t = flipped(w1_ref[...])[:ROWS, : w1_ref.shape[0]]
    w2_t = flipped(w2_ref[...])[:ROWS, :ROWS]
    lane = lax.broadcasted_iota(jnp.int32, (OWN, LANES), 1)
    low_half = lane < ROWS

    def net(step, carry):
        cols = pl.ds(pl.multiple_of(step * STEP, STEP), STEP)
        s1, c1 = sin_cos(dot3(w1_t, emb_ref[:, cols]))
        act1[:, cols] = s1
        cos1[:, cols] = c1
        s2, c2 = sin_cos(dot3(w2_t, s1))
        act2[:, cols] = s2
        cos2[:, cols] = c2
        raw = dot3(wo_t, s2)
        for pair in range(STEP // LANES):
            both = raw[:, pair * LANES : (pair + 1) * LANES]
            other = pltpu.roll(both, ROWS, 1)
            base = pl.multiple_of((step * (STEP // ROWS) + 2 * pair) * OWN, OWN)
            filt[pl.ds(base, OWN), :] = jnp.where(low_half, both, other)
            filt[pl.ds(base + OWN, OWN), :] = jnp.where(low_half, other, both)
        return carry

    lax.fori_loop(0, SEQ // STEP, net, 0)

    place = lax.broadcasted_iota(jnp.int32, (ROWS, LANES), 0) * ROWS + (
        lax.broadcasted_iota(jnp.int32, (ROWS, LANES), 1) & (ROWS - 1)
    )
    place = place.astype(FLOAT)

    def envelope(ch):
        rate = rates_ref[me * OWN + ch]
        return jnp.exp(place * -rate) * jnp.sqrt(jnp.full((1, LANES), 2.0 * rate + 1.0 / SEQ, FLOAT))

    def strided(ref, base, ch):
        return ref[pl.ds(base + ch, ROWS, stride=OWN), :]

    def group_rows(step):
        return pl.ds(pl.multiple_of(step * GROUP * ROWS, GROUP * ROWS), GROUP * ROWS)

    def cut(value):
        return [value[i * ROWS : (i + 1) * ROWS] for i in range(GROUP)]

    def filters(step, carry):
        chans = [step * GROUP + i for i in range(GROUP)]
        signals = [strided(filt, 0, ch) * envelope(ch) for ch in chans]
        fspec[group_rows(step), :] = forward(signals, first_ref, turn_ref, middle_ref)
        return carry

    lax.fori_loop(0, OWN // GROUP, filters, 0)
    to_peers(sends, got, 1, 2)

    def put(value, base, step):
        for i in range(GROUP):
            backs[pl.ds(base + step * GROUP + i, ROWS, stride=OWN), :] = value[
                :, i * LANES : (i + 1) * LANES
            ]

    peers_done(got, 1).wait_recv()

    def convolve(step, carry):
        signals = [strided(got, 0, step * GROUP + i) for i in range(GROUP)]
        spec = forward(signals, first_ref, turn_ref, middle_ref)
        pspec[group_rows(step), :] = spec
        rows = cut(times(spec, fspec[group_rows(step), :]))
        put(inverse(rows, last_ref, turn_ref, middle_ref), 0, step)
        return carry

    lax.fori_loop(0, OWN // GROUP, convolve, 0)
    to_peers(backs, home, 0, 3)
    peers_done(got, 2).wait_recv()

    def correlate(step, carry):
        signals = [strided(got, AREA, step * GROUP + i) for i in range(GROUP)]
        spec = forward(signals, first_ref, turn_ref, middle_ref)
        rows = cut(times_conj(fspec[group_rows(step), :], spec))
        put(inverse(rows, last_ref, turn_ref, middle_ref), AREA, step)
        gspec[group_rows(step), :] = spec
        return carry

    lax.fori_loop(0, OWN // GROUP, correlate, 0)
    to_peers(backs, home, 1, 4)

    def filter_back(step, carry):
        pair = times_conj(pspec[group_rows(step), :], gspec[group_rows(step), :])
        re, im = pair[:, :LANES], pair[:, LANES:]
        rows = cut(columns([re + pltpu.roll(re, ROWS, 1), im + pltpu.roll(im, ROWS, 1)]))
        value = inverse(rows, last_ref, turn_ref, middle_ref)
        for i in range(GROUP):
            ch = step * GROUP + i
            filt[pl.ds(ch, ROWS, stride=OWN), :] = value[:, i * LANES : (i + 1) * LANES] * envelope(ch)
        return carry

    lax.fori_loop(0, OWN // GROUP, filter_back, 0)
    acc_out[...] = jnp.zeros_like(acc_out)
    acc_net[...] = jnp.zeros_like(acc_net)

    def net_back(step, carry):
        cols = pl.ds(pl.multiple_of(step * STEP, STEP), STEP)
        parts = []
        for pair in range(STEP // LANES):
            base = pl.multiple_of((step * (STEP // ROWS) + 2 * pair) * OWN, OWN)
            parts.append(jnp.where(low_half, filt[pl.ds(base, OWN), :], filt[pl.ds(base + OWN, OWN), :]))
        kgrad = columns(parts)
        acc_out[...] += dot3(kgrad, act2[:, cols], "nt")
        pre2 = dot3(wo_own, kgrad) * cos2[:, cols]
        acc_net[32:, :] += dot3(act1[:, cols], pre2, "nt")
        pre1 = dot3(w2_ref[...], pre2) * cos1[:, cols]
        acc_net[:32, :] += dot3(emb_ref[:, cols], pre1, "nt")
        return carry

    lax.fori_loop(0, SEQ // STEP, net_back, 0)
    out_mine[...] = columns([acc_out[:8, :], acc_out[8:, :]])
    by_chan[chan] = columns([acc_net[:48, :], acc_net[48:, :]])
    swap = remote(out_mine, out_dp, sent.at[5], came.at[5], {"dp": 1 - core})
    swap.start()
    for d in range(1, 4):
        part = by_chan.at[chan]
        remote(part, part, sent.at[6], came.at[6], {"chan": lax.rem(chan + d, 4)}).start()
    swap.wait()
    outs[z, xy] = out_mine[...] + out_dp[...]
    for d in range(1, 4):
        part = outs.at[z, xy]
        remote(part, part, sent.at[7], came.at[7], {"seq": lax.rem(z + d, 4) * 16 + xy}).start()
    chans_done = remote(by_chan.at[pl.ds(0, 3)], by_chan.at[pl.ds(0, 3)], sent.at[6], came.at[6], {"seq": me})
    zs_done = remote(outs.at[pl.ds(0, 3), 0], outs.at[pl.ds(0, 3), 0], sent.at[7], came.at[7], {"seq": me})
    zs_done.wait()

    def around(i):
        return z * 16 + lax.rem(x + i // 4, 4) * 4 + lax.rem(y + lax.rem(i, 4), 4)

    def spread_outs(i, carry):
        column = outs.at[:, xy]
        remote(column, column, sent.at[8], came.at[8], {"seq": around(i)}).start()
        return carry

    lax.fori_loop(1, 16, spread_outs, 0)
    chans_done.wait()
    net_sum = (by_chan[0] + by_chan[1]) + (by_chan[2] + by_chan[3])
    for i in range(6):
        tiles[24 + i] = net_sum[i * 8 : (i + 1) * 8]
    tiles[30] = jnp.zeros((8, LANES), FLOAT)
    tiles[31] = jnp.zeros((8, LANES), FLOAT)

    def scatter():
        phase1[xy] = tiles[pl.ds(2 * xy, 2)]

        def send(i, carry):
            q = around(i)
            part = tiles.at[pl.ds(2 * (q - z * 16), 2)]
            remote(part, phase1.at[xy], sent.at[10], came.at[10], {"seq": q}).start()
            return carry

        lax.fori_loop(1, 16, send, 0)

    def exchange():
        first15 = phase1.at[pl.ds(0, 15)]
        remote(first15, first15, sent.at[10], came.at[10], {"seq": me}).wait()
        sum1[...] = jnp.sum(phase1[...], axis=0)
        mine = phase2.at[z * 2 + core]
        phase2[z * 2 + core] = sum1[...]
        for dz in (2, 1, 3, 0):
            for dc in (0, 1):
                if dz or dc:
                    to = {"seq": lax.rem(z + dz, 4) * 16 + xy, "dp": lax.rem(core + dc, 2)}
                    remote(sum1, mine, sent.at[11], came.at[11], to).start()

    def gather():
        first7 = phase2.at[pl.ds(0, 7)]
        remote(first7, first7, sent.at[11], came.at[11], {"seq": me}).wait()
        sum2[...] = jnp.sum(phase2[...], axis=0)
        phase3[xy] = sum2[...]

        def send(i, carry):
            remote(sum2, phase3.at[xy], sent.at[12], came.at[12], {"seq": around(i)}).start()
            return carry

        lax.fori_loop(1, 16, send, 0)

    def tap_sums(features):
        def body(b, carry):
            cols = lanes(b)
            for i in features:
                sums = []
                for j in range(RIM + 1):
                    both = ahead[i, 0, :ROWS, cols] * ext[i, 0, 8 - j : 8 - j + ROWS, cols]
                    both = both + ahead[i, 1, :ROWS, cols] * ext[i, 1, 8 - j : 8 - j + ROWS, cols]
                    sums.append(jnp.sum(both, axis=0, keepdims=True))
                sums.append(jnp.zeros((1, LANES), FLOAT))
                tiles[i * 8 + b] = jnp.concatenate(sums, axis=0)
            return carry

        lax.fori_loop(0, blocks, body, 0)

    def raws(i):
        def body(b, carry):
            cols = lanes(b)
            for w in range(2):
                total = taps_ref[i, 0:1, cols] * ahead[i, w, :ROWS, cols]
                for j in range(1, RIM + 1):
                    total = total + taps_ref[i, j : j + 1, cols] * ahead[i, w, j : j + ROWS, cols]
                raw_ref[i, w, :, cols] = total
            return carry

        lax.fori_loop(0, blocks, body, 0)
        save = pltpu.make_async_copy(raw_ref.at[i], raw_hbm.at[i], saves.at[1 + i])
        save.start()
        return save

    peers_done(home, 3).wait_recv()

    def mix(b, carry):
        cols = lanes(b)
        conv = home[lanes(b), :].T
        for w in range(2):
            part = conv[w * ROWS : (w + 1) * ROWS]
            mixed_ref[w, :, cols] = feat[0, w, :, cols] * part
            ahead[0, w, :ROWS, cols] = cot_ref[w, :, cols] * part
        return carry

    lax.fori_loop(0, blocks, mix, 0)
    packed(edge_q, ahead, (0,), 0)
    after_q = remote(edge_q, after_q_rows, sent.at[9], came.at[9], {"seq": previous})
    after_q.start()
    save_mixed = pltpu.make_async_copy(mixed_ref, mixed_hbm, saves.at[0])
    save_mixed.start()
    tap_sums((0,))

    outs_part = outs.at[:, pl.ds(0, 15)]
    remote(outs_part, outs_part, sent.at[8], came.at[8], {"seq": me}).wait()
    windows = 4
    tail = 1.0 / math.sqrt(windows * SEQ)
    scale = 4.0 / math.sqrt(windows * SEQ * blocks * LANES * 4)
    for b in range(blocks):
        rows = []
        for s in range(8 * b, 8 * b + 8):
            tile = outs[s // 16, s % 16]
            rows += [tile, pltpu.roll(tile, ROWS, 1)]
        square = jnp.concatenate(rows, axis=0).T
        out_ref[:, b * LANES : (b + 1) * LANES] = square[:ROWS] * tail

    peers_done(home, 4).wait_recv()

    def unmix(b, carry):
        cols = lanes(b)
        back = home[pl.ds(pl.multiple_of(AREA + b * LANES, LANES), LANES), :].T
        for w in range(2):
            part = back[w * ROWS : (w + 1) * ROWS]
            ahead[1, w, :ROWS, cols] = part * feat[2, w, :, cols]
            ahead[2, w, :ROWS, cols] = part * feat[1, w, :, cols]
        return carry

    lax.fori_loop(0, blocks, unmix, 0)
    packed(edge_kv, ahead, keys, 0)
    after_kv = remote(edge_kv, after_kv_rows, sent.at[14], came.at[14], {"seq": previous})
    after_kv.start()
    tap_sums(keys)
    scatter()
    after_q.wait()
    unpacked(after_q_rows, ahead, (0,), ROWS)
    no_rows(ahead, (0,), ROWS, ROWS - 1)
    save_q = raws(0)
    exchange()
    after_kv.wait()
    unpacked(after_kv_rows, ahead, keys, ROWS)
    no_rows(ahead, keys, ROWS, ROWS - 1)
    save_k = raws(1)
    save_v = raws(2)
    gather()
    for sem in (1, 2):
        peers_done(sends, sem).wait_send()
    for sem in (3, 4):
        peers_done(backs, sem).wait_send()
    for save in (save_mixed, save_q, save_k, save_v):
        save.wait()
    last15 = phase3.at[pl.ds(0, 15)]
    remote(last15, last15, sent.at[12], came.at[12], {"seq": me}).wait()
    for i in range(3):
        for b in range(blocks):
            t = i * 8 + b
            short_ref[i, :, b * LANES : (b + 1) * LANES] = phase3[t // 2, t % 2][: RIM + 1] * tail
    net_sum = jnp.concatenate([phase3[t // 2, t % 2] for t in range(24, 30)], axis=0) * scale
    netf_ref[...] = net_sum[:32, :ROWS]
    nets_ref[:16, :] = net_sum[32:, :ROWS]
    nets_ref[16:, :] = net_sum[:, ROWS:]


def land_kernel(*refs):
    count = (len(refs) - 2) // 3
    sources, targets, held = refs[:count], refs[count : 2 * count], refs[2 * count : 3 * count]
    loads, stores = refs[3 * count :]
    pieces = []
    for n, source in enumerate(sources):
        lead = source.shape[:-2]
        pieces += [(n, at) for at in np.ndindex(*lead)] if source.shape[-2] == ROWS else [(n, ())]

    def part(ref, at):
        return ref.at[at] if at else ref

    first = [
        pltpu.make_async_copy(part(sources[n], at), part(held[n], at), loads.at[k])
        for k, (n, at) in enumerate(pieces)
    ]
    second = [
        pltpu.make_async_copy(part(held[n], at), part(targets[n], at), stores.at[k])
        for k, (n, at) in enumerate(pieces)
    ]
    for copy in first:
        copy.start()
    for load, store in zip(first, second):
        load.wait()
        store.start()
    for copy in second:
        copy.wait()


def shards(projected, short_weight, decay_rates, w1, w2, out_weight, cotangent):
    first_stack, last_stack, turn, middle, embedded = tables()
    vmem = pl.BlockSpec(memory_space=pltpu.VMEM)
    hbm = pl.BlockSpec(memory_space=pl.ANY)
    group = projected.shape[3]
    hidden = w2.shape[0]

    def buffer(*shape):
        return pltpu.VMEM(shape, FLOAT)

    def held(value):
        return buffer(*value.shape)

    def like(value):
        return jax.ShapeDtypeStruct(value.shape, FLOAT)

    rows = projected.shape[2] + 8
    results = pl.pallas_call(
        whole_kernel,
        out_shape=(
            like(cotangent),
            like(projected),
            like(short_weight),
            like(out_weight),
            like(w1),
            like(w2),
        ),
        in_specs=[pl.BlockSpec(memory_space=pltpu.SMEM)] + [hbm] * 11,
        out_specs=(hbm, hbm) + (vmem,) * 4,
        scratch_shapes=[
            held(short_weight),
            held(cotangent),
            buffer(w1.shape[0], SEQ),
            held(w1),
            held(w2),
            held(out_weight),
            held(first_stack),
            held(last_stack),
            held(turn),
            held(middle),
            pltpu.VMEM(first_stack.shape, HALF),
            pltpu.VMEM(last_stack.shape, HALF),
            pltpu.VMEM(middle.shape, HALF),
            held(cotangent),
            held(projected),
            buffer(3, 2, rows, group),
            buffer(3, 2, rows, group),
            buffer(3, 2, ROWS, group),
            buffer(2 * AREA, LANES),
            buffer(2 * AREA, LANES),
            buffer(2 * AREA, LANES),
            buffer(2 * AREA, LANES),
            buffer(hidden, SEQ),
            buffer(hidden, SEQ),
            buffer(hidden, SEQ),
            buffer(hidden, SEQ),
            buffer(AREA, LANES),
            buffer(AREA, 2 * LANES),
            buffer(AREA, 2 * LANES),
            buffer(AREA, 2 * LANES),
            buffer(8, LANES),
            buffer(8, LANES),
            buffer(4, 48, LANES),
            buffer(4, 16, 8, LANES),
            buffer(32, 8, LANES),
            buffer(16, 2, 8, LANES),
            buffer(2, 8, LANES),
            buffer(8, 2, 8, LANES),
            buffer(2, 8, LANES),
            buffer(16, 2, 8, LANES),
            buffer(OWN, hidden),
            buffer(96, hidden),
            buffer(24, group),
            buffer(24, group),
            buffer(24, group),
            buffer(24, group),
            buffer(16, group),
            buffer(16, group),
            buffer(16, group),
            pltpu.SemaphoreType.DMA((11,)),
            pltpu.SemaphoreType.DMA((4,)),
            pltpu.SemaphoreType.DMA((18,)),
            pltpu.SemaphoreType.DMA((18,)),
        ],
        compiler_params=pltpu.CompilerParams(
            collective_id=1, has_side_effects=True, vmem_limit_bytes=60 << 20
        ),
        name="whole",
    )(
        decay_rates,
        projected,
        short_weight,
        cotangent,
        jnp.asarray(embedded),
        w1,
        w2,
        out_weight,
        jnp.asarray(first_stack),
        jnp.asarray(last_stack),
        jnp.asarray(turn),
        jnp.asarray(middle),
    )
    return pl.pallas_call(
        land_kernel,
        out_shape=tuple(like(v) for v in results),
        in_specs=[hbm] * len(results),
        out_specs=(hbm,) * len(results),
        scratch_shapes=[held(v) for v in results]
        + [pltpu.SemaphoreType.DMA((16,)), pltpu.SemaphoreType.DMA((16,))],
        compiler_params=pltpu.CompilerParams(vmem_limit_bytes=60 << 20),
        name="land",
    )(*results)


def solution(mesh):
    return jax.shard_map(
        shards,
        mesh=mesh,
        in_specs=(
            P(None, "dp", "seq", "chan"),
            P(None, None, "chan"),
            P("chan"),
            P(),
            P(),
            P(None, "chan"),
            P("dp", "seq", "chan"),
        ),
        out_specs=(
            P("dp", "seq", "chan"),
            P(None, "dp", "seq", "chan"),
            P(None, None, "chan"),
            P(None, "chan"),
            P(),
            P(),
        ),
        check_vma=False,
    )
```

```python
import functools
import math

import jax
import jax.numpy as jnp
import ml_dtypes
import numpy as np
from jax import lax
from jax.experimental import pallas as pl
from jax.experimental.pallas import tpu as pltpu
from jax.sharding import PartitionSpec as P

MESH = pl.DeviceIdType.MESH
ROWS = 64
OWN = 16
LANES = 128
SEQ = ROWS * ROWS
RIM = 6
STEP = 512
FLOAT = jnp.float32
HALF = jnp.bfloat16


def halves(table):
    high = table.astype(ml_dtypes.bfloat16)
    low = (table - high.astype(np.float64)).astype(ml_dtypes.bfloat16)
    return high, low


@functools.cache
def tables():
    k = np.arange(ROWS)[:, None] + 0.25
    s = np.arange(ROWS)[None, :]
    theta = 2 * np.pi * k * s / ROWS
    first = np.concatenate([np.cos(theta), -np.sin(theta)], axis=0)
    high, low = halves(first)
    first_stack = np.concatenate([high, high, low], axis=1)
    last = np.concatenate([np.cos(theta).T, -np.sin(theta).T], axis=1) / SEQ
    high, low = halves(last)
    last_stack = np.concatenate([high, high, low], axis=1)
    phi = 2 * np.pi * k * s / SEQ
    turn = np.stack([np.tile(np.cos(phi), (1, 2)), np.tile(np.sin(phi), (1, 2))]).astype(np.float32)
    inner = 2 * np.pi * (np.arange(ROWS)[:, None] * s % ROWS) / ROWS
    cos, sin = np.kron(np.eye(2), np.cos(inner)), np.kron(np.eye(2), np.sin(inner))
    there = np.block([[cos, -sin], [sin, cos]])
    back = np.block([[cos, sin], [-sin, cos]])
    middle = np.stack(halves(there) + halves(back))
    half = 16
    orders = np.arange(half, dtype=np.int64)
    factors = 1 + (SEQ // 2 - 2) * orders * orders // max((half - 1) ** 2, 1)
    angle = 2 * np.pi * (factors[:, None] * np.arange(SEQ)[None, :] % SEQ) / SEQ
    embedded = np.concatenate([np.cos(angle), np.sin(angle)], axis=0).astype(np.float32)
    return (*(t.astype(np.float32) for t in (first_stack, last_stack)), turn, middle.astype(np.float32), embedded)


def split(value):
    high = value.astype(HALF)
    return high, (value - high.astype(FLOAT)).astype(HALF)


def dot(a, b, kind="nn"):
    dims = {"nn": ((1,), (0,)), "nt": ((1,), (1,))}[kind]
    return lax.dot_general(a, b, (dims, ((), ())), preferred_element_type=FLOAT)


def dot3(a, b, kind="nn"):
    ah, al = split(a)
    bh, bl = split(b)
    return dot(ah, bh, kind) + (dot(ah, bl, kind) + dot(al, bh, kind))


def sin_cos(x):
    n = jnp.floor(x * (2.0 / math.pi) + 0.5)
    r = x - n * 1.5703125
    r = r - n * 4.837512969970703125e-4
    r = r - n * 7.549789948768648e-8
    z = r * r
    s = r + r * z * (-1.6666654611e-1 + z * (8.3321608736e-3 + z * -1.9515295891e-4))
    c = 1.0 - 0.5 * z + z * z * (4.166664568298827e-2 + z * (-1.388731625493765e-3 + z * 2.443315711809948e-5))
    q = n.astype(jnp.int32)
    odd = (q & 1) == 1
    sin = jnp.where(odd, c, s)
    cos = jnp.where(odd, s, c)
    sin = jnp.where((q & 2) == 2, -sin, sin)
    cos = jnp.where(((q + 1) & 2) == 2, -cos, cos)
    return sin, cos


def columns(parts):
    return jnp.concatenate(parts, axis=1)


def forward(signals, first, turn, middle):
    cos, sin = turn[0], turn[1]
    high, low = split(columns(signals))
    spec = dot(first[...], jnp.concatenate([high, low, high], axis=0))
    rows = []
    for i in range(len(signals)):
        re = spec[:ROWS, i * LANES : (i + 1) * LANES]
        im = spec[ROWS:, i * LANES : (i + 1) * LANES]
        rows.append(columns([re * cos + im * sin, im * cos - re * sin]))
    high, low = split(jnp.concatenate(rows, axis=0))
    return dot(high, middle[0]) + (dot(low, middle[0]) + dot(high, middle[1]))


def inverse(rows, last, turn, middle):
    cos, sin = turn[0], turn[1]
    high, low = split(jnp.concatenate(rows, axis=0))
    freq = dot(high, middle[2]) + (dot(low, middle[2]) + dot(high, middle[3]))
    cols = []
    for i in range(len(rows)):
        re = freq[i * ROWS : (i + 1) * ROWS, :LANES]
        im = freq[i * ROWS : (i + 1) * ROWS, LANES:]
        cols.append(jnp.concatenate([re * cos - im * sin, re * sin + im * cos], axis=0))
    high, low = split(columns(cols))
    return dot(last[...], jnp.concatenate([high, low, high], axis=0))


def times(a, b):
    ar, ai, br, bi = a[:, :LANES], a[:, LANES:], b[:, :LANES], b[:, LANES:]
    return columns([ar * br - ai * bi, ar * bi + ai * br])


def times_conj(a, b):
    ar, ai, br, bi = a[:, :LANES], a[:, LANES:], b[:, :LANES], b[:, LANES:]
    return columns([ar * br + ai * bi, ar * bi - ai * br])


def flipped(small):
    rows, cols = small.shape
    tall = jnp.concatenate([small, jnp.zeros((LANES - rows, cols), FLOAT)], axis=0)
    square = columns([tall, jnp.zeros((LANES, LANES - cols), FLOAT)]) if cols < LANES else tall
    return square.T


def remote(src, dst, send_sem, recv_sem, device):
    return pltpu.make_async_remote_copy(
        src_ref=src,
        dst_ref=dst,
        send_sem=send_sem,
        recv_sem=recv_sem,
        device_id=device,
        device_id_type=MESH,
    )


GROUP = 4
AREA = ROWS * OWN


def whole_kernel(
    rates_ref,
    proj_hbm,
    taps_hbm,
    cot_hbm,
    emb_hbm,
    w1_hbm,
    w2_hbm,
    wo_hbm,
    first_hbm,
    last_hbm,
    turn_hbm,
    middle_hbm,
    mixed_hbm,
    raw_hbm,
    short_ref,
    out_ref,
    netf_ref,
    nets_ref,
    taps_ref,
    cot_ref,
    emb_ref,
    w1_ref,
    w2_ref,
    wo_ref,
    first_wide,
    last_wide,
    turn_ref,
    middle_wide,
    first_ref,
    last_ref,
    middle_ref,
    mixed_ref,
    raw_ref,
    ext,
    ahead,
    feat,
    sends,
    got,
    backs,
    home,
    act1,
    cos1,
    act2,
    cos2,
    filt,
    fspec,
    pspec,
    gspec,
    out_mine,
    out_dp,
    by_chan,
    outs,
    tiles,
    phase1,
    sum1,
    phase2,
    sum2,
    phase3,
    acc_out,
    acc_net,
    edge_kv,
    rim_kv,
    relay,
    after_kv_rows,
    edge_q,
    rim_q,
    after_q_rows,
    loads,
    saves,
    sent,
    came,
):
    me = lax.axis_index("seq")
    chan = lax.axis_index("chan")
    core = lax.axis_index("dp")
    z, xy = me // 16, lax.rem(me, 16)
    x, y = xy // 4, lax.rem(xy, 4)
    following, previous = lax.rem(me + 1, ROWS), lax.rem(me + ROWS - 1, ROWS)
    blocks = feat.shape[3] // LANES
    barrier = pltpu.get_barrier_semaphore()

    def signal(sem, **device):
        pl.semaphore_signal(sem, inc=1, device_id=device, device_id_type=MESH)

    for dz in (2, 1, 3, 0):
        plane = lax.rem(z + dz, 4) * 16

        def greet(i, carry):
            signal(barrier, seq=plane + lax.rem(xy + i, 16))
            return carry

        lax.fori_loop(0 if dz else 1, 16, greet, 0)
        signal(barrier, seq=plane + xy, dp=1 - core)
    for d in range(1, 4):
        signal(barrier, chan=lax.rem(chan + d, 4))

    pairs = [
        (proj_hbm, ext.at[:, :, pl.ds(8, ROWS), :]),
        (taps_hbm, taps_ref),
        (cot_hbm, cot_ref),
        (emb_hbm, emb_ref),
        (w1_hbm, w1_ref),
        (w2_hbm, w2_ref),
        (wo_hbm, wo_ref),
        (first_hbm, first_wide),
        (last_hbm, last_wide),
        (turn_hbm, turn_ref),
        (middle_hbm, middle_wide),
    ]
    copies = [pltpu.make_async_copy(src, dst, loads.at[i]) for i, (src, dst) in enumerate(pairs)]
    for copy in copies:
        copy.start()
    copies[0].wait()
    copies[1].wait()

    def lanes(b):
        return pl.ds(pl.multiple_of(b * LANES, LANES), LANES)

    def tapped(i, w, cols, start, count):
        total = taps_ref[i, 0:1, cols] * ext[i, w, 8 + start : 8 + start + count, cols]
        for j in range(1, RIM + 1):
            rows = slice(8 + start - j, 8 + start - j + count)
            total = total + taps_ref[i, j : j + 1, cols] * ext[i, w, rows, cols]
        feat[i, w, start : start + count, cols] = total

    def later_rows(group):
        def body(b, carry):
            for i in group:
                for w in range(2):
                    tapped(i, w, lanes(b), 8, ROWS - 8)
            return carry

        lax.fori_loop(0, blocks, body, 0)

    def to_peers(source, target, signal_at, sem):
        base = signal_at * AREA
        mine = pl.ds(pl.multiple_of(base + me * OWN, OWN), OWN)
        target[mine, :] = source[mine, :]

        def send(i, carry):
            i = lax.rem(i - 1 + 31 * core + 5 * xy + 17 * chan, ROWS - 1) + 1
            px, py = lax.rem(x + lax.rem(i // 4, 4), 4), lax.rem(y + i // 16, 4)
            peer = lax.rem(z + lax.rem(i, 4), 4) * 16 + px * 4 + py
            block = pl.ds(pl.multiple_of(base + peer * OWN, OWN), OWN)
            remote(source.at[block], target.at[mine], sent.at[sem], came.at[sem], {"seq": peer}).start()
            return carry

        lax.fori_loop(1, ROWS, send, 0)

    def peers_done(ref, sem):
        part = ref.at[pl.ds(0, AREA - OWN)]
        return remote(part, part, sent.at[sem], came.at[sem], {"seq": me})

    def pack(buffer, features, row):
        for n, (i, w) in enumerate((i, w) for i in features for w in range(2)):
            yield n * RIM, buffer.at[i, w, pl.ds(row, RIM), :]

    def packed(target, buffer, features, row):
        for at, part in pack(buffer, features, row):
            target[at : at + RIM, :] = part[...]

    def unpacked(source, buffer, features, row):
        for at, part in pack(buffer, features, row):
            part[...] = source[at : at + RIM, :]

    def no_rows(buffer, features, row, where):
        @pl.when(me == where)
        def _():
            for i in features:
                buffer[i, :, row : row + 8, :] = jnp.zeros((2, 8, buffer.shape[3]), FLOAT)

    keys = (1, 2)
    edge_q[8:, :] = jnp.zeros((8, edge_q.shape[1]), FLOAT)
    packed(edge_kv, ext, keys, ROWS + 8 - RIM)
    packed(edge_q, ext, (0,), ROWS + 8 - RIM)
    later_rows(keys)
    later_rows((0,))
    pl.semaphore_wait(barrier, ROWS - 1 + 7)

    quarter = edge_kv.shape[1] // 4
    ahead_plane = lax.rem(z + 1, 4) * 16

    def piece(ref, c):
        return ref.at[:, c * quarter : (c + 1) * quarter]

    @pl.when(xy != 15)
    def _():
        remote(edge_kv, rim_kv, sent.at[0], came.at[0], {"seq": following}).start()

    @pl.when(xy == 15)
    def _():
        for c, via in enumerate((3, 12, 0)):
            to = {"seq": z * 16 + via}
            remote(piece(edge_kv, c), piece(relay, c), sent.at[0], came.at[16], to).start()
        remote(piece(edge_kv, 3), piece(rim_kv, 3), sent.at[0], came.at[0], {"seq": following}).start()

    for c, via in enumerate((3, 12, 0)):

        @pl.when(xy == via)
        def _(c=c):
            part = piece(relay, c)
            remote(part, part, sent.at[16], came.at[16], {"seq": me}).wait_recv()
            on = remote(part, piece(rim_kv, c), sent.at[16], came.at[0], {"seq": ahead_plane})
            on.start()
            on.wait_send()

    remote(rim_kv, rim_kv, sent.at[0], came.at[0], {"seq": me}).wait()
    to_q = remote(edge_q, rim_q, sent.at[13], came.at[13], {"seq": following})
    to_q.start()
    unpacked(rim_kv, ext, keys, 8 - RIM)
    no_rows(ext, keys, 0, 0)

    def products(b, carry):
        cols = lanes(b)
        for i in (1, 2):
            for w in range(2):
                tapped(i, w, cols, 0, 8)
        parts = [feat[1, w, :, cols] * feat[2, w, :, cols] for w in range(2)]
        sends[lanes(b), :] = jnp.concatenate(parts, axis=0).T
        return carry

    lax.fori_loop(0, blocks, products, 0)
    to_peers(sends, got, 0, 1)
    to_q.wait()
    unpacked(rim_q, ext, (0,), 8 - RIM)
    no_rows(ext, (0,), 0, 0)
    copies[2].wait()

    def gradients(b, carry):
        cols = lanes(b)
        for w in range(2):
            tapped(0, w, cols, 0, 8)
        parts = [feat[0, w, :, cols] * cot_ref[w, :, cols] for w in range(2)]
        rows = pl.ds(pl.multiple_of(AREA + b * LANES, LANES), LANES)
        sends[rows, :] = jnp.concatenate(parts, axis=0).T
        return carry

    lax.fori_loop(0, blocks, gradients, 0)
    for copy in copies[3:]:
        copy.wait()
    first_ref[...] = first_wide[...].astype(HALF)
    last_ref[...] = last_wide[...].astype(HALF)
    middle_ref[...] = middle_wide[...].astype(HALF)

    turned = pltpu.roll(
        wo_ref[:, lanes(me // 8)], lax.rem(LANES - lax.rem(me, 8) * OWN, LANES), 1
    )
    wo_own = turned[:, :OWN]
    wo_t = flipped(turned)[:OWN, :ROWS]
    w1_t = flipped(w1_ref[...])[:ROWS, : w1_ref.shape[0]]
    w2_t = flipped(w2_ref[...])[:ROWS, :ROWS]
    lane = lax.broadcasted_iota(jnp.int32, (OWN, LANES), 1)
    low_half = lane < ROWS

    def net(step, carry):
        cols = pl.ds(pl.multiple_of(step * STEP, STEP), STEP)
        s1, c1 = sin_cos(dot3(w1_t, emb_ref[:, cols]))
        act1[:, cols] = s1
        cos1[:, cols] = c1
        s2, c2 = sin_cos(dot3(w2_t, s1))
        act2[:, cols] = s2
        cos2[:, cols] = c2
        raw = dot3(wo_t, s2)
        for pair in range(STEP // LANES):
            both = raw[:, pair * LANES : (pair + 1) * LANES]
            other = pltpu.roll(both, ROWS, 1)
            base = pl.multiple_of((step * (STEP // ROWS) + 2 * pair) * OWN, OWN)
            filt[pl.ds(base, OWN), :] = jnp.where(low_half, both, other)
            filt[pl.ds(base + OWN, OWN), :] = jnp.where(low_half, other, both)
        return carry

    lax.fori_loop(0, SEQ // STEP, net, 0)

    place = lax.broadcasted_iota(jnp.int32, (ROWS, LANES), 0) * ROWS + (
        lax.broadcasted_iota(jnp.int32, (ROWS, LANES), 1) & (ROWS - 1)
    )
    place = place.astype(FLOAT)

    def envelope(ch):
        rate = rates_ref[me * OWN + ch]
        return jnp.exp(place * -rate) * jnp.sqrt(jnp.full((1, LANES), 2.0 * rate + 1.0 / SEQ, FLOAT))

    def strided(ref, base, ch):
        return ref[pl.ds(base + ch, ROWS, stride=OWN), :]

    def group_rows(step):
        return pl.ds(pl.multiple_of(step * GROUP * ROWS, GROUP * ROWS), GROUP * ROWS)

    def cut(value):
        return [value[i * ROWS : (i + 1) * ROWS] for i in range(GROUP)]

    def filters(step, carry):
        chans = [step * GROUP + i for i in range(GROUP)]
        signals = [strided(filt, 0, ch) * envelope(ch) for ch in chans]
        fspec[group_rows(step), :] = forward(signals, first_ref, turn_ref, middle_ref)
        return carry

    lax.fori_loop(0, OWN // GROUP, filters, 0)
    to_peers(sends, got, 1, 2)

    def put(value, base, step):
        for i in range(GROUP):
            backs[pl.ds(base + step * GROUP + i, ROWS, stride=OWN), :] = value[
                :, i * LANES : (i + 1) * LANES
            ]

    peers_done(got, 1).wait_recv()

    def convolve(step, carry):
        signals = [strided(got, 0, step * GROUP + i) for i in range(GROUP)]
        spec = forward(signals, first_ref, turn_ref, middle_ref)
        pspec[group_rows(step), :] = spec
        rows = cut(times(spec, fspec[group_rows(step), :]))
        put(inverse(rows, last_ref, turn_ref, middle_ref), 0, step)
        return carry

    lax.fori_loop(0, OWN // GROUP, convolve, 0)
    to_peers(backs, home, 0, 3)
    peers_done(got, 2).wait_recv()

    def correlate(step, carry):
        signals = [strided(got, AREA, step * GROUP + i) for i in range(GROUP)]
        spec = forward(signals, first_ref, turn_ref, middle_ref)
        rows = cut(times_conj(fspec[group_rows(step), :], spec))
        put(inverse(rows, last_ref, turn_ref, middle_ref), AREA, step)
        gspec[group_rows(step), :] = spec
        return carry

    lax.fori_loop(0, OWN // GROUP, correlate, 0)
    to_peers(backs, home, 1, 4)

    def filter_back(step, carry):
        pair = times_conj(pspec[group_rows(step), :], gspec[group_rows(step), :])
        re, im = pair[:, :LANES], pair[:, LANES:]
        rows = cut(columns([re + pltpu.roll(re, ROWS, 1), im + pltpu.roll(im, ROWS, 1)]))
        value = inverse(rows, last_ref, turn_ref, middle_ref)
        for i in range(GROUP):
            ch = step * GROUP + i
            filt[pl.ds(ch, ROWS, stride=OWN), :] = value[:, i * LANES : (i + 1) * LANES] * envelope(ch)
        return carry

    lax.fori_loop(0, OWN // GROUP, filter_back, 0)
    acc_out[...] = jnp.zeros_like(acc_out)
    acc_net[...] = jnp.zeros_like(acc_net)

    def net_back(step, carry):
        cols = pl.ds(pl.multiple_of(step * STEP, STEP), STEP)
        parts = []
        for pair in range(STEP // LANES):
            base = pl.multiple_of((step * (STEP // ROWS) + 2 * pair) * OWN, OWN)
            parts.append(jnp.where(low_half, filt[pl.ds(base, OWN), :], filt[pl.ds(base + OWN, OWN), :]))
        kgrad = columns(parts)
        acc_out[...] += dot3(kgrad, act2[:, cols], "nt")
        pre2 = dot3(wo_own, kgrad) * cos2[:, cols]
        acc_net[32:, :] += dot3(act1[:, cols], pre2, "nt")
        pre1 = dot3(w2_ref[...], pre2) * cos1[:, cols]
        acc_net[:32, :] += dot3(emb_ref[:, cols], pre1, "nt")
        return carry

    lax.fori_loop(0, SEQ // STEP, net_back, 0)
    out_mine[...] = columns([acc_out[:8, :], acc_out[8:, :]])
    by_chan[chan] = columns([acc_net[:48, :], acc_net[48:, :]])
    swap = remote(out_mine, out_dp, sent.at[5], came.at[5], {"dp": 1 - core})
    swap.start()
    for d in range(1, 4):
        part = by_chan.at[chan]
        remote(part, part, sent.at[6], came.at[6], {"chan": lax.rem(chan + d, 4)}).start()
    swap.wait()
    outs[z, xy] = out_mine[...] + out_dp[...]
    for d in range(1, 4):
        part = outs.at[z, xy]
        remote(part, part, sent.at[7], came.at[7], {"seq": lax.rem(z + d, 4) * 16 + xy}).start()
    chans_done = remote(by_chan.at[pl.ds(0, 3)], by_chan.at[pl.ds(0, 3)], sent.at[6], came.at[6], {"seq": me})
    zs_done = remote(outs.at[pl.ds(0, 3), 0], outs.at[pl.ds(0, 3), 0], sent.at[7], came.at[7], {"seq": me})
    zs_done.wait()

    def around(i):
        return z * 16 + lax.rem(x + i // 4, 4) * 4 + lax.rem(y + lax.rem(i, 4), 4)

    def spread_outs(i, carry):
        column = outs.at[:, xy]
        remote(column, column, sent.at[8], came.at[8], {"seq": around(i)}).start()
        return carry

    lax.fori_loop(1, 16, spread_outs, 0)
    chans_done.wait()
    net_sum = (by_chan[0] + by_chan[1]) + (by_chan[2] + by_chan[3])
    for i in range(6):
        tiles[24 + i] = net_sum[i * 8 : (i + 1) * 8]
    tiles[30] = jnp.zeros((8, LANES), FLOAT)
    tiles[31] = jnp.zeros((8, LANES), FLOAT)

    def scatter():
        phase1[xy] = tiles[pl.ds(2 * xy, 2)]

        def send(i, carry):
            q = around(i)
            part = tiles.at[pl.ds(2 * (q - z * 16), 2)]
            remote(part, phase1.at[xy], sent.at[10], came.at[10], {"seq": q}).start()
            return carry

        lax.fori_loop(1, 16, send, 0)

    def exchange():
        first15 = phase1.at[pl.ds(0, 15)]
        remote(first15, first15, sent.at[10], came.at[10], {"seq": me}).wait()
        sum1[...] = jnp.sum(phase1[...], axis=0)
        mine = phase2.at[z * 2 + core]
        phase2[z * 2 + core] = sum1[...]
        for dz in (2, 1, 3, 0):
            for dc in (0, 1):
                if dz or dc:
                    to = {"seq": lax.rem(z + dz, 4) * 16 + xy, "dp": lax.rem(core + dc, 2)}
                    remote(sum1, mine, sent.at[11], came.at[11], to).start()

    def gather():
        first7 = phase2.at[pl.ds(0, 7)]
        remote(first7, first7, sent.at[11], came.at[11], {"seq": me}).wait()
        sum2[...] = jnp.sum(phase2[...], axis=0)
        phase3[xy] = sum2[...]

        def send(i, carry):
            remote(sum2, phase3.at[xy], sent.at[12], came.at[12], {"seq": around(i)}).start()
            return carry

        lax.fori_loop(1, 16, send, 0)

    def tap_sums(features):
        def body(b, carry):
            cols = lanes(b)
            for i in features:
                sums = []
                for j in range(RIM + 1):
                    both = ahead[i, 0, :ROWS, cols] * ext[i, 0, 8 - j : 8 - j + ROWS, cols]
                    both = both + ahead[i, 1, :ROWS, cols] * ext[i, 1, 8 - j : 8 - j + ROWS, cols]
                    sums.append(jnp.sum(both, axis=0, keepdims=True))
                sums.append(jnp.zeros((1, LANES), FLOAT))
                tiles[i * 8 + b] = jnp.concatenate(sums, axis=0)
            return carry

        lax.fori_loop(0, blocks, body, 0)

    def raws(i):
        def body(b, carry):
            cols = lanes(b)
            for w in range(2):
                total = taps_ref[i, 0:1, cols] * ahead[i, w, :ROWS, cols]
                for j in range(1, RIM + 1):
                    total = total + taps_ref[i, j : j + 1, cols] * ahead[i, w, j : j + ROWS, cols]
                raw_ref[i, w, :, cols] = total
            return carry

        lax.fori_loop(0, blocks, body, 0)
        save = pltpu.make_async_copy(raw_ref.at[i], raw_hbm.at[i], saves.at[1 + i])
        save.start()
        return save

    peers_done(home, 3).wait_recv()

    def mix(b, carry):
        cols = lanes(b)
        conv = home[lanes(b), :].T
        for w in range(2):
            part = conv[w * ROWS : (w + 1) * ROWS]
            mixed_ref[w, :, cols] = feat[0, w, :, cols] * part
            ahead[0, w, :ROWS, cols] = cot_ref[w, :, cols] * part
        return carry

    lax.fori_loop(0, blocks, mix, 0)
    packed(edge_q, ahead, (0,), 0)
    after_q = remote(edge_q, after_q_rows, sent.at[9], came.at[9], {"seq": previous})
    after_q.start()
    save_mixed = pltpu.make_async_copy(mixed_ref, mixed_hbm, saves.at[0])
    save_mixed.start()
    tap_sums((0,))

    outs_part = outs.at[:, pl.ds(0, 15)]
    remote(outs_part, outs_part, sent.at[8], came.at[8], {"seq": me}).wait()
    windows = 4
    tail = 1.0 / math.sqrt(windows * SEQ)
    scale = 4.0 / math.sqrt(windows * SEQ * blocks * LANES * 4)
    for b in range(blocks):
        rows = []
        for s in range(8 * b, 8 * b + 8):
            tile = outs[s // 16, s % 16]
            rows += [tile, pltpu.roll(tile, ROWS, 1)]
        square = jnp.concatenate(rows, axis=0).T
        out_ref[:, b * LANES : (b + 1) * LANES] = square[:ROWS] * tail

    peers_done(home, 4).wait_recv()

    def unmix(b, carry):
        cols = lanes(b)
        back = home[pl.ds(pl.multiple_of(AREA + b * LANES, LANES), LANES), :].T
        for w in range(2):
            part = back[w * ROWS : (w + 1) * ROWS]
            ahead[1, w, :ROWS, cols] = part * feat[2, w, :, cols]
            ahead[2, w, :ROWS, cols] = part * feat[1, w, :, cols]
        return carry

    lax.fori_loop(0, blocks, unmix, 0)
    packed(edge_kv, ahead, keys, 0)
    after_kv = remote(edge_kv, after_kv_rows, sent.at[14], came.at[14], {"seq": previous})
    after_kv.start()
    tap_sums(keys)
    scatter()
    after_q.wait()
    unpacked(after_q_rows, ahead, (0,), ROWS)
    no_rows(ahead, (0,), ROWS, ROWS - 1)
    save_q = raws(0)
    exchange()
    after_kv.wait()
    unpacked(after_kv_rows, ahead, keys, ROWS)
    no_rows(ahead, keys, ROWS, ROWS - 1)
    save_k = raws(1)
    save_v = raws(2)
    gather()
    for sem in (1, 2):
        peers_done(sends, sem).wait_send()
    for sem in (3, 4):
        peers_done(backs, sem).wait_send()
    for save in (save_mixed, save_q, save_k, save_v):
        save.wait()
    last15 = phase3.at[pl.ds(0, 15)]
    remote(last15, last15, sent.at[12], came.at[12], {"seq": me}).wait()
    for i in range(3):
        for b in range(blocks):
            t = i * 8 + b
            short_ref[i, :, b * LANES : (b + 1) * LANES] = phase3[t // 2, t % 2][: RIM + 1] * tail
    net_sum = jnp.concatenate([phase3[t // 2, t % 2] for t in range(24, 30)], axis=0) * scale
    netf_ref[...] = net_sum[:32, :ROWS]
    nets_ref[:16, :] = net_sum[32:, :ROWS]
    nets_ref[16:, :] = net_sum[:, ROWS:]


def land_kernel(*refs):
    count = (len(refs) - 2) // 3
    sources, targets, held = refs[:count], refs[count : 2 * count], refs[2 * count : 3 * count]
    loads, stores = refs[3 * count :]
    pieces = []
    for n, source in enumerate(sources):
        lead = source.shape[:-2]
        pieces += [(n, at) for at in np.ndindex(*lead)] if source.shape[-2] == ROWS else [(n, ())]

    def part(ref, at):
        return ref.at[at] if at else ref

    first = [
        pltpu.make_async_copy(part(sources[n], at), part(held[n], at), loads.at[k])
        for k, (n, at) in enumerate(pieces)
    ]
    second = [
        pltpu.make_async_copy(part(held[n], at), part(targets[n], at), stores.at[k])
        for k, (n, at) in enumerate(pieces)
    ]
    for copy in first:
        copy.start()
    for load, store in zip(first, second):
        load.wait()
        store.start()
    for copy in second:
        copy.wait()


def shards(projected, short_weight, decay_rates, w1, w2, out_weight, cotangent):
    first_stack, last_stack, turn, middle, embedded = tables()
    vmem = pl.BlockSpec(memory_space=pltpu.VMEM)
    hbm = pl.BlockSpec(memory_space=pl.ANY)
    group = projected.shape[3]
    hidden = w2.shape[0]

    def buffer(*shape):
        return pltpu.VMEM(shape, FLOAT)

    def held(value):
        return buffer(*value.shape)

    def like(value):
        return jax.ShapeDtypeStruct(value.shape, FLOAT)

    rows = projected.shape[2] + 8
    results = pl.pallas_call(
        whole_kernel,
        out_shape=(
            like(cotangent),
            like(projected),
            like(short_weight),
            like(out_weight),
            like(w1),
            like(w2),
        ),
        in_specs=[pl.BlockSpec(memory_space=pltpu.SMEM)] + [hbm] * 11,
        out_specs=(hbm, hbm) + (vmem,) * 4,
        scratch_shapes=[
            held(short_weight),
            held(cotangent),
            buffer(w1.shape[0], SEQ),
            held(w1),
            held(w2),
            held(out_weight),
            held(first_stack),
            held(last_stack),
            held(turn),
            held(middle),
            pltpu.VMEM(first_stack.shape, HALF),
            pltpu.VMEM(last_stack.shape, HALF),
            pltpu.VMEM(middle.shape, HALF),
            held(cotangent),
            held(projected),
            buffer(3, 2, rows, group),
            buffer(3, 2, rows, group),
            buffer(3, 2, ROWS, group),
            buffer(2 * AREA, LANES),
            buffer(2 * AREA, LANES),
            buffer(2 * AREA, LANES),
            buffer(2 * AREA, LANES),
            buffer(hidden, SEQ),
            buffer(hidden, SEQ),
            buffer(hidden, SEQ),
            buffer(hidden, SEQ),
            buffer(AREA, LANES),
            buffer(AREA, 2 * LANES),
            buffer(AREA, 2 * LANES),
            buffer(AREA, 2 * LANES),
            buffer(8, LANES),
            buffer(8, LANES),
            buffer(4, 48, LANES),
            buffer(4, 16, 8, LANES),
            buffer(32, 8, LANES),
            buffer(16, 2, 8, LANES),
            buffer(2, 8, LANES),
            buffer(8, 2, 8, LANES),
            buffer(2, 8, LANES),
            buffer(16, 2, 8, LANES),
            buffer(OWN, hidden),
            buffer(96, hidden),
            buffer(24, group),
            buffer(24, group),
            buffer(24, group),
            buffer(24, group),
            buffer(16, group),
            buffer(16, group),
            buffer(16, group),
            pltpu.SemaphoreType.DMA((11,)),
            pltpu.SemaphoreType.DMA((4,)),
            pltpu.SemaphoreType.DMA((18,)),
            pltpu.SemaphoreType.DMA((18,)),
        ],
        compiler_params=pltpu.CompilerParams(
            collective_id=1, has_side_effects=True, vmem_limit_bytes=60 << 20
        ),
        name="whole",
    )(
        decay_rates,
        projected,
        short_weight,
        cotangent,
        jnp.asarray(embedded),
        w1,
        w2,
        out_weight,
        jnp.asarray(first_stack),
        jnp.asarray(last_stack),
        jnp.asarray(turn),
        jnp.asarray(middle),
    )
    return pl.pallas_call(
        land_kernel,
        out_shape=tuple(like(v) for v in results),
        in_specs=[hbm] * len(results),
        out_specs=(hbm,) * len(results),
        scratch_shapes=[held(v) for v in results]
        + [pltpu.SemaphoreType.DMA((16,)), pltpu.SemaphoreType.DMA((16,))],
        compiler_params=pltpu.CompilerParams(vmem_limit_bytes=60 << 20),
        name="land",
    )(*results)


def solution(mesh):
    return jax.shard_map(
        shards,
        mesh=mesh,
        in_specs=(
            P(None, "dp", "seq", "chan"),
            P(None, None, "chan"),
            P("chan"),
            P(),
            P(),
            P(None, "chan"),
            P("dp", "seq", "chan"),
        ),
        out_specs=(
            P("dp", "seq", "chan"),
            P(None, "dp", "seq", "chan"),
            P(None, None, "chan"),
            P(None, "chan"),
            P(),
            P(),
        ),
        check_vma=False,
    )
```
